512 devices in a mesh: gz: 16 (over z), row: 32 (over y, x, core).
Axes of the slice: x: 4, y: 4, z: 16, core: 2. Of those that a mesh axis runs over, the one named last changes fastest.
Arguments:
- rhs_local: float32 [8, 8, 8, 131072], P(None, None, None, ('gz', 'row')), may hold values from -10 to 10
- stretch: float32 [3, 131072], P(None, ('gz', 'row')), may hold values from 0.25 to 4
Outputs:
- precond: float32 [8, 8, 8, 131072], P(None, None, None, ('gz', 'row'))
The draws below stay inside these ranges and needn't reach their ends.
All inputs are finite; a program needn't handle non-finite values.
Results may differ from the reference program's by a relative error of at most 0.0003.
Values sent between devices are 32-bit elements; how exact they have to be, the bound alone decides.
A program may use at most 128 MiB of HBM per device.

```python
import math
import jax
import jax.numpy as jnp
from jax import lax

ORDER = 7
MID = 3
ITERS = 5
EZ = 4
EA = 4
ER = 16
ELEMS = 131072
N_GZ = 16
N_ROW = 32


def draw_rhs_local(key, part):
    key = jax.random.fold_in(key, 7)
    value_key, scale_key = jax.random.split(key)
    points = ORDER + 1
    scales = jnp.exp(jax.random.uniform(scale_key, (1, 1, 1, ELEMS), jnp.float32, 0.0, math.log(10.0)))
    values = jnp.clip(jax.random.normal(value_key, (points, points, points, ELEMS), jnp.float32), -4.0, 4.0)
    return (values * scales * 0.25).astype(jnp.float32)


def steps_of(own_key, extent, shards, low, largest):
    factor_of, own = 1.0, jax.random.fold_in(own_key, 6)
    for dim, shards_of in shards:
        steps = jnp.exp(jax.random.uniform(jax.random.fold_in(own, dim), (shards_of,), jnp.float32, low / len(shards), largest / len(shards)))
        factor_of = factor_of * jnp.repeat(steps, extent[dim] // shards_of).reshape([-1 if axis == dim else 1 for axis in range(len(extent))])
    return factor_of


def setup_inputs(seed: int = 0) -> dict:
    splits = jax.random.split(jax.random.key(seed), 3)
    rhs_local = draw_rhs_local(jax.random.fold_in(splits[2], 71), 0)
    stretch = jnp.clip(jnp.exp(math.log(4.0) - 2.7725887 * jax.random.uniform(splits[1], (3, ELEMS), jnp.float32) ** steps_of(splits[1], (3, ELEMS), ((1, 512),), -0.2, 0.2)), 0.25, 4.0)
    return dict(rhs_local=rhs_local, stretch=stretch)


LOW_BOUND = 0.4
HIGH_BOUND = 4.0
HIGHEST = lax.Precision.HIGHEST


def node_points(order):
    steps = jnp.arange(order + 1).astype(jnp.float32)
    return -jnp.cos(steps * (math.pi / order))


def level_tables(order):
    points = node_points(order)
    count = order + 1
    identity = jnp.eye(count, dtype=jnp.float32)
    distance = points[:, None] - points[None, :] + identity
    barycentric = 1.0 / jnp.prod(distance, axis=1)
    offdiag = (barycentric[None, :] / barycentric[:, None]) / distance * (1.0 - identity)
    derivative = offdiag - jnp.diag(jnp.sum(offdiag, axis=1))
    place = jnp.arange(count).astype(jnp.float32)
    running = jnp.ones((count,), jnp.float32)
    for freq in range(1, order // 2 + 1):
        factor = 1.0 if 2 * freq == order else 2.0
        running = running - factor / (4.0 * freq * freq - 1.0) * jnp.cos(2.0 * freq * place * math.pi / order)
    endpoint = jnp.where((place == 0) | (place == order), 1.0, 2.0).astype(jnp.float32)
    weights = endpoint / order * running
    stiffness = jnp.dot(derivative.T * weights[None, :], derivative, precision=HIGHEST)
    return weights, stiffness


def interpolation(fine_order, coarse_order):
    fine_points = node_points(fine_order)
    coarse_points = node_points(coarse_order)
    columns = []
    for column in range(coarse_order + 1):
        value = jnp.ones((fine_order + 1,), jnp.float32)
        for other in range(coarse_order + 1):
            if other != column:
                value = value * (fine_points - coarse_points[other]) / (coarse_points[column] - coarse_points[other])
        columns.append(value)
    return jnp.stack(columns, axis=1)


def weight_shape(values, position, ndim):
    shape = [1] * ndim
    shape[position] = values.shape[0]
    return values.reshape(shape)


def element_apply(field, coeff, weights, stiffness):
    ndim = field.ndim
    along_z = weight_shape(weights, 0, ndim)
    along_a = weight_shape(weights, 1, ndim)
    along_r = weight_shape(weights, 2, ndim)
    part_z = jnp.einsum("ij,jbc...->ibc...", stiffness, field, precision=HIGHEST)
    part_a = jnp.einsum("ij,ajc...->aic...", stiffness, field, precision=HIGHEST)
    part_r = jnp.einsum("ij,abj...->abi...", stiffness, field, precision=HIGHEST)
    return coeff[0] * along_a * along_r * part_z + coeff[1] * along_z * along_r * part_a + coeff[2] * along_z * along_a * part_r


def element_diagonal(coeff, weights, stiffness, ndim):
    diag_k = jnp.diagonal(stiffness)
    term_z = weight_shape(diag_k, 0, ndim) * weight_shape(weights, 1, ndim) * weight_shape(weights, 2, ndim)
    term_a = weight_shape(weights, 0, ndim) * weight_shape(diag_k, 1, ndim) * weight_shape(weights, 2, ndim)
    term_r = weight_shape(weights, 0, ndim) * weight_shape(weights, 1, ndim) * weight_shape(diag_k, 2, ndim)
    return coeff[0] * term_z + coeff[1] * term_a + coeff[2] * term_r


def global_face_add(field, node_dim, periodic):
    count = field.shape[node_dim]
    moved = jnp.moveaxis(field, node_dim, 0)
    low_face = moved[0]
    high_face = moved[count - 1]
    elem_dim = 2 + node_dim
    from_below = jnp.roll(high_face, 1, axis=elem_dim)
    from_above = jnp.roll(low_face, -1, axis=elem_dim)
    if not periodic:
        length = low_face.shape[elem_dim]
        place = weight_shape(jnp.arange(length), elem_dim, low_face.ndim)
        from_below = jnp.where(place > 0, from_below, 0.0)
        from_above = jnp.where(place < length - 1, from_above, 0.0)
    moved = moved.at[0].set(low_face + from_below)
    moved = moved.at[count - 1].set(high_face + from_above)
    return jnp.moveaxis(moved, 0, node_dim)


def assemble(field):
    field = global_face_add(field, 2, False)
    field = global_face_add(field, 1, True)
    return global_face_add(field, 0, True)


def level_data(order):
    weights, stiffness = level_tables(order)
    count = order + 1
    node_index = jnp.arange(count)
    radial = jnp.arange(ER)
    at_wall = ((node_index[:, None] == 0) & (radial[None, :] == 0)) | ((node_index[:, None] == count - 1) & (radial[None, :] == ER - 1))
    wall_mask = jnp.where(at_wall, 0.0, 1.0).astype(jnp.float32).reshape(1, 1, count, 1, 1, ER)
    edge = jnp.where((node_index == 0) | (node_index == count - 1), 0.5, 1.0).astype(jnp.float32)
    share = (edge[:, None, None] * edge[None, :, None] * edge[None, None, :]).reshape(count, count, count, 1, 1, 1)
    return weights, stiffness, wall_mask, share


def chebyshev(operate, inverse_diag, rhs):
    theta = 0.5 * (HIGH_BOUND + LOW_BOUND)
    delta = 0.5 * (HIGH_BOUND - LOW_BOUND)
    rho_now = delta / theta
    step = inverse_diag * rhs / theta
    solution = step
    residual = rhs - operate(step)
    rho_next = 1.0 / (2.0 * theta / delta - rho_now)
    step = rho_next * rho_now * step + (2.0 * rho_next / delta) * inverse_diag * residual
    return solution + step, step, residual


def restrict(field, table):
    return jnp.einsum("ia,jb,kc,ijk...->abc...", table, table, table, field, precision=HIGHEST)


def prolong(field, table):
    return jnp.einsum("ia,jb,kc,abc...->ijk...", table, table, table, field, precision=HIGHEST)


def reference(rhs_local, stretch):
    points = ORDER + 1
    whole_z = N_GZ * EZ
    whole_a = N_ROW * EA
    fine_rhs = rhs_local.reshape(points, points, points, N_GZ, N_ROW, EZ, EA, ER).transpose(0, 1, 2, 3, 5, 4, 6, 7).reshape(points, points, points, whole_z, whole_a, ER)
    coeff = stretch.reshape(3, N_GZ, N_ROW, EZ, EA, ER).transpose(0, 1, 3, 2, 4, 5).reshape(3, whole_z, whole_a, ER)
    fine_tab = level_data(ORDER)
    mid_tab = level_data(MID)
    low_tab = level_data(1)

    def make_operator(tables):
        def operate(field):
            return tables[2] * assemble(element_apply(field, coeff, tables[0], tables[1]))
        return operate

    fine_op = make_operator(fine_tab)
    mid_op = make_operator(mid_tab)
    low_op = make_operator(low_tab)
    fine_inv = fine_tab[2] / assemble(element_diagonal(coeff, fine_tab[0], fine_tab[1], 6))
    mid_inv = mid_tab[2] / assemble(element_diagonal(coeff, mid_tab[0], mid_tab[1], 6))
    to_mid = interpolation(ORDER, MID)
    to_low = interpolation(MID, 1)

    fine_b = fine_tab[2] * assemble(fine_rhs)
    fine_sol, fine_step, fine_res = chebyshev(fine_op, fine_inv, fine_b)
    fine_res = fine_res - fine_op(fine_step)
    mid_b = mid_tab[2] * assemble(restrict(fine_tab[3] * fine_res, to_mid))
    mid_sol, mid_step, mid_res = chebyshev(mid_op, mid_inv, mid_b)
    mid_res = mid_res - mid_op(mid_step)
    low_b = low_tab[2] * assemble(restrict(mid_tab[3] * mid_res, to_low))

    weight = low_tab[2] * low_tab[3]
    low_sol = jnp.zeros_like(low_b)
    low_res = low_b
    direction = low_b
    norm_now = jnp.sum(weight * low_res * low_res)
    for iteration in range(ITERS):
        image = low_op(direction)
        alpha = norm_now / jnp.sum(weight * direction * image)
        low_sol = low_sol + alpha * direction
        low_res = low_res - alpha * image
        norm_next = jnp.sum(weight * low_res * low_res)
        direction = low_res + (norm_next / norm_now) * direction
        norm_now = norm_next

    lifted = prolong(low_sol, to_low)
    mid_sol = mid_sol + lifted
    mid_res = mid_res - mid_op(lifted)
    mid_sol = mid_sol + chebyshev(mid_op, mid_inv, mid_res)[0]
    raised = prolong(mid_sol, to_mid)
    fine_sol = fine_sol + raised
    fine_res = fine_res - fine_op(raised)
    fine_sol = fine_sol + chebyshev(fine_op, fine_inv, fine_res)[0]
    return fine_sol.reshape(points, points, points, N_GZ, EZ, N_ROW, EA, ER).transpose(0, 1, 2, 3, 5, 4, 6, 7).reshape(points, points, points, ELEMS)
```

```python
import functools

import numpy as np

import jax
import jax.numpy as jnp
from jax import lax
from jax.experimental import pallas as pl
from jax.experimental.pallas import tpu as pltpu
from jax.sharding import PartitionSpec as P

ORDER = 7
MID = 3
ITERS = 5
EZ = 4
EA = 4
ER = 16
LANES = 128

LOW_BOUND = 0.4
HIGH_BOUND = 4.0
THETA = 0.5 * (HIGH_BOUND + LOW_BOUND)
DELTA = 0.5 * (HIGH_BOUND - LOW_BOUND)
RHO = DELTA / THETA
RHO2 = 1.0 / (2.0 * THETA / DELTA - RHO)

DIRS = ((0, 1), (0, -1), (1, 0), (-1, 0), (1, 1), (1, -1), (-1, 1), (-1, -1))
ROUNDS = ((8, 8, 4), (8,), (8,), (4,), (4,), (4,), (2,), (2,), (2,), (2,), (2,), (4,), (4,), (8,), (8,))


def points_of(order):
    return -np.cos(np.pi * np.arange(order + 1) / order)


def tables_of(order):
    x = points_of(order)
    n = order + 1
    place = np.arange(n)
    running = np.ones(n)
    for j in range(1, order // 2 + 1):
        b = 1.0 if 2 * j == order else 2.0
        running = running - b * np.cos(2 * np.pi * j * place / order) / (4 * j * j - 1)
    weights = np.where((place == 0) | (place == order), 1.0, 2.0) / order * running
    gap = x[:, None] - x[None, :] + np.eye(n)
    bary = 1.0 / np.prod(gap, axis=1)
    deriv = bary[None, :] / bary[:, None] / gap * (1.0 - np.eye(n))
    deriv = deriv - np.diag(deriv.sum(axis=1))
    stiff = deriv.T @ (weights[:, None] * deriv)
    return weights, stiff / weights[:, None]


def interpolation(fine_order, coarse_order):
    x = points_of(fine_order)
    y = points_of(coarse_order)
    table = np.ones((fine_order + 1, coarse_order + 1))
    for j in range(coarse_order + 1):
        for k in range(coarse_order + 1):
            if k != j:
                table[:, j] *= (x - y[k]) / (y[j] - y[k])
    return table


def shared(table):
    out = table.copy()
    out[0] *= 0.5
    out[-1] *= 0.5
    return out


WK = {n: tables_of(n - 1) for n in (8, 4, 2)}
UP = {(4, 8): interpolation(7, 3), (2, 4): interpolation(3, 1)}
DOWN = {(8, 4): shared(UP[4, 8]).T, (4, 2): shared(UP[2, 4]).T}


def column_blocks(table):
    blocks = np.zeros((table.shape[1], 8))
    blocks[:, : table.shape[0]] = table.T
    return blocks


def constant_table():
    blocks, where = [], {}

    def put(name, rows):
        where[name] = sum(len(b) for b in blocks)
        blocks.append(rows)

    for n in (8, 4, 2):
        w, k = WK[n]
        put(("k", n), column_blocks(k))
        put(("w", n), column_blocks(np.outer(w, w)))
        put(("d", n), column_blocks(np.diag(k)[:, None]))
    for key, table in list(UP.items()) + list(DOWN.items()):
        put(("j",) + key, column_blocks(table))
    flat = np.concatenate(blocks).reshape(-1, 1).astype(np.float32)
    return np.broadcast_to(flat, (flat.shape[0], LANES)).copy(), where


CONST, WHERE = constant_table()


def line(table, values):
    rows, cols = table.shape
    half = cols // 2
    even = [values[k] + values[cols - 1 - k] for k in range(half)]
    odd = [values[k] - values[cols - 1 - k] for k in range(half)]
    out = [None] * rows
    for i in range(rows // 2):
        e = o = None
        for k in range(half):
            te = float(np.float32(0.5 * (table[i, k] + table[i, cols - 1 - k])))
            to = float(np.float32(0.5 * (table[i, k] - table[i, cols - 1 - k])))
            e = te * even[k] if e is None else e + te * even[k]
            o = to * odd[k] if o is None else o + to * odd[k]
        out[i] = e + o
        out[rows - 1 - i] = e - o
    return out


def rows8(start):
    if isinstance(start, int):
        return pl.ds(start, 8)
    return pl.ds(pl.multiple_of(start, 8), 8)


def roll(value, shift):
    shift = shift % LANES
    return value if shift == 0 else pltpu.roll(value, shift, 1)


def loop(count, body, unroll_all):
    if unroll_all:
        for i in range(count):
            body(i)
    else:
        pl.loop(0, count)(body)


def split(i, size):
    if isinstance(i, int):
        return i // size, i % size
    return lax.div(i, size), lax.rem(i, size)


def kernel(
    nz, nr, rhs, stretch, tab, out,
    x7, d7, r7, inv7, o7, t1, t2, x3, d3, r3, inv3, o3, t3, x1, r1, p1, s1, o1, coef,
    send, recv, send_diag, recv_diag, row_box, gz_box, gz_part,
    send_sem, recv_sem, row_send, row_recv, gz_send, gz_recv,
):
    gz = lax.axis_index("gz")
    row = lax.axis_index("row")
    mesh_ids = pl.DeviceIdType.MESH
    shape = (8, LANES)
    lane = lax.broadcasted_iota(jnp.int32, shape, 1)
    sub = lax.broadcasted_iota(jnp.int32, shape, 0)
    in_r = lane % ER
    in_a = (lane // ER) % EA
    low_half = lane < 64

    def as_float(cond):
        return jnp.where(cond, 1.0, 0.0).astype(jnp.float32)

    def at_device(dz, da):
        return (lax.rem(gz + (dz + nz), nz), lax.rem(row + (da + nr), nr))

    barrier = pltpu.get_barrier_semaphore()

    @pl.loop(1, nr)
    def _(o):
        pl.semaphore_signal(barrier, inc=1, device_id=(gz, lax.rem(row + o, nr)), device_id_type=mesh_ids)

    @pl.loop(1, nz)
    def _(o):
        pl.semaphore_signal(barrier, inc=1, device_id=(lax.rem(gz + o, nz), row), device_id_type=mesh_ids)

    for dz, da in DIRS[4:]:
        pl.semaphore_signal(barrier, inc=1, device_id=at_device(dz, da), device_id_type=mesh_ids)

    def const(name, j=0):
        return tab[rows8((WHERE[name] + j) * 8), :]

    def live(n):
        wall = ((sub == 0) & (in_r == 0)) | ((sub == n - 1) & (in_r == ER - 1))
        return jnp.logical_not(wall) & (sub < n)

    for g in range(2):
        for k in range(3):
            coef[rows8((g * 3 + k) * 8), :] = jnp.broadcast_to(
                stretch[pl.ds(k, 1), pl.ds(g * LANES, LANES)], shape
            )

    def coeff(g, k):
        return coef[rows8((g * 3 + k) * 8), :]

    def add_r(field, n, base):
        lo_at = pl.ds(base, 8, stride=8)
        hi_at = pl.ds(base + n - 1, 8, stride=8)
        lo, hi = field[lo_at, :], field[hi_at, :]
        field[lo_at, :] = lo + jnp.where(in_r > 0, roll(hi, 1), 0.0)
        field[hi_at, :] = hi + jnp.where(in_r < ER - 1, roll(lo, -1), 0.0)

    def add_a(field, n, base):
        lo_at, hi_at = rows8(base), rows8(base + (n - 1) * 8)
        lo, hi = field[lo_at, :], field[hi_at, :]
        field[lo_at, :] = lo + jnp.where(in_a > 0, roll(hi, ER), 0.0)
        field[hi_at, :] = hi + jnp.where(in_a < EA - 1, roll(lo, -ER), 0.0)

    def block_at(n, g, iz, ia):
        return rows8(((g * n + iz) * n + ia) * 8)

    def add_z(field, n):
        for ia in range(n):
            at = [block_at(n, g, iz, ia) for g, iz in ((0, 0), (1, 0), (0, n - 1), (1, n - 1))]
            lo0, lo1, hi0, hi1 = [field[a, :] for a in at]
            up0, up1, dn0, dn1 = [roll(v, 64) for v in (hi0, hi1, lo0, lo1)]
            field[at[0], :] = lo0 + jnp.where(low_half, 0.0, up0)
            field[at[1], :] = lo1 + jnp.where(low_half, up0, up1)
            field[at[2], :] = hi0 + jnp.where(low_half, dn0, dn1)
            field[at[3], :] = hi1 + jnp.where(low_half, dn1, 0.0)

    def device_sum(field, n):
        loop(2 * n * n // 8, lambda i: add_r(field, n, i * 64), n < 8)
        loop(2 * n, lambda i: add_a(field, n, i * n * 8), n < 8)
        add_z(field, n)

    def element(field, image, n, sums):
        w, k = WK[n]

        def along_z(i):
            g, ia = split(i, n)
            base = g * (n * n * 8) + ia * 8
            got = line(k, [field[rows8(base + iz * n * 8), :] for iz in range(n)])
            c0 = coef[rows8(g * 24), :]
            for iz in range(n):
                image[rows8(base + iz * n * 8), :] = c0 * got[iz]

        def along_rest(i):
            g, iz = split(i, n)
            base = i * (n * 8)
            got = line(k, [field[rows8(base + ia * 8), :] for ia in range(n)])
            c1 = coef[rows8(g * 24 + 8), :]
            c2 = coef[rows8(g * 24 + 16), :]
            scale = tab[rows8((WHERE["w", n] + iz) * 8), :]
            for ia in range(n):
                at = base + ia * 8
                part = None
                for j in range(n):
                    term = const(("k", n), j) * field[pl.ds(at + j, 1), :]
                    part = term if part is None else part + term
                image[rows8(at), :] = (float(w[ia]) * scale) * (image[rows8(at), :] + c1 * got[ia] + c2 * part)
            if sums and n == 8:
                add_r(image, n, base)
                add_a(image, n, base)

        loop(2 * n, along_z, n < 8)
        loop(2 * n, along_rest, n < 8)
        if sums:
            if n == 8:
                add_z(image, n)
            else:
                device_sum(image, n)

    def diagonal(field, n):
        w, k = WK[n]

        def body(i):
            g, iz = split(i, n)
            c0 = coef[rows8(g * 24), :]
            c1 = coef[rows8(g * 24 + 8), :]
            c2 = coef[rows8(g * 24 + 16), :]
            scale = tab[rows8((WHERE["w", n] + iz) * 8), :]
            kz = jnp.broadcast_to(tab[pl.ds(WHERE["d", n] * 8 + iz, 1), :], shape)
            fixed = c0 * kz + c2 * const(("d", n))
            for ia in range(n):
                field[rows8(i * (n * 8) + ia * 8), :] = (float(w[ia]) * scale) * (fixed + float(k[ia, ia]) * c1)

        loop(2 * n, body, n < 8)

    quarter = in_a

    def pack(field, n, at, at_diag):
        half = n // 2
        for m in range(half):
            rows = rows8(at + m * 8)
            to_up = to_down = None
            for k in range(4):
                g, iz = divmod(m + k * half, n)
                up = roll(field[block_at(n, g, iz, n - 1), :], 80 + 16 * k)
                down = roll(field[block_at(n, g, iz, 0), :], 16 * k)
                to_up = up if k == 0 else jnp.where(quarter == k, up, to_up)
                to_down = down if k == 0 else jnp.where(quarter == k, down, to_down)
            send[0, rows, :] = to_up
            send[1, rows, :] = to_down
            hi = [field[block_at(n, 1, n - 1, ia), :] for ia in (m, m + half)]
            lo = [field[block_at(n, 0, 0, ia), :] for ia in (m, m + half)]
            send[2, rows, :] = jnp.where(low_half, roll(hi[0], 64), hi[1])
            send[3, rows, :] = jnp.where(low_half, lo[0], roll(lo[1], 64))
        rows = rows8(at_diag)
        send_diag[0, rows, :] = field[block_at(n, 1, n - 1, n - 1), :]
        send_diag[1, rows, :] = field[block_at(n, 1, n - 1, 0), :]
        send_diag[2, rows, :] = field[block_at(n, 0, 0, n - 1), :]
        send_diag[3, rows, :] = field[block_at(n, 0, 0, 0), :]

    def unpack(field, n, at, at_diag):
        half = n // 2

        def add(where, keep, value):
            field[where, :] = field[where, :] + jnp.where(keep, value, 0.0)

        for m in range(half):
            rows = rows8(at + m * 8)
            got = [recv[d, rows, :] for d in range(4)]
            for k in range(4):
                g, iz = divmod(m + k * half, n)
                add(block_at(n, g, iz, 0), in_a == 0, roll(got[0], -16 * k))
                add(block_at(n, g, iz, n - 1), in_a == EA - 1, roll(got[1], 48 - 16 * k))
        for m in range(half):
            rows = rows8(at + m * 8)
            got = [recv[d, rows, :] for d in range(4)]
            for k in range(2):
                add(block_at(n, 0, 0, m + k * half), low_half, roll(got[2], 64 * k))
                add(block_at(n, 1, n - 1, m + k * half), jnp.logical_not(low_half), roll(got[3], 64 - 64 * k))
        rows = rows8(at_diag)
        add(block_at(n, 0, 0, 0), lane < 16, roll(recv_diag[0, rows, :], 16))
        add(block_at(n, 0, 0, n - 1), (lane >= 48) & (lane < 64), roll(recv_diag[1, rows, :], -16))
        add(block_at(n, 1, n - 1, 0), (lane >= 64) & (lane < 80), roll(recv_diag[2, rows, :], 16))
        add(block_at(n, 1, n - 1, n - 1), lane >= 112, roll(recv_diag[3, rows, :], -16))

    offsets, diag_offsets = [0], [0]
    for counts in ROUNDS:
        offsets.append(offsets[-1] + sum(counts) * 4)
        diag_offsets.append(diag_offsets[-1] + len(counts) * 8)
    state = {"next": 0}

    def exchange_start(*fields):
        turn = state["next"]
        state["next"] += 1
        counts = ROUNDS[turn]
        at, at_diag = offsets[turn], diag_offsets[turn]
        for field, n in zip(fields, counts):
            pack(field, n, at, at_diag)
            at += n * 4
            at_diag += 8
        copies = []
        for d, (dz, da) in enumerate(DIRS):
            if d < 4:
                rows = pl.ds(offsets[turn], sum(counts) * 4)
                src, dst = send.at[d, rows], recv.at[d, rows]
            else:
                rows = pl.ds(diag_offsets[turn], len(counts) * 8)
                src, dst = send_diag.at[d - 4, rows], recv_diag.at[d - 4, rows]
            copy = pltpu.make_async_remote_copy(
                src_ref=src, dst_ref=dst, send_sem=send_sem.at[turn, d], recv_sem=recv_sem.at[turn, d],
                device_id=at_device(dz, da), device_id_type=mesh_ids,
            )
            copy.start()
            copies.append(copy)

        def finish():
            for copy in copies:
                copy.wait()
            at, at_diag = offsets[turn], diag_offsets[turn]
            for field, n in zip(fields, counts):
                unpack(field, n, at, at_diag)
                at += n * 4
                at_diag += 8

        return finish

    def exchange(*fields):
        exchange_start(*fields)()

    def apply(field, image, n):
        element(field, image, n, True)
        exchange(image)

    def blocks(n, body):
        def step(i):
            if isinstance(i, int):
                body(pl.ds(i * 64, 64))
            else:
                body(pl.ds(pl.multiple_of(i * 64, 64), 64))

        loop(2 * n * n // 8, step, n < 8)

    def masked(n, value):
        keep = jnp.concatenate([as_float(live(n))] * 8, axis=0)
        return keep * value

    @pl.loop(0, 8)
    def _(i):
        rows = pl.ds(pl.multiple_of(i * 64, 64), 64)
        for g in range(2):
            r7[pl.ds(pl.multiple_of(g * 512 + i * 64, 64), 64), :] = rhs[rows, pl.ds(g * LANES, LANES)]

    device_sum(r7, 8)
    diagonal(inv7, 8)
    device_sum(inv7, 8)
    diagonal(inv3, 4)
    device_sum(inv3, 4)
    pl.semaphore_wait(barrier, (nr - 1) + (nz - 1) + 4)
    exchange(r7, inv7, inv3)

    def invert(inv, n):
        keep = jnp.concatenate([live(n)] * 8, axis=0)

        def body(at):
            inv[at, :] = jnp.where(keep, 1.0 / jnp.where(keep, inv[at, :], 1.0), 0.0)

        blocks(n, body)

    invert(inv7, 8)
    invert(inv3, 4)

    def smooth_first(inv, r, d, n):
        def body(at):
            d[at, :] = (1.0 / THETA) * (inv[at, :] * r[at, :])

        blocks(n, body)

    def smooth_second(inv, r, d, x, image, n, add, keep_r=True):
        def body(at):
            step = d[at, :]
            left = r[at, :] - image[at, :]
            second = (RHO2 * RHO) * step + (2.0 * RHO2 / DELTA) * (inv[at, :] * left)
            x[at, :] = (x[at, :] + (step + second)) if add else step + second
            if keep_r:
                d[at, :] = second
                r[at, :] = left

        blocks(n, body)

    def residual(r, image, n):
        def body(at):
            r[at, :] = masked(n, r[at, :] - image[at, :])

        blocks(n, body)

    def r_line(name, field, at, count):
        part = None
        for j in range(count):
            term = const(name, j) * field[pl.ds(at + j, 1), :]
            part = term if part is None else part + term
        return part

    def restrict(fine, nf, nc, coarse, tz, ta):
        table = DOWN[nf, nc]

        def along_z(i):
            g, ia = split(i, nf)
            got = line(table, [fine[rows8((g * nf + iz) * (nf * 8) + ia * 8), :] for iz in range(nf)])
            for c in range(nc):
                tz[rows8((g * nc + c) * (nf * 8) + ia * 8), :] = got[c]

        def along_a(i):
            got = line(table, [tz[rows8(i * (nf * 8) + ia * 8), :] for ia in range(nf)])
            for c in range(nc):
                ta[rows8(i * (nc * 8) + c * 8), :] = got[c]
            for c in range(nc):
                at = i * (nc * 8) + c * 8
                coarse[rows8(at), :] = r_line(("j", nf, nc), ta, at, nf)

        loop(2 * nf, along_z, nf < 8)
        loop(2 * nc, along_a, nf < 8)

    def prolong(coarse, nc, nf, fine, tz, ta):
        table = UP[nc, nf]

        def along_a(i):
            for c in range(nc):
                at = i * (nc * 8) + c * 8
                ta[rows8(at), :] = r_line(("j", nc, nf), coarse, at, nc)
            got = line(table, [ta[rows8(i * (nc * 8) + c * 8), :] for c in range(nc)])
            for ia in range(nf):
                tz[rows8(i * (nf * 8) + ia * 8), :] = got[ia]

        def along_z(i):
            g, ia = split(i, nf)
            got = line(table, [tz[rows8((g * nc + c) * (nf * 8) + ia * 8), :] for c in range(nc)])
            for iz in range(nf):
                fine[rows8((g * nf + iz) * (nf * 8) + ia * 8), :] = got[iz]

        loop(2 * nc, along_a, nf < 8)
        loop(2 * nf, along_z, nf < 8)

    smooth_first(inv7, r7, d7, 8)
    apply(d7, o7, 8)
    smooth_second(inv7, r7, d7, x7, o7, 8, False)
    apply(d7, o7, 8)
    residual(r7, o7, 8)

    restrict(r7, 8, 4, r3, t1, t2)
    device_sum(r3, 4)
    exchange(r3)
    smooth_first(inv3, r3, d3, 4)
    apply(d3, o3, 4)
    smooth_second(inv3, r3, d3, x3, o3, 4, False)
    apply(d3, o3, 4)
    residual(r3, o3, 4)

    restrict(r3, 4, 2, r1, t3, t2)
    device_sum(r1, 2)
    exchange(r1)
    r1[...] = masked(2, r1[...])

    def all_sum_start(turn, first, second):
        def column(value):
            total = value[0:8]
            for k in range(1, 8):
                total = total + value[k * 8 : k * 8 + 8]
            return jnp.sum(total, axis=0, keepdims=True)

        row_box[turn, 0, pl.ds(0, 1), :] = column(first)
        row_box[turn, 0, pl.ds(1, 1), :] = column(second)

        @pl.loop(1, nr)
        def _(o):
            pltpu.make_async_remote_copy(
                src_ref=row_box.at[turn, 0], dst_ref=row_box.at[turn, o],
                send_sem=row_send.at[turn], recv_sem=row_recv.at[turn],
                device_id=(gz, lax.rem(row + o, nr)), device_id_type=mesh_ids,
            ).start()

    def wait_for(box, turn, count, sem):
        rest = box.at[turn, pl.ds(1, count - 1)]
        pltpu.make_async_copy(rest, rest, sem.at[turn]).wait()

    def total_of(box, turn, count):
        total = box[turn, 0]
        for o in range(1, count):
            total = total + box[turn, o]
        return total

    def all_sum_middle(turn):
        wait_for(row_box, turn, nr, row_recv)
        gz_box[turn, 0] = total_of(row_box, turn, nr)

        @pl.loop(1, nz)
        def _(o):
            pltpu.make_async_remote_copy(
                src_ref=gz_box.at[turn, 0], dst_ref=gz_box.at[turn, o],
                send_sem=gz_send.at[turn], recv_sem=gz_recv.at[turn],
                device_id=(lax.rem(gz + o, nz), row), device_id_type=mesh_ids,
            ).start()

    def all_sum_finish(turn):
        wait_for(gz_box, turn, nz, gz_recv)
        gz_part[...] = total_of(gz_box, turn, nz)
        total = jnp.sum(gz_part[...], axis=1, keepdims=True)
        wait_for(row_box, turn, nr, row_send)
        wait_for(gz_box, turn, nz, gz_send)
        return total[0:1, :], total[1:2, :]

    norm_old = alpha = None
    for turn in range(ITERS):
        last = turn == ITERS - 1
        element(r1, o1, 2, False)
        res = r1[...]
        all_sum_start(turn, 0.125 * (res * res), res * o1[...])
        finish = None
        if not last:
            device_sum(o1, 2)
            finish = exchange_start(o1)
        all_sum_middle(turn)
        if not last:
            finish()
        norm, energy = all_sum_finish(turn)
        if turn == 0:
            alpha = norm / energy
            direction = res
        else:
            beta = norm / norm_old
            alpha = norm / (energy - beta * norm / alpha)
            direction = res + beta * p1[...]
        norm_old = norm
        x1[...] = alpha * direction if turn == 0 else x1[...] + alpha * direction
        if not last:
            image = masked(2, o1[...])
            if turn > 0:
                image = image + beta * s1[...]
            p1[...] = direction
            s1[...] = image
            r1[...] = res - alpha * image

    prolong(x1, 2, 4, d3, t3, t2)
    x3[...] = x3[...] + d3[...]
    apply(d3, o3, 4)
    r3[...] = r3[...] - o3[...]
    smooth_first(inv3, r3, d3, 4)
    apply(d3, o3, 4)
    smooth_second(inv3, r3, d3, x3, o3, 4, True, False)

    prolong(x3, 4, 8, d7, t1, t2)
    apply(d7, o7, 8)

    def before_last(at):
        x7[at, :] = x7[at, :] + d7[at, :]
        left = r7[at, :] - o7[at, :]
        r7[at, :] = left
        d7[at, :] = (1.0 / THETA) * (inv7[at, :] * left)

    blocks(8, before_last)
    apply(d7, o7, 8)
    smooth_second(inv7, r7, d7, x7, o7, 8, True, False)

    @pl.loop(0, 8)
    def _(i):
        rows = pl.ds(pl.multiple_of(i * 64, 64), 64)
        for g in range(2):
            out[rows, pl.ds(g * LANES, LANES)] = x7[pl.ds(pl.multiple_of(g * 512 + i * 64, 64), 64), :]


def per_device(rhs_local, stretch):
    nz = lax.axis_size("gz")
    nr = lax.axis_size("row")
    nodes = (ORDER + 1) ** 3
    elems = EZ * EA * ER
    face_rows = sum(sum(c) * 4 for c in ROUNDS)
    diag_rows = sum(len(c) * 8 for c in ROUNDS)

    def field(rows):
        return pltpu.VMEM((rows, LANES), jnp.float32)

    out = pl.pallas_call(
        functools.partial(kernel, nz, nr),
        out_shape=jax.ShapeDtypeStruct((nodes, elems), jnp.float32),
        in_specs=[pl.BlockSpec(memory_space=pltpu.VMEM)] * 3,
        out_specs=pl.BlockSpec(memory_space=pltpu.VMEM),
        scratch_shapes=[field(1024)] * 5
        + [field(512), field(256)]
        + [field(256)] * 5
        + [field(128)]
        + [field(64)] * 5
        + [field(48)]
        + [
            pltpu.VMEM((4, face_rows, LANES), jnp.float32),
            pltpu.VMEM((4, face_rows, LANES), jnp.float32),
            pltpu.VMEM((4, diag_rows, LANES), jnp.float32),
            pltpu.VMEM((4, diag_rows, LANES), jnp.float32),
            pltpu.VMEM((ITERS, nr, 2, LANES), jnp.float32),
            pltpu.VMEM((ITERS, nz, 2, LANES), jnp.float32),
            pltpu.VMEM((2, LANES), jnp.float32),
            pltpu.SemaphoreType.DMA((len(ROUNDS), 8)),
            pltpu.SemaphoreType.DMA((len(ROUNDS), 8)),
            pltpu.SemaphoreType.DMA((ITERS,)),
            pltpu.SemaphoreType.DMA((ITERS,)),
            pltpu.SemaphoreType.DMA((ITERS,)),
            pltpu.SemaphoreType.DMA((ITERS,)),
        ],
        compiler_params=pltpu.CompilerParams(
            collective_id=0, has_side_effects=True, vmem_limit_bytes=32 * 1024 * 1024
        ),
    )(rhs_local.reshape(nodes, elems), stretch, jnp.asarray(CONST))
    return out.reshape(rhs_local.shape)


def solution(mesh):
    placed = (P(None, None, None, ("gz", "row")), P(None, ("gz", "row")))
    return jax.shard_map(
        per_device,
        mesh=mesh,
        in_specs=placed,
        out_specs=P(None, None, None, ("gz", "row")),
        check_vma=False,
    )
```

```python
import functools

import numpy as np

import jax
import jax.numpy as jnp
from jax import lax
from jax.experimental import pallas as pl
from jax.experimental.pallas import tpu as pltpu
from jax.sharding import PartitionSpec as P

ORDER = 7
MID = 3
ITERS = 5
EZ = 4
EA = 4
ER = 16
LANES = 128

LOW_BOUND = 0.4
HIGH_BOUND = 4.0
THETA = 0.5 * (HIGH_BOUND + LOW_BOUND)
DELTA = 0.5 * (HIGH_BOUND - LOW_BOUND)
RHO = DELTA / THETA
RHO2 = 1.0 / (2.0 * THETA / DELTA - RHO)

DIRS = ((0, 1), (0, -1), (1, 0), (-1, 0), (1, 1), (1, -1), (-1, 1), (-1, -1))
ROUNDS = ((8, 8, 4), (8,), (4,), (4,), (2,), (4,), (4,), (8,), (8,))
SCALE = 16.0
TINY = 1e-13


def points_of(order):
    return -np.cos(np.pi * np.arange(order + 1) / order)


def tables_of(order):
    x = points_of(order)
    n = order + 1
    place = np.arange(n)
    running = np.ones(n)
    for j in range(1, order // 2 + 1):
        b = 1.0 if 2 * j == order else 2.0
        running = running - b * np.cos(2 * np.pi * j * place / order) / (4 * j * j - 1)
    weights = np.where((place == 0) | (place == order), 1.0, 2.0) / order * running
    gap = x[:, None] - x[None, :] + np.eye(n)
    bary = 1.0 / np.prod(gap, axis=1)
    deriv = bary[None, :] / bary[:, None] / gap * (1.0 - np.eye(n))
    deriv = deriv - np.diag(deriv.sum(axis=1))
    stiff = deriv.T @ (weights[:, None] * deriv)
    return weights, stiff / weights[:, None]


def interpolation(fine_order, coarse_order):
    x = points_of(fine_order)
    y = points_of(coarse_order)
    table = np.ones((fine_order + 1, coarse_order + 1))
    for j in range(coarse_order + 1):
        for k in range(coarse_order + 1):
            if k != j:
                table[:, j] *= (x - y[k]) / (y[j] - y[k])
    return table


WK = {n: tables_of(n - 1) for n in (8, 4, 2)}
UP = {(4, 8): interpolation(7, 3), (2, 4): interpolation(3, 1)}
DOWN = {(8, 4): UP[4, 8].T, (4, 2): UP[2, 4].T}
PAIRS = [(i, j) for i in range(ITERS) for j in range(i, ITERS)] + [(i, ITERS) for i in range(ITERS)]


def column_blocks(table):
    blocks = np.zeros((table.shape[1], 8))
    blocks[:, : table.shape[0]] = table.T
    return blocks


def constant_table():
    blocks, where = [], {}

    def put(name, rows):
        where[name] = sum(len(b) for b in blocks)
        blocks.append(rows)

    for n in (8, 4, 2):
        w, k = WK[n]
        put(("k", n), column_blocks(k))
        put(("w", n), column_blocks(np.outer(w, w)))
        put(("d", n), column_blocks(np.diag(k)[:, None]))
    for key, table in list(UP.items()) + list(DOWN.items()):
        put(("j",) + key, column_blocks(table))
    flat = np.concatenate(blocks).reshape(-1, 1).astype(np.float32)
    wide = np.broadcast_to(flat, (flat.shape[0], LANES))
    where["pick"] = wide.shape[0] // 8
    pick = np.zeros((24, LANES), np.float32)
    for e, (i, j) in enumerate(PAIRS):
        pick[e, 8 * i + j] = 1.0
        if j < ITERS:
            pick[e, 8 * j + i] = 1.0
    return np.concatenate([wide, pick]), where


CONST, WHERE = constant_table()


def line(table, values):
    rows, cols = table.shape
    half = cols // 2
    even = [values[k] + values[cols - 1 - k] for k in range(half)]
    odd = [values[k] - values[cols - 1 - k] for k in range(half)]
    out = [None] * rows
    for i in range(rows // 2):
        e = o = None
        for k in range(half):
            te = float(np.float32(0.5 * (table[i, k] + table[i, cols - 1 - k])))
            to = float(np.float32(0.5 * (table[i, k] - table[i, cols - 1 - k])))
            e = te * even[k] if e is None else e + te * even[k]
            o = to * odd[k] if o is None else o + to * odd[k]
        out[i] = e + o
        out[rows - 1 - i] = e - o
    return out


def rows8(start):
    if isinstance(start, int):
        return pl.ds(start, 8)
    return pl.ds(pl.multiple_of(start, 8), 8)


def roll(value, shift):
    shift = shift % LANES
    return value if shift == 0 else pltpu.roll(value, shift, 1)


def loop(count, body, unroll_all):
    if unroll_all:
        for i in range(count):
            body(i)
    else:
        pl.loop(0, count)(body)


def split(i, size):
    if isinstance(i, int):
        return i // size, i % size
    return lax.div(i, size), lax.rem(i, size)


def two_sum(a, b):
    s = a + b
    t = s - a
    return s, (a - (s - t)) + (b - t)


def halves(a):
    t = 4097.0 * a
    hi = t - (t - a)
    return a, hi, a - hi


def two_prod(x, y):
    a, ah, al = x
    b, bh, bl = y
    p = a * b
    return p, ((ah * bh - p) + ah * bl + al * bh) + al * bl


def add2(x, y):
    s, e = two_sum(x[0], y[0])
    return two_sum(s, e + (x[1] + y[1]))


def mul2(x, y):
    p, e = two_prod(halves(x[0]), halves(y[0]))
    return two_sum(p, e + (x[0] * y[1] + x[1] * y[0]))


def inverse2(x):
    r = 1.0 / x[0]
    p, e = two_prod(halves(x[0]), halves(r))
    return two_sum(r, r * (((1.0 - p) - e) - x[1] * r))


def kernel(
    nz, nr, rhs, stretch, tab, out,
    x7, d7, r7, inv7, o7, t1, t2, x3, d3, r3, inv3, o3, t3, x1, r1, coef,
    send, recv, send_diag, recv_diag, send_block, recv_block, row_box, gz_box,
    send_sem, recv_sem, block_send, block_recv, row_send, row_recv, gz_send, gz_recv,
):
    gz = lax.axis_index("gz")
    row = lax.axis_index("row")
    mesh_ids = pl.DeviceIdType.MESH
    shape = (8, LANES)
    lane = lax.broadcasted_iota(jnp.int32, shape, 1)
    sub = lax.broadcasted_iota(jnp.int32, shape, 0)
    in_r = lane % ER
    in_a = (lane // ER) % EA
    low_half = lane < 64

    def as_float(cond):
        return jnp.where(cond, 1.0, 0.0).astype(jnp.float32)

    def at_device(dz, da):
        return (lax.rem(gz + (dz + nz), nz), lax.rem(row + (da + nr), nr))

    barrier = pltpu.get_barrier_semaphore()

    @pl.loop(1, nr)
    def _(o):
        pl.semaphore_signal(barrier, inc=1, device_id=(gz, lax.rem(row + o, nr)), device_id_type=mesh_ids)

    @pl.loop(1, nz)
    def _(o):
        pl.semaphore_signal(barrier, inc=1, device_id=(lax.rem(gz + o, nz), row), device_id_type=mesh_ids)

    for dz, da in DIRS[4:]:
        pl.semaphore_signal(barrier, inc=1, device_id=at_device(dz, da), device_id_type=mesh_ids)

    def const(name, j=0):
        return tab[rows8((WHERE[name] + j) * 8), :]

    def live(n):
        wall = ((sub == 0) & (in_r == 0)) | ((sub == n - 1) & (in_r == ER - 1))
        return jnp.logical_not(wall) & (sub < n)

    for g in range(2):
        for k in range(3):
            coef[rows8((g * 3 + k) * 8), :] = jnp.broadcast_to(
                stretch[pl.ds(k, 1), pl.ds(g * LANES, LANES)], shape
            )

    def coeff(g, k):
        return coef[rows8((g * 3 + k) * 8), :]

    def add_r(field, n, base):
        lo_at = pl.ds(base, 8, stride=8)
        hi_at = pl.ds(base + n - 1, 8, stride=8)
        lo, hi = field[lo_at, :], field[hi_at, :]
        field[lo_at, :] = lo + jnp.where(in_r > 0, roll(hi, 1), 0.0)
        field[hi_at, :] = hi + jnp.where(in_r < ER - 1, roll(lo, -1), 0.0)

    def add_a(field, n, base):
        lo_at, hi_at = rows8(base), rows8(base + (n - 1) * 8)
        lo, hi = field[lo_at, :], field[hi_at, :]
        field[lo_at, :] = lo + jnp.where(in_a > 0, roll(hi, ER), 0.0)
        field[hi_at, :] = hi + jnp.where(in_a < EA - 1, roll(lo, -ER), 0.0)

    def block_at(n, g, iz, ia):
        return rows8(((g * n + iz) * n + ia) * 8)

    def add_z(field, n):
        for ia in range(n):
            at = [block_at(n, g, iz, ia) for g, iz in ((0, 0), (1, 0), (0, n - 1), (1, n - 1))]
            lo0, lo1, hi0, hi1 = [field[a, :] for a in at]
            up0, up1, dn0, dn1 = [roll(v, 64) for v in (hi0, hi1, lo0, lo1)]
            field[at[0], :] = lo0 + jnp.where(low_half, 0.0, up0)
            field[at[1], :] = lo1 + jnp.where(low_half, up0, up1)
            field[at[2], :] = hi0 + jnp.where(low_half, dn0, dn1)
            field[at[3], :] = hi1 + jnp.where(low_half, dn1, 0.0)

    def device_sum(field, n):
        loop(2 * n * n // 8, lambda i: add_r(field, n, i * 64), n < 8)
        loop(2 * n, lambda i: add_a(field, n, i * n * 8), n < 8)
        add_z(field, n)

    def shared(iz, ia, n):
        along = jnp.where((sub == 0) | (sub == n - 1), 0.5, 1.0)
        if ia in (0, n - 1):
            along = 0.5 * along
        if isinstance(iz, int):
            return 0.5 * along if iz in (0, n - 1) else along
        return jnp.where((iz == 0) | (iz == n - 1), 0.5, 1.0) * along

    def element(field, image, n, sums, left=None):
        w, k = WK[n]

        def along_z(i):
            g, ia = split(i, n)
            base = g * (n * n * 8) + ia * 8
            got = line(k, [field[rows8(base + iz * n * 8), :] for iz in range(n)])
            c0 = coef[rows8(g * 24), :]
            for iz in range(n):
                image[rows8(base + iz * n * 8), :] = c0 * got[iz]

        def along_rest(i):
            g, iz = split(i, n)
            base = i * (n * 8)
            got = line(k, [field[rows8(base + ia * 8), :] for ia in range(n)])
            c1 = coef[rows8(g * 24 + 8), :]
            c2 = coef[rows8(g * 24 + 16), :]
            scale = tab[rows8((WHERE["w", n] + iz) * 8), :]
            for ia in range(n):
                at = base + ia * 8
                part = None
                for j in range(n):
                    term = const(("k", n), j) * field[pl.ds(at + j, 1), :]
                    part = term if part is None else part + term
                value = (float(w[ia]) * scale) * (image[rows8(at), :] + c1 * got[ia] + c2 * part)
                if left is not None:
                    value = shared(iz, ia, n) * left[rows8(at), :] - value
                image[rows8(at), :] = value
            if sums and n == 8:
                add_r(image, n, base)
                add_a(image, n, base)

        loop(2 * n, along_z, n < 8)
        loop(2 * n, along_rest, n < 8)
        if sums:
            if n == 8:
                add_z(image, n)
            else:
                device_sum(image, n)

    def diagonal(field, n):
        w, k = WK[n]

        def body(i):
            g, iz = split(i, n)
            c0 = coef[rows8(g * 24), :]
            c1 = coef[rows8(g * 24 + 8), :]
            c2 = coef[rows8(g * 24 + 16), :]
            scale = tab[rows8((WHERE["w", n] + iz) * 8), :]
            kz = jnp.broadcast_to(tab[pl.ds(WHERE["d", n] * 8 + iz, 1), :], shape)
            fixed = c0 * kz + c2 * const(("d", n))
            for ia in range(n):
                field[rows8(i * (n * 8) + ia * 8), :] = (float(w[ia]) * scale) * (fixed + float(k[ia, ia]) * c1)

        loop(2 * n, body, n < 8)

    quarter = in_a

    def pack(field, n, at, at_diag):
        half = n // 2
        for m in range(half):
            rows = rows8(at + m * 8)
            to_up = to_down = None
            for k in range(4):
                g, iz = divmod(m + k * half, n)
                up = roll(field[block_at(n, g, iz, n - 1), :], 80 + 16 * k)
                down = roll(field[block_at(n, g, iz, 0), :], 16 * k)
                to_up = up if k == 0 else jnp.where(quarter == k, up, to_up)
                to_down = down if k == 0 else jnp.where(quarter == k, down, to_down)
            send[0, rows, :] = to_up
            send[1, rows, :] = to_down
            hi = [field[block_at(n, 1, n - 1, ia), :] for ia in (m, m + half)]
            lo = [field[block_at(n, 0, 0, ia), :] for ia in (m, m + half)]
            send[2, rows, :] = jnp.where(low_half, roll(hi[0], 64), hi[1])
            send[3, rows, :] = jnp.where(low_half, lo[0], roll(lo[1], 64))
        rows = rows8(at_diag)
        send_diag[0, rows, :] = field[block_at(n, 1, n - 1, n - 1), :]
        send_diag[1, rows, :] = field[block_at(n, 1, n - 1, 0), :]
        send_diag[2, rows, :] = field[block_at(n, 0, 0, n - 1), :]
        send_diag[3, rows, :] = field[block_at(n, 0, 0, 0), :]

    def unpack(field, n, at, at_diag):
        half = n // 2

        def add(where, keep, value):
            field[where, :] = field[where, :] + jnp.where(keep, value, 0.0)

        for m in range(half):
            rows = rows8(at + m * 8)
            got = [recv[d, rows, :] for d in range(4)]
            for k in range(4):
                g, iz = divmod(m + k * half, n)
                add(block_at(n, g, iz, 0), in_a == 0, roll(got[0], -16 * k))
                add(block_at(n, g, iz, n - 1), in_a == EA - 1, roll(got[1], 48 - 16 * k))
        for m in range(half):
            rows = rows8(at + m * 8)
            got = [recv[d, rows, :] for d in range(4)]
            for k in range(2):
                add(block_at(n, 0, 0, m + k * half), low_half, roll(got[2], 64 * k))
                add(block_at(n, 1, n - 1, m + k * half), jnp.logical_not(low_half), roll(got[3], 64 - 64 * k))
        rows = rows8(at_diag)
        add(block_at(n, 0, 0, 0), lane < 16, roll(recv_diag[0, rows, :], 16))
        add(block_at(n, 0, 0, n - 1), (lane >= 48) & (lane < 64), roll(recv_diag[1, rows, :], -16))
        add(block_at(n, 1, n - 1, 0), (lane >= 64) & (lane < 80), roll(recv_diag[2, rows, :], 16))
        add(block_at(n, 1, n - 1, n - 1), lane >= 112, roll(recv_diag[3, rows, :], -16))

    offsets, diag_offsets = [0], [0]
    for counts in ROUNDS:
        offsets.append(offsets[-1] + sum(counts) * 4)
        diag_offsets.append(diag_offsets[-1] + len(counts) * 8)
    state = {"next": 0}

    def exchange_start(*fields):
        turn = state["next"]
        state["next"] += 1
        counts = ROUNDS[turn]
        at, at_diag = offsets[turn], diag_offsets[turn]
        for field, n in zip(fields, counts):
            pack(field, n, at, at_diag)
            at += n * 4
            at_diag += 8
        copies = []
        for d, (dz, da) in enumerate(DIRS):
            if d < 4:
                rows = pl.ds(offsets[turn], sum(counts) * 4)
                src, dst = send.at[d, rows], recv.at[d, rows]
            else:
                rows = pl.ds(diag_offsets[turn], len(counts) * 8)
                src, dst = send_diag.at[d - 4, rows], recv_diag.at[d - 4, rows]
            copy = pltpu.make_async_remote_copy(
                src_ref=src, dst_ref=dst, send_sem=send_sem.at[turn, d], recv_sem=recv_sem.at[turn, d],
                device_id=at_device(dz, da), device_id_type=mesh_ids,
            )
            copy.start()
            copies.append(copy)

        def finish():
            for copy in copies:
                copy.wait()
            at, at_diag = offsets[turn], diag_offsets[turn]
            for field, n in zip(fields, counts):
                unpack(field, n, at, at_diag)
                at += n * 4
                at_diag += 8

        return finish

    def block_start(turn, at, count):
        copies = []
        for d, (dz, da) in enumerate(DIRS):
            copy = pltpu.make_async_remote_copy(
                src_ref=send_block.at[pl.ds(at, count)], dst_ref=recv_block.at[d, pl.ds(at, count)],
                send_sem=block_send.at[turn, d], recv_sem=block_recv.at[turn, d],
                device_id=at_device(dz, da), device_id_type=mesh_ids,
            )
            copy.start()
            copies.append(copy)
        return copies

    def wide(at):
        def block(dz, da):
            if (dz, da) == (0, 0):
                return send_block[rows8(at), :]
            return recv_block[DIRS.index((-dz, -da)), rows8(at), :]

        def left_part(dz):
            return jnp.where(low_half, block(dz, -1), roll(block(dz, 0), 64))

        def below(low, own):
            return jnp.where(sub < 4, low, pltpu.roll(own, 4, 0))

        top = jnp.concatenate([below(left_part(-1), left_part(0)), below(block(-1, 1), block(0, 1))], axis=1)
        bottom = jnp.concatenate([left_part(1), block(1, 1)], axis=1)
        return jnp.concatenate([top, bottom], axis=0)

    def exchange(*fields):
        exchange_start(*fields)()

    def apply(field, image, n):
        element(field, image, n, True)
        exchange(image)

    def blocks(n, body):
        def step(i):
            if isinstance(i, int):
                body(pl.ds(i * 64, 64))
            else:
                body(pl.ds(pl.multiple_of(i * 64, 64), 64))

        loop(2 * n * n // 8, step, n < 8)

    def masked(n, value):
        keep = jnp.concatenate([as_float(live(n))] * 8, axis=0)
        return keep * value

    @pl.loop(0, 8)
    def _(i):
        rows = pl.ds(pl.multiple_of(i * 64, 64), 64)
        for g in range(2):
            r7[pl.ds(pl.multiple_of(g * 512 + i * 64, 64), 64), :] = rhs[rows, pl.ds(g * LANES, LANES)]

    device_sum(r7, 8)
    diagonal(inv7, 8)
    device_sum(inv7, 8)
    diagonal(inv3, 4)
    device_sum(inv3, 4)
    for k in range(3):
        rows = jnp.where(sub < 2, coeff(0, k), coeff(1, k))
        send_block[rows8(k * 8), :] = jnp.where(sub % 2 == 0, rows, roll(rows, 64))
    pl.semaphore_wait(barrier, (nr - 1) + (nz - 1) + 4)
    finish_first = exchange_start(r7, inv7, inv3)
    stretch_copies = block_start(0, 0, 24)
    finish_first()

    def invert(inv, n):
        keep = jnp.concatenate([live(n)] * 8, axis=0)

        def body(at):
            inv[at, :] = jnp.where(keep, 1.0 / jnp.where(keep, inv[at, :], 1.0), 0.0)

        blocks(n, body)

    invert(inv7, 8)
    invert(inv3, 4)

    def smooth_first(inv, r, d, n):
        def body(at):
            d[at, :] = (1.0 / THETA) * (inv[at, :] * r[at, :])

        blocks(n, body)

    def smooth_second(inv, r, d, x, image, n, add, keep_r=True):
        def body(at):
            step = d[at, :]
            left = r[at, :] - image[at, :]
            second = (RHO2 * RHO) * step + (2.0 * RHO2 / DELTA) * (inv[at, :] * left)
            x[at, :] = (x[at, :] + (step + second)) if add else step + second
            if keep_r:
                d[at, :] = second
                r[at, :] = left

        blocks(n, body)

    def r_line(name, field, at, count):
        part = None
        for j in range(count):
            term = const(name, j) * field[pl.ds(at + j, 1), :]
            part = term if part is None else part + term
        return part

    def restrict(fine, nf, nc, coarse, tz, ta):
        table = DOWN[nf, nc]

        def along_z(i):
            g, ia = split(i, nf)
            got = line(table, [fine[rows8((g * nf + iz) * (nf * 8) + ia * 8), :] for iz in range(nf)])
            for c in range(nc):
                tz[rows8((g * nc + c) * (nf * 8) + ia * 8), :] = got[c]

        def along_a(i):
            got = line(table, [tz[rows8(i * (nf * 8) + ia * 8), :] for ia in range(nf)])
            for c in range(nc):
                ta[rows8(i * (nc * 8) + c * 8), :] = got[c]
            for c in range(nc):
                at = i * (nc * 8) + c * 8
                coarse[rows8(at), :] = r_line(("j", nf, nc), ta, at, nf)

        loop(2 * nf, along_z, nf < 8)
        loop(2 * nc, along_a, nf < 8)

    def prolong(coarse, nc, nf, fields, tz, ta):
        table = UP[nc, nf]

        def along_a(i):
            for c in range(nc):
                at = i * (nc * 8) + c * 8
                ta[rows8(at), :] = r_line(("j", nc, nf), coarse, at, nc)
            got = line(table, [ta[rows8(i * (nc * 8) + c * 8), :] for c in range(nc)])
            for ia in range(nf):
                tz[rows8(i * (nf * 8) + ia * 8), :] = got[ia]

        def along_z(i):
            g, ia = split(i, nf)
            got = line(table, [tz[rows8((g * nc + c) * (nf * 8) + ia * 8), :] for c in range(nc)])
            for iz in range(nf):
                at = rows8((g * nf + iz) * (nf * 8) + ia * 8)
                for field in fields:
                    field[at, :] = field[at, :] + got[iz]

        loop(2 * nc, along_a, nf < 8)
        loop(2 * nf, along_z, nf < 8)

    smooth_first(inv7, r7, d7, 8)
    apply(d7, o7, 8)
    smooth_second(inv7, r7, d7, x7, o7, 8, False)
    element(d7, o7, 8, False, left=r7)

    restrict(o7, 8, 4, r3, t1, t2)
    device_sum(r3, 4)
    exchange(r3)
    smooth_first(inv3, r3, d3, 4)
    apply(d3, o3, 4)
    smooth_second(inv3, r3, d3, x3, o3, 4, False)
    element(d3, o3, 4, False, left=r3)

    restrict(o3, 4, 2, r1, t3, t2)
    device_sum(r1, 2)
    exchange(r1)
    r1[...] = masked(2, r1[...])

    for copy in stretch_copies:
        copy.wait()
    lane_wide = lax.broadcasted_iota(jnp.int32, (16, 256), 1)
    inside = lane_wide % ER > 0

    def step(value, axis, amount):
        if axis == 0:
            return pltpu.roll(value, amount % 16, 0)
        return pltpu.roll(value, (amount * (ER if axis == 1 else 1)) % 256, 1)

    edges = []
    for axis in range(3):
        total = wide(axis * 8)
        for other in range(3):
            if other != axis:
                total = total + step(total, other, 1)
        edges.append(0.5 * total)

    def differences(value):
        return [value - step(value, axis, -1) for axis in range(3)]

    def vertex_image(slopes):
        total = None
        for axis in range(3):
            flux = edges[axis] * slopes[axis]
            flux = flux - step(flux, axis, 1)
            total = flux if total is None else total + flux
        return jnp.where(inside, (1.0 / SCALE) * total, 0.0)

    def vertex_row(g, iz, odd):
        inner = jnp.broadcast_to(r1[pl.ds(((g * 2 + iz) * 2) * 8, 1), :], shape)
        outer = jnp.broadcast_to(r1[pl.ds(((g * 2 + iz) * 2 + 1) * 8, 1), :], shape)
        shift = 64 if odd else 0
        return jnp.where(low_half, roll(inner, shift), roll(outer, shift + ER))

    block = vertex_row(1, 1, True)
    for z in range(EZ):
        block = jnp.where(sub == z, vertex_row(z // 2, 0, z % 2 == 1), block)
    send_block[rows8(24), :] = block
    for copy in block_start(1, 24, 8):
        copy.wait()

    basis = [wide(24)]
    slopes = [differences(basis[0])]
    for k in range(1, ITERS):
        basis.append(vertex_image(slopes[-1]))
        slopes.append(differences(basis[-1]))

    own = (sub >= 4) & jnp.logical_not(low_half)
    roots = [jnp.where(own, jnp.sqrt(edge[0:8, 0:LANES]), 0.0) for edge in edges]
    flows = [[halves(roots[axis] * slope[axis][0:8, 0:LANES]) for axis in range(3)] for slope in slopes]
    points = [halves(jnp.where(own, value[0:8, 0:LANES], 0.0)) for value in basis]

    tiles = [None] * 6
    for e, (i, j) in enumerate(PAIRS):
        if j < ITERS:
            total = two_prod(flows[i][0], flows[j][0])
            for axis in (1, 2):
                total = add2(total, two_prod(flows[i][axis], flows[j][axis]))
        else:
            total = two_prod(points[i], points[0])
        for amount in (2, 1):
            total = add2(total, tuple(pltpu.roll(part, amount, 0) for part in total))
        for half in range(2):
            row_of = jnp.broadcast_to(total[half][7:8, :], shape)
            slot = 2 * (e // 8) + half
            tiles[slot] = row_of if e % 8 == 0 else jnp.where(sub == e % 8, row_of, tiles[slot])
    sent = [0.0, 0.0]
    for t in range(3):
        total = (tiles[2 * t], tiles[2 * t + 1])
        for amount in (64, 32, 16, 8, 4, 2, 1):
            total = add2(total, tuple(roll(part, amount) for part in total))
        pick = tab[rows8((WHERE["pick"] + t) * 8), :] > 0.0
        for half in range(2):
            sent[half] = sent[half] + jnp.sum(jnp.where(pick, total[half], 0.0), axis=0, keepdims=True)
    for half in range(2):
        row_box[0, pl.ds(half, 1), :] = sent[half]

    @pl.loop(1, nr)
    def _(o):
        pltpu.make_async_remote_copy(
            src_ref=row_box.at[0], dst_ref=row_box.at[o], send_sem=row_send, recv_sem=row_recv,
            device_id=(gz, lax.rem(row + o, nr)), device_id_type=mesh_ids,
        ).start()

    def wait_for(box, count, sem):
        rest = box.at[pl.ds(1, count - 1)]
        pltpu.make_async_copy(rest, rest, sem).wait()

    def total_of(box, count):
        parts = [(box[o, pl.ds(0, 1), :], box[o, pl.ds(1, 1), :]) for o in range(count)]
        while len(parts) > 1:
            half = len(parts) // 2
            parts = [add2(parts[k], parts[k + half]) for k in range(half)] + parts[2 * half :]
        return parts[0]

    wait_for(row_box, nr, row_recv)
    total = total_of(row_box, nr)
    for half in range(2):
        gz_box[0, pl.ds(half, 1), :] = total[half]

    @pl.loop(1, nz)
    def _(o):
        pltpu.make_async_remote_copy(
            src_ref=gz_box.at[0], dst_ref=gz_box.at[o], send_sem=gz_send, recv_sem=gz_recv,
            device_id=(lax.rem(gz + o, nz), row), device_id_type=mesh_ids,
        ).start()

    wait_for(gz_box, nz, gz_recv)
    total = total_of(gz_box, nz)
    wait_for(row_box, nr, row_send)
    wait_for(gz_box, nz, gz_send)

    system = []
    for half in range(2):
        wide_row = jnp.broadcast_to(total[half], shape)
        part = jnp.zeros(shape, jnp.float32)
        for i in range(ITERS):
            part = jnp.where(sub == i, roll(wide_row, -8 * i), part)
        system.append(jnp.where(lane <= ITERS, part, 0.0))
    start = system[0]
    for p in range(ITERS):
        column = [jnp.broadcast_to(part[:, p : p + 1], shape) for part in system]
        line_p = [jnp.broadcast_to(part[p : p + 1, :], shape) for part in system]
        pivot = [jnp.broadcast_to(part[p : p + 1, :], shape) for part in column]
        least = TINY * jnp.broadcast_to(jnp.broadcast_to(start[p : p + 1, :], shape)[:, p : p + 1], shape)
        usable = pivot[0] > least
        inverse = inverse2((jnp.where(usable, pivot[0], 1.0), jnp.where(usable, pivot[1], 0.0)))
        scaled = mul2(line_p, tuple(jnp.where(usable, part, 0.0) for part in inverse))
        taken = mul2(column, scaled)
        rest = add2(system, (-taken[0], -taken[1]))
        system = [jnp.where(sub == p, scaled[half], rest[half]) for half in range(2)]

    solved = None
    for k in range(ITERS):
        factor = jnp.broadcast_to(jnp.broadcast_to(system[0][k : k + 1, :], (16, LANES))[:, ITERS : ITERS + 1], (16, 256))
        term = factor * basis[k]
        solved = term if solved is None else solved + term

    for ia in range(2):
        at_node = []
        for ir in range(2):
            back = 64 + ER * ia + ir
            at_node.append([pltpu.roll(solved, (shift - back) % 256, 1)[:, 0:LANES] for shift in (0, 64)])
        for g in range(2):
            for iz in range(2):
                row_at = 4 + 2 * g + iz
                pair = [
                    jnp.where(low_half, jnp.broadcast_to(v[0][row_at : row_at + 1], shape), jnp.broadcast_to(v[1][row_at + 1 : row_at + 2], shape))
                    for v in at_node
                ]
                x1[block_at(2, g, iz, ia), :] = jnp.where(sub == 0, pair[0], jnp.where(sub == 1, pair[1], 0.0))

    prolong(x1, 2, 4, (d3, x3), t3, t2)
    apply(d3, o3, 4)
    r3[...] = r3[...] - o3[...]
    smooth_first(inv3, r3, d3, 4)
    apply(d3, o3, 4)
    smooth_second(inv3, r3, d3, x3, o3, 4, True, False)

    prolong(x3, 4, 8, (d7, x7), t1, t2)
    apply(d7, o7, 8)

    def before_last(at):
        left = r7[at, :] - o7[at, :]
        r7[at, :] = left
        d7[at, :] = (1.0 / THETA) * (inv7[at, :] * left)

    blocks(8, before_last)
    apply(d7, o7, 8)
    smooth_second(inv7, r7, d7, x7, o7, 8, True, False)

    @pl.loop(0, 8)
    def _(i):
        rows = pl.ds(pl.multiple_of(i * 64, 64), 64)
        for g in range(2):
            out[rows, pl.ds(g * LANES, LANES)] = x7[pl.ds(pl.multiple_of(g * 512 + i * 64, 64), 64), :]


def per_device(rhs_local, stretch):
    nz = lax.axis_size("gz")
    nr = lax.axis_size("row")
    nodes = (ORDER + 1) ** 3
    elems = EZ * EA * ER
    face_rows = sum(sum(c) * 4 for c in ROUNDS)
    diag_rows = sum(len(c) * 8 for c in ROUNDS)

    def field(rows):
        return pltpu.VMEM((rows, LANES), jnp.float32)

    out = pl.pallas_call(
        functools.partial(kernel, nz, nr),
        out_shape=jax.ShapeDtypeStruct((nodes, elems), jnp.float32),
        in_specs=[pl.BlockSpec(memory_space=pltpu.VMEM)] * 3,
        out_specs=pl.BlockSpec(memory_space=pltpu.VMEM),
        scratch_shapes=[field(1024)] * 5
        + [field(512), field(256)]
        + [field(256)] * 5
        + [field(128)]
        + [field(64)] * 2
        + [field(48)]
        + [
            pltpu.VMEM((4, face_rows, LANES), jnp.float32),
            pltpu.VMEM((4, face_rows, LANES), jnp.float32),
            pltpu.VMEM((4, diag_rows, LANES), jnp.float32),
            pltpu.VMEM((4, diag_rows, LANES), jnp.float32),
            pltpu.VMEM((32, LANES), jnp.float32),
            pltpu.VMEM((8, 32, LANES), jnp.float32),
            pltpu.VMEM((nr, 2, LANES), jnp.float32),
            pltpu.VMEM((nz, 2, LANES), jnp.float32),
            pltpu.SemaphoreType.DMA((len(ROUNDS), 8)),
            pltpu.SemaphoreType.DMA((len(ROUNDS), 8)),
            pltpu.SemaphoreType.DMA((2, 8)),
            pltpu.SemaphoreType.DMA((2, 8)),
            pltpu.SemaphoreType.DMA,
            pltpu.SemaphoreType.DMA,
            pltpu.SemaphoreType.DMA,
            pltpu.SemaphoreType.DMA,
        ],
        compiler_params=pltpu.CompilerParams(
            collective_id=0, has_side_effects=True, vmem_limit_bytes=32 * 1024 * 1024
        ),
    )(rhs_local.reshape(nodes, elems), stretch, jnp.asarray(CONST))
    return out.reshape(rhs_local.shape)


def solution(mesh):
    placed = (P(None, None, None, ("gz", "row")), P(None, ("gz", "row")))
    return jax.shard_map(
        per_device,
        mesh=mesh,
        in_specs=placed,
        out_specs=P(None, None, None, ("gz", "row")),
        check_vma=False,
    )
```

```python
import functools

import numpy as np

import jax
import jax.numpy as jnp
from jax import lax
from jax.experimental import pallas as pl
from jax.experimental.pallas import tpu as pltpu
from jax.sharding import PartitionSpec as P

ORDER = 7
MID = 3
ITERS = 5
EZ = 4
EA = 4
ER = 16
LANES = 128

LOW_BOUND = 0.4
HIGH_BOUND = 4.0
THETA = 0.5 * (HIGH_BOUND + LOW_BOUND)
DELTA = 0.5 * (HIGH_BOUND - LOW_BOUND)
RHO = DELTA / THETA
RHO2 = 1.0 / (2.0 * THETA / DELTA - RHO)

DIRS = ((0, 1), (0, -1), (1, 0), (-1, 0), (1, 1), (1, -1), (-1, 1), (-1, -1))
ROUNDS = ((8, 8, 4), (8,), (4,), (4,), (2,), (4,), (4,), (8,), (8,))
SCALE = 16.0
TINY = 1e-13


def points_of(order):
    return -np.cos(np.pi * np.arange(order + 1) / order)


def tables_of(order):
    x = points_of(order)
    n = order + 1
    place = np.arange(n)
    running = np.ones(n)
    for j in range(1, order // 2 + 1):
        b = 1.0 if 2 * j == order else 2.0
        running = running - b * np.cos(2 * np.pi * j * place / order) / (4 * j * j - 1)
    weights = np.where((place == 0) | (place == order), 1.0, 2.0) / order * running
    gap = x[:, None] - x[None, :] + np.eye(n)
    bary = 1.0 / np.prod(gap, axis=1)
    deriv = bary[None, :] / bary[:, None] / gap * (1.0 - np.eye(n))
    deriv = deriv - np.diag(deriv.sum(axis=1))
    stiff = deriv.T @ (weights[:, None] * deriv)
    return weights, stiff / weights[:, None]


def interpolation(fine_order, coarse_order):
    x = points_of(fine_order)
    y = points_of(coarse_order)
    table = np.ones((fine_order + 1, coarse_order + 1))
    for j in range(coarse_order + 1):
        for k in range(coarse_order + 1):
            if k != j:
                table[:, j] *= (x - y[k]) / (y[j] - y[k])
    return table


WK = {n: tables_of(n - 1) for n in (8, 4, 2)}
UP = {(4, 8): interpolation(7, 3), (2, 4): interpolation(3, 1)}
DOWN = {(8, 4): UP[4, 8].T, (4, 2): UP[2, 4].T}
PAIRS = [(i, j) for i in range(ITERS) for j in range(i, ITERS)] + [(i, ITERS) for i in range(ITERS)]


def column_blocks(table):
    blocks = np.zeros((table.shape[1], 8))
    blocks[:, : table.shape[0]] = table.T
    return blocks


def constant_table():
    blocks, where = [], {}

    def put(name, rows):
        where[name] = sum(len(b) for b in blocks)
        blocks.append(rows)

    for n in (8, 4, 2):
        w, k = WK[n]
        put(("k", n), column_blocks(k))
        put(("w", n), column_blocks(np.outer(w, w)))
        put(("d", n), column_blocks(np.diag(k)[:, None]))
    for key, table in list(UP.items()) + list(DOWN.items()):
        put(("j",) + key, column_blocks(table))
    return np.concatenate(blocks).astype(np.float32), where


CONST, WHERE = constant_table()


def line(table, values, pairs=None):
    rows, cols = table.shape
    half = cols // 2
    even = [values[k] + values[cols - 1 - k] for k in range(half)]
    odd = [values[k] - values[cols - 1 - k] for k in range(half)]
    out = [None] * rows
    for i in range(rows // 2) if pairs is None else pairs:
        e = o = None
        for k in range(half):
            te = float(np.float32(0.5 * (table[i, k] + table[i, cols - 1 - k])))
            to = float(np.float32(0.5 * (table[i, k] - table[i, cols - 1 - k])))
            e = te * even[k] if e is None else e + te * even[k]
            o = to * odd[k] if o is None else o + to * odd[k]
        out[i] = e + o
        out[rows - 1 - i] = e - o
    return out


def rows8(start):
    if isinstance(start, int):
        return pl.ds(start, 8)
    return pl.ds(pl.multiple_of(start, 8), 8)


def roll(value, shift):
    shift = shift % LANES
    return value if shift == 0 else pltpu.roll(value, shift, 1)


def loop(count, body, unroll_all):
    if unroll_all:
        for i in range(count):
            body(i)
    else:
        pl.loop(0, count)(body)


def split(i, size):
    if isinstance(i, int):
        return i // size, i % size
    return lax.div(i, size), lax.rem(i, size)


def two_sum(a, b):
    s = a + b
    t = s - a
    return s, (a - (s - t)) + (b - t)


def halves(a):
    t = 4097.0 * a
    hi = t - (t - a)
    return a, hi, a - hi


def two_prod(x, y):
    a, ah, al = x
    b, bh, bl = y
    p = a * b
    return p, ((ah * bh - p) + ah * bl + al * bh) + al * bl


def add2(x, y):
    s, e = two_sum(x[0], y[0])
    return two_sum(s, e + (x[1] + y[1]))


def mul2(x, y):
    p, e = two_prod(halves(x[0]), halves(y[0]))
    return two_sum(p, e + (x[0] * y[1] + x[1] * y[0]))


def inverse2(x):
    r = 1.0 / x[0]
    p, e = two_prod(halves(x[0]), halves(r))
    return two_sum(r, r * (((1.0 - p) - e) - x[1] * r))


def kernel(
    nz, nr, rhs, stretch_in, out, stretch, tab,
    x7, d7, r7, inv7, o7, t1, t2, x3, d3, r3, inv3, o3, t3, x1, r1, coef,
    send, recv, send_diag, recv_diag, send_block, recv_block, row_box, gz_box,
    load_sem, send_sem, recv_sem, block_send, block_recv, row_send, row_recv, gz_send, gz_recv,
):
    gz = lax.axis_index("gz")
    row = lax.axis_index("row")
    mesh_ids = pl.DeviceIdType.MESH
    shape = (8, LANES)
    lane = lax.broadcasted_iota(jnp.int32, shape, 1)
    sub = lax.broadcasted_iota(jnp.int32, shape, 0)
    in_r = lane % ER
    in_a = (lane // ER) % EA
    low_half = lane < 64

    def as_float(cond):
        return jnp.where(cond, 1.0, 0.0).astype(jnp.float32)

    def at_device(dz, da):
        return (lax.rem(gz + (dz + nz), nz), lax.rem(row + (da + nr), nr))

    barrier = pltpu.get_barrier_semaphore()

    @pl.loop(1, nr)
    def _(o):
        pl.semaphore_signal(barrier, inc=1, device_id=(gz, lax.rem(row + o, nr)), device_id_type=mesh_ids)

    @pl.loop(1, nz)
    def _(o):
        pl.semaphore_signal(barrier, inc=1, device_id=(lax.rem(gz + o, nz), row), device_id_type=mesh_ids)

    for dz, da in DIRS[4:]:
        pl.semaphore_signal(barrier, inc=1, device_id=at_device(dz, da), device_id_type=mesh_ids)

    loads = [pltpu.make_async_copy(stretch_in, stretch, load_sem.at[2])]
    for g in range(2):
        loads.append(
            pltpu.make_async_copy(rhs.at[:, pl.ds(g * LANES, LANES)], r7.at[pl.ds(g * 512, 512)], load_sem.at[g])
        )
    for load in loads:
        load.start()

    for b, values in enumerate(CONST):
        block = jnp.full(shape, float(values[0]), jnp.float32)
        for i in range(1, 8):
            block = jnp.where(sub == i, float(values[i]), block)
        tab[rows8(b * 8), :] = block
    loads[0].wait()

    def const(name, j=0):
        return tab[rows8((WHERE[name] + j) * 8), :]

    def live(n):
        wall = ((sub == 0) & (in_r == 0)) | ((sub == n - 1) & (in_r == ER - 1))
        return jnp.logical_not(wall) & (sub < n)

    for g in range(2):
        for k in range(3):
            coef[rows8((g * 3 + k) * 8), :] = jnp.broadcast_to(
                stretch[pl.ds(k, 1), pl.ds(g * LANES, LANES)], shape
            )

    def coeff(g, k):
        return coef[rows8((g * 3 + k) * 8), :]

    def add_r(field, n, base, stride=8, inner=False):
        lo_at = pl.ds(base, 8, stride=stride)
        hi_at = pl.ds(base + n - 1, 8, stride=stride)
        lo, hi = field[lo_at, :], field[hi_at, :]
        keep = (sub > 0) & (sub < 7) if inner else sub >= 0
        field[lo_at, :] = lo + jnp.where(keep & (in_r > 0), roll(hi, 1), 0.0)
        field[hi_at, :] = hi + jnp.where(keep & (in_r < ER - 1), roll(lo, -1), 0.0)

    def with_r(value):
        from_below = roll(pltpu.roll(value, 1, 0), 1)
        from_above = roll(pltpu.roll(value, 7, 0), -1)
        value = value + jnp.where((sub == 0) & (in_r > 0), from_below, 0.0)
        return value + jnp.where((sub == 7) & (in_r < ER - 1), from_above, 0.0)

    def add_a(field, n, base):
        lo_at, hi_at = rows8(base), rows8(base + (n - 1) * 8)
        lo, hi = field[lo_at, :], field[hi_at, :]
        field[lo_at, :] = lo + jnp.where(in_a > 0, roll(hi, ER), 0.0)
        field[hi_at, :] = hi + jnp.where(in_a < EA - 1, roll(lo, -ER), 0.0)

    def block_at(n, g, iz, ia):
        return rows8(((g * n + iz) * n + ia) * 8)

    def add_z(field, n, which=None):
        for ia in range(n) if which is None else which:
            at = [block_at(n, g, iz, ia) for g, iz in ((0, 0), (1, 0), (0, n - 1), (1, n - 1))]
            lo0, lo1, hi0, hi1 = [field[a, :] for a in at]
            up0, up1, dn0, dn1 = [roll(v, 64) for v in (hi0, hi1, lo0, lo1)]
            field[at[0], :] = lo0 + jnp.where(low_half, 0.0, up0)
            field[at[1], :] = lo1 + jnp.where(low_half, up0, up1)
            field[at[2], :] = hi0 + jnp.where(low_half, dn0, dn1)
            field[at[3], :] = hi1 + jnp.where(low_half, dn1, 0.0)

    def device_sum(field, n):
        loop(2 * n * n // 8, lambda i: add_r(field, n, i * 64), n < 8)
        loop(2 * n, lambda i: add_a(field, n, i * n * 8), n < 8)
        add_z(field, n)

    def shared(iz, ia, n):
        along = jnp.where((sub == 0) | (sub == n - 1), 0.5, 1.0)
        if ia in (0, n - 1):
            along = 0.5 * along
        if isinstance(iz, int):
            return 0.5 * along if iz in (0, n - 1) else along
        return jnp.where((iz == 0) | (iz == n - 1), 0.5, 1.0) * along

    def along_z(field, image, n, g, ia):
        base = g * (n * n * 8) + ia * 8
        got = line(WK[n][1], [field[rows8(base + iz * n * 8), :] for iz in range(n)])
        c0 = coef[rows8(g * 24), :]
        for iz in range(n):
            image[rows8(base + iz * n * 8), :] = c0 * got[iz]

    def rest_values(field, image, n, g, iz, pairs):
        w, k = WK[n]
        base = (g * n + iz) * (n * 8)
        got = line(k, [field[rows8(base + ia * 8), :] for ia in range(n)], pairs)
        c1 = coef[rows8(g * 24 + 8), :]
        c2 = coef[rows8(g * 24 + 16), :]
        scale = tab[rows8((WHERE["w", n] + iz) * 8), :]
        values = []
        for ia in sorted(list(pairs) + [n - 1 - p for p in pairs]):
            at = base + ia * 8
            part = None
            for j in range(n):
                term = const(("k", n), j) * field[pl.ds(at + j, 1), :]
                part = term if part is None else part + term
            values.append((ia, (float(w[ia]) * scale) * (image[rows8(at), :] + c1 * got[ia] + c2 * part)))
        return values

    def element(field, image, n, sums, left=None):
        loop(2 * n, lambda i: along_z(field, image, n, *split(i, n)), n < 8)

        def along_rest(i):
            g, iz = split(i, n)
            for ia, value in rest_values(field, image, n, g, iz, range(n // 2)):
                at = rows8(i * (n * 8) + ia * 8)
                image[at, :] = value if left is None else shared(iz, ia, n) * left[at, :] - value

        loop(2 * n, along_rest, n < 8)
        if sums:
            device_sum(image, n)

    def diagonal(field, n):
        w, k = WK[n]

        def body(i):
            g, iz = split(i, n)
            c0 = coef[rows8(g * 24), :]
            c1 = coef[rows8(g * 24 + 8), :]
            c2 = coef[rows8(g * 24 + 16), :]
            scale = tab[rows8((WHERE["w", n] + iz) * 8), :]
            kz = jnp.broadcast_to(tab[pl.ds(WHERE["d", n] * 8 + iz, 1), :], shape)
            fixed = c0 * kz + c2 * const(("d", n))
            for ia in range(n):
                field[rows8(i * (n * 8) + ia * 8), :] = (float(w[ia]) * scale) * (fixed + float(k[ia, ia]) * c1)

        loop(2 * n, body, n < 8)

    quarter = in_a

    def pack_a(field, n, at):
        half = n // 2
        for m in range(half):
            rows = rows8(at + m * 8)
            to_up = to_down = None
            for k in range(4):
                g, iz = divmod(m + k * half, n)
                up = roll(field[block_at(n, g, iz, n - 1), :], 80 + 16 * k)
                down = roll(field[block_at(n, g, iz, 0), :], 16 * k)
                to_up = up if k == 0 else jnp.where(quarter == k, up, to_up)
                to_down = down if k == 0 else jnp.where(quarter == k, down, to_down)
            send[0, rows, :] = to_up
            send[1, rows, :] = to_down

    def pack_z(field, n, at):
        half = n // 2
        for m in range(half):
            rows = rows8(at + m * 8)
            hi = [field[block_at(n, 1, n - 1, ia), :] for ia in (m, m + half)]
            lo = [field[block_at(n, 0, 0, ia), :] for ia in (m, m + half)]
            send[2, rows, :] = jnp.where(low_half, roll(hi[0], 64), hi[1])
            send[3, rows, :] = jnp.where(low_half, lo[0], roll(lo[1], 64))

    def pack(field, n, at, at_diag):
        pack_a(field, n, at)
        pack_z(field, n, at)
        for d, (g, iz, ia) in enumerate(corners(n)):
            send_diag[d, rows8(at_diag), :] = field[block_at(n, g, iz, ia), :]

    def corners(n):
        return ((1, n - 1, n - 1), (1, n - 1, 0), (0, 0, n - 1), (0, 0, 0))

    def unpack(field, n, at, at_diag):
        half = n // 2

        def add(where, keep, value):
            field[where, :] = field[where, :] + jnp.where(keep, value, 0.0)

        for m in range(half):
            rows = rows8(at + m * 8)
            got = [recv[d, rows, :] for d in range(4)]
            for k in range(4):
                g, iz = divmod(m + k * half, n)
                add(block_at(n, g, iz, 0), in_a == 0, roll(got[0], -16 * k))
                add(block_at(n, g, iz, n - 1), in_a == EA - 1, roll(got[1], 48 - 16 * k))
        for m in range(half):
            rows = rows8(at + m * 8)
            got = [recv[d, rows, :] for d in range(4)]
            for k in range(2):
                add(block_at(n, 0, 0, m + k * half), low_half, roll(got[2], 64 * k))
                add(block_at(n, 1, n - 1, m + k * half), jnp.logical_not(low_half), roll(got[3], 64 - 64 * k))
        rows = rows8(at_diag)
        add(block_at(n, 0, 0, 0), lane < 16, roll(recv_diag[0, rows, :], 16))
        add(block_at(n, 0, 0, n - 1), (lane >= 48) & (lane < 64), roll(recv_diag[1, rows, :], -16))
        add(block_at(n, 1, n - 1, 0), (lane >= 64) & (lane < 80), roll(recv_diag[2, rows, :], 16))
        add(block_at(n, 1, n - 1, n - 1), lane >= 112, roll(recv_diag[3, rows, :], -16))

    offsets, diag_offsets = [0], [0]
    for counts in ROUNDS:
        offsets.append(offsets[-1] + sum(counts) * 4)
        diag_offsets.append(diag_offsets[-1] + len(counts) * 8)
    state = {"next": 0}

    class Round:
        def __init__(self, *fields):
            self.turn = state["next"]
            state["next"] += 1
            self.counts = ROUNDS[self.turn]
            self.at, self.at_diag = offsets[self.turn], diag_offsets[self.turn]
            self.fields = fields
            self.copies = []

        def places(self):
            at, at_diag = self.at, self.at_diag
            for field, n in zip(self.fields, self.counts):
                yield field, n, at, at_diag
                at += n * 4
                at_diag += 8

        def pack(self):
            for place in self.places():
                pack(*place)

        def start(self, which):
            for d in which:
                dz, da = DIRS[d]
                if d < 4:
                    rows = pl.ds(self.at, sum(self.counts) * 4)
                    src, dst = send.at[d, rows], recv.at[d, rows]
                else:
                    rows = pl.ds(self.at_diag, len(self.counts) * 8)
                    src, dst = send_diag.at[d - 4, rows], recv_diag.at[d - 4, rows]
                copy = pltpu.make_async_remote_copy(
                    src_ref=src, dst_ref=dst, send_sem=send_sem.at[self.turn, d], recv_sem=recv_sem.at[self.turn, d],
                    device_id=at_device(dz, da), device_id_type=mesh_ids,
                )
                copy.start()
                self.copies.append(copy)

        def finish(self):
            for copy in self.copies:
                copy.wait()
            for place in self.places():
                unpack(*place)

    LATE_FIRST = (4, 5, 6, 7, 0, 1, 2, 3)

    def block_start(turn, at, count):
        copies = []
        for d, (dz, da) in enumerate(DIRS):
            copy = pltpu.make_async_remote_copy(
                src_ref=send_block.at[pl.ds(at, count)], dst_ref=recv_block.at[d, pl.ds(at, count)],
                send_sem=block_send.at[turn, d], recv_sem=block_recv.at[turn, d],
                device_id=at_device(dz, da), device_id_type=mesh_ids,
            )
            copy.start()
            copies.append(copy)
        return copies

    def wide(at):
        def block(dz, da):
            if (dz, da) == (0, 0):
                return send_block[rows8(at), :]
            return recv_block[DIRS.index((-dz, -da)), rows8(at), :]

        def left_part(dz):
            return jnp.where(low_half, block(dz, -1), roll(block(dz, 0), 64))

        def below(low, own):
            return jnp.where(sub < 4, low, pltpu.roll(own, 4, 0))

        top = jnp.concatenate([below(left_part(-1), left_part(0)), below(block(-1, 1), block(0, 1))], axis=1)
        bottom = jnp.concatenate([left_part(1), block(1, 1)], axis=1)
        return jnp.concatenate([top, bottom], axis=0)

    def exchange(*fields):
        turn = Round(*fields)
        turn.pack()
        turn.start(LATE_FIRST)
        turn.finish()

    def apply(field, image, n):
        if n == 8:
            apply_fine(field, image)
        else:
            element(field, image, n, True)
            exchange(image)

    def apply_fine(field, image):
        turn = Round(image)
        for g in range(2):
            for ia in (0, 7):
                along_z(field, image, 8, g, ia)
        for d, (g, iz) in enumerate(((1, 7), (0, 0))):
            (_, first), (_, last) = rest_values(field, image, 8, g, iz, (0,))
            send_diag[2 * d, rows8(turn.at_diag), :] = with_r(last)
            send_diag[2 * d + 1, rows8(turn.at_diag), :] = with_r(first)
        turn.start((4, 5, 6, 7))

        @pl.loop(0, 16)
        def _(i):
            g, iz = split(i, 8)
            for ia, value in rest_values(field, image, 8, g, iz, (0,)):
                image[rows8(i * 64 + ia * 8), :] = value

        for g in range(2):
            for ia in (0, 7):
                add_r(image, 8, g * 512 + ia * 8, 64)
        for i in range(16):
            add_a(image, 8, i * 64)
        add_z(image, 8, (0, 7))
        pack_a(image, 8, turn.at)
        turn.start((0, 1))

        @pl.loop(0, 12)
        def _(i):
            g, ia = split(i, 6)
            along_z(field, image, 8, g, ia + 1)

        def inner(i):
            g, iz = split(i, 8)
            for ia, value in rest_values(field, image, 8, g, iz, (1, 2, 3)):
                image[rows8(i * 64 + ia * 8), :] = value
            add_r(image, 8, i * 64, 8, True)

        inner(0)
        inner(15)
        pack_z(image, 8, turn.at)
        turn.start((2, 3))
        pl.loop(1, 15)(inner)
        add_z(image, 8, range(1, 7))
        turn.finish()

    def blocks(n, body):
        def step(i):
            if isinstance(i, int):
                body(pl.ds(i * 64, 64))
            else:
                body(pl.ds(pl.multiple_of(i * 64, 64), 64))

        loop(2 * n * n // 8, step, n < 8)

    def masked(n, value):
        keep = jnp.concatenate([as_float(live(n))] * 8, axis=0)
        return keep * value

    for load in loads[1:]:
        load.wait()
    device_sum(r7, 8)
    diagonal(inv7, 8)
    device_sum(inv7, 8)
    diagonal(inv3, 4)
    device_sum(inv3, 4)
    for k in range(3):
        rows = jnp.where(sub < 2, coeff(0, k), coeff(1, k))
        send_block[rows8(k * 8), :] = jnp.where(sub % 2 == 0, rows, roll(rows, 64))
    first_round = Round(r7, inv7, inv3)
    first_round.pack()
    pl.semaphore_wait(barrier, (nr - 1) + (nz - 1) + 4)
    first_round.start(LATE_FIRST)
    stretch_copies = block_start(0, 0, 24)
    first_round.finish()

    def invert(inv, n):
        keep = jnp.concatenate([live(n)] * 8, axis=0)

        def body(at):
            inv[at, :] = jnp.where(keep, 1.0 / jnp.where(keep, inv[at, :], 1.0), 0.0)

        blocks(n, body)

    invert(inv7, 8)
    invert(inv3, 4)

    def smooth_first(inv, r, d, n):
        def body(at):
            d[at, :] = (1.0 / THETA) * (inv[at, :] * r[at, :])

        blocks(n, body)

    def smooth_second(inv, r, d, x, image, n, add, keep_r=True):
        def body(at):
            step = d[at, :]
            left = r[at, :] - image[at, :]
            second = (RHO2 * RHO) * step + (2.0 * RHO2 / DELTA) * (inv[at, :] * left)
            x[at, :] = (x[at, :] + (step + second)) if add else step + second
            if keep_r:
                d[at, :] = second
                r[at, :] = left

        blocks(n, body)

    def r_line(name, field, at, count):
        part = None
        for j in range(count):
            term = const(name, j) * field[pl.ds(at + j, 1), :]
            part = term if part is None else part + term
        return part

    def restrict(fine, nf, nc, coarse, tz, ta):
        table = DOWN[nf, nc]

        def along_z(i):
            g, ia = split(i, nf)
            got = line(table, [fine[rows8((g * nf + iz) * (nf * 8) + ia * 8), :] for iz in range(nf)])
            for c in range(nc):
                tz[rows8((g * nc + c) * (nf * 8) + ia * 8), :] = got[c]

        def along_a(i):
            got = line(table, [tz[rows8(i * (nf * 8) + ia * 8), :] for ia in range(nf)])
            for c in range(nc):
                ta[rows8(i * (nc * 8) + c * 8), :] = got[c]
            for c in range(nc):
                at = i * (nc * 8) + c * 8
                coarse[rows8(at), :] = r_line(("j", nf, nc), ta, at, nf)

        loop(2 * nf, along_z, nf < 8)
        loop(2 * nc, along_a, nf < 8)

    def prolong(coarse, nc, nf, fields, tz, ta):
        table = UP[nc, nf]

        def along_a(i):
            for c in range(nc):
                at = i * (nc * 8) + c * 8
                ta[rows8(at), :] = r_line(("j", nc, nf), coarse, at, nc)
            got = line(table, [ta[rows8(i * (nc * 8) + c * 8), :] for c in range(nc)])
            for ia in range(nf):
                tz[rows8(i * (nf * 8) + ia * 8), :] = got[ia]

        def along_z(i):
            g, ia = split(i, nf)
            got = line(table, [tz[rows8((g * nc + c) * (nf * 8) + ia * 8), :] for c in range(nc)])
            for iz in range(nf):
                at = rows8((g * nf + iz) * (nf * 8) + ia * 8)
                for field in fields:
                    field[at, :] = field[at, :] + got[iz]

        loop(2 * nc, along_a, nf < 8)
        loop(2 * nf, along_z, nf < 8)

    smooth_first(inv7, r7, d7, 8)
    apply(d7, o7, 8)
    smooth_second(inv7, r7, d7, x7, o7, 8, False)
    element(d7, o7, 8, False, left=r7)

    restrict(o7, 8, 4, r3, t1, t2)
    device_sum(r3, 4)
    exchange(r3)
    smooth_first(inv3, r3, d3, 4)
    apply(d3, o3, 4)
    smooth_second(inv3, r3, d3, x3, o3, 4, False)
    element(d3, o3, 4, False, left=r3)

    restrict(o3, 4, 2, r1, t3, t2)
    device_sum(r1, 2)
    exchange(r1)
    r1[...] = masked(2, r1[...])

    for copy in stretch_copies:
        copy.wait()
    lane_wide = lax.broadcasted_iota(jnp.int32, (16, 256), 1)
    inside = lane_wide % ER > 0

    def step(value, axis, amount):
        if axis == 0:
            return pltpu.roll(value, amount % 16, 0)
        return pltpu.roll(value, (amount * (ER if axis == 1 else 1)) % 256, 1)

    edges = []
    for axis in range(3):
        total = wide(axis * 8)
        for other in range(3):
            if other != axis:
                total = total + step(total, other, 1)
        edges.append(0.5 * total)

    def differences(value):
        return [value - step(value, axis, -1) for axis in range(3)]

    def vertex_image(slopes):
        total = None
        for axis in range(3):
            flux = edges[axis] * slopes[axis]
            flux = flux - step(flux, axis, 1)
            total = flux if total is None else total + flux
        return jnp.where(inside, (1.0 / SCALE) * total, 0.0)

    def vertex_row(g, iz, odd):
        inner = jnp.broadcast_to(r1[pl.ds(((g * 2 + iz) * 2) * 8, 1), :], shape)
        outer = jnp.broadcast_to(r1[pl.ds(((g * 2 + iz) * 2 + 1) * 8, 1), :], shape)
        shift = 64 if odd else 0
        return jnp.where(low_half, roll(inner, shift), roll(outer, shift + ER))

    block = vertex_row(1, 1, True)
    for z in range(EZ):
        block = jnp.where(sub == z, vertex_row(z // 2, 0, z % 2 == 1), block)
    send_block[rows8(24), :] = block
    for copy in block_start(1, 24, 8):
        copy.wait()

    basis = [wide(24)]
    slopes = [differences(basis[0])]
    for k in range(1, ITERS):
        basis.append(vertex_image(slopes[-1]))
        slopes.append(differences(basis[-1]))

    own = (sub >= 4) & jnp.logical_not(low_half)
    roots = [jnp.where(own, jnp.sqrt(edge[0:8, 0:LANES]), 0.0) for edge in edges]
    flows = [[halves(roots[axis] * slope[axis][0:8, 0:LANES]) for axis in range(3)] for slope in slopes]
    points = [halves(jnp.where(own, value[0:8, 0:LANES], 0.0)) for value in basis]

    tiles = [None] * 6
    for e, (i, j) in enumerate(PAIRS):
        if j < ITERS:
            total = two_prod(flows[i][0], flows[j][0])
            for axis in (1, 2):
                total = add2(total, two_prod(flows[i][axis], flows[j][axis]))
        else:
            total = two_prod(points[i], points[0])
        for amount in (2, 1):
            total = add2(total, tuple(pltpu.roll(part, amount, 0) for part in total))
        for half in range(2):
            row_of = jnp.broadcast_to(total[half][7:8, :], shape)
            slot = 2 * (e // 8) + half
            tiles[slot] = row_of if e % 8 == 0 else jnp.where(sub == e % 8, row_of, tiles[slot])
    sent = [0.0, 0.0]
    for t in range(3):
        total = (tiles[2 * t], tiles[2 * t + 1])
        for amount in (64, 32, 16, 8, 4, 2, 1):
            total = add2(total, tuple(roll(part, amount) for part in total))
        pick = sub < 0
        for e in range(8 * t, min(8 * t + 8, len(PAIRS))):
            i, j = PAIRS[e]
            spot = lane == 8 * i + j
            if j < ITERS:
                spot = spot | (lane == 8 * j + i)
            pick = pick | ((sub == e % 8) & spot)
        for half in range(2):
            sent[half] = sent[half] + jnp.sum(jnp.where(pick, total[half], 0.0), axis=0, keepdims=True)
    for half in range(2):
        row_box[0, pl.ds(half, 1), :] = sent[half]

    @pl.loop(1, nr)
    def _(o):
        pltpu.make_async_remote_copy(
            src_ref=row_box.at[0], dst_ref=row_box.at[o], send_sem=row_send, recv_sem=row_recv,
            device_id=(gz, lax.rem(row + o, nr)), device_id_type=mesh_ids,
        ).start()

    def wait_for(box, count, sem):
        rest = box.at[pl.ds(1, count - 1)]
        pltpu.make_async_copy(rest, rest, sem).wait()

    def total_of(box, count):
        parts = [(box[o, pl.ds(0, 1), :], box[o, pl.ds(1, 1), :]) for o in range(count)]
        while len(parts) > 1:
            half = len(parts) // 2
            parts = [add2(parts[k], parts[k + half]) for k in range(half)] + parts[2 * half :]
        return parts[0]

    wait_for(row_box, nr, row_recv)
    total = total_of(row_box, nr)
    for half in range(2):
        gz_box[0, pl.ds(half, 1), :] = total[half]

    @pl.loop(1, nz)
    def _(o):
        pltpu.make_async_remote_copy(
            src_ref=gz_box.at[0], dst_ref=gz_box.at[o], send_sem=gz_send, recv_sem=gz_recv,
            device_id=(lax.rem(gz + o, nz), row), device_id_type=mesh_ids,
        ).start()

    wait_for(gz_box, nz, gz_recv)
    total = total_of(gz_box, nz)
    wait_for(row_box, nr, row_send)
    wait_for(gz_box, nz, gz_send)

    system = []
    for half in range(2):
        wide_row = jnp.broadcast_to(total[half], shape)
        part = jnp.zeros(shape, jnp.float32)
        for i in range(ITERS):
            part = jnp.where(sub == i, roll(wide_row, -8 * i), part)
        system.append(jnp.where(lane <= ITERS, part, 0.0))
    start = system[0]
    for p in range(ITERS):
        column = [jnp.broadcast_to(part[:, p : p + 1], shape) for part in system]
        line_p = [jnp.broadcast_to(part[p : p + 1, :], shape) for part in system]
        pivot = [jnp.broadcast_to(part[p : p + 1, :], shape) for part in column]
        least = TINY * jnp.broadcast_to(jnp.broadcast_to(start[p : p + 1, :], shape)[:, p : p + 1], shape)
        usable = pivot[0] > least
        inverse = inverse2((jnp.where(usable, pivot[0], 1.0), jnp.where(usable, pivot[1], 0.0)))
        scaled = mul2(line_p, tuple(jnp.where(usable, part, 0.0) for part in inverse))
        taken = mul2(column, scaled)
        rest = add2(system, (-taken[0], -taken[1]))
        system = [jnp.where(sub == p, scaled[half], rest[half]) for half in range(2)]

    solved = None
    for k in range(ITERS):
        factor = jnp.broadcast_to(jnp.broadcast_to(system[0][k : k + 1, :], (16, LANES))[:, ITERS : ITERS + 1], (16, 256))
        term = factor * basis[k]
        solved = term if solved is None else solved + term

    for ia in range(2):
        at_node = []
        for ir in range(2):
            back = 64 + ER * ia + ir
            at_node.append([pltpu.roll(solved, (shift - back) % 256, 1)[:, 0:LANES] for shift in (0, 64)])
        for g in range(2):
            for iz in range(2):
                row_at = 4 + 2 * g + iz
                pair = [
                    jnp.where(low_half, jnp.broadcast_to(v[0][row_at : row_at + 1], shape), jnp.broadcast_to(v[1][row_at + 1 : row_at + 2], shape))
                    for v in at_node
                ]
                x1[block_at(2, g, iz, ia), :] = jnp.where(sub == 0, pair[0], jnp.where(sub == 1, pair[1], 0.0))

    prolong(x1, 2, 4, (d3, x3), t3, t2)
    apply(d3, o3, 4)
    r3[...] = r3[...] - o3[...]
    smooth_first(inv3, r3, d3, 4)
    apply(d3, o3, 4)
    smooth_second(inv3, r3, d3, x3, o3, 4, True, False)

    prolong(x3, 4, 8, (d7, x7), t1, t2)
    apply(d7, o7, 8)

    def before_last(at):
        left = r7[at, :] - o7[at, :]
        r7[at, :] = left
        d7[at, :] = (1.0 / THETA) * (inv7[at, :] * left)

    blocks(8, before_last)
    apply(d7, o7, 8)
    smooth_second(inv7, r7, d7, x7, o7, 8, True, False)

    @pl.loop(0, 8)
    def _(i):
        rows = pl.ds(pl.multiple_of(i * 64, 64), 64)
        for g in range(2):
            out[rows, pl.ds(g * LANES, LANES)] = x7[pl.ds(pl.multiple_of(g * 512 + i * 64, 64), 64), :]


def per_device(rhs_local, stretch):
    nz = lax.axis_size("gz")
    nr = lax.axis_size("row")
    nodes = (ORDER + 1) ** 3
    elems = EZ * EA * ER
    face_rows = sum(sum(c) * 4 for c in ROUNDS)
    diag_rows = sum(len(c) * 8 for c in ROUNDS)

    def field(rows):
        return pltpu.VMEM((rows, LANES), jnp.float32)

    out = pl.pallas_call(
        functools.partial(kernel, nz, nr),
        out_shape=jax.ShapeDtypeStruct((nodes, elems), jnp.float32),
        in_specs=[pl.BlockSpec(memory_space=pltpu.HBM)] * 2,
        out_specs=pl.BlockSpec(memory_space=pltpu.VMEM),
        scratch_shapes=[pltpu.VMEM((3, elems), jnp.float32), field(CONST.shape[0] * 8)]
        + [field(1024)] * 5
        + [field(512), field(256)]
        + [field(256)] * 5
        + [field(128)]
        + [field(64)] * 2
        + [field(48)]
        + [
            pltpu.VMEM((4, face_rows, LANES), jnp.float32),
            pltpu.VMEM((4, face_rows, LANES), jnp.float32),
            pltpu.VMEM((4, diag_rows, LANES), jnp.float32),
            pltpu.VMEM((4, diag_rows, LANES), jnp.float32),
            pltpu.VMEM((32, LANES), jnp.float32),
            pltpu.VMEM((8, 32, LANES), jnp.float32),
            pltpu.VMEM((nr, 2, LANES), jnp.float32),
            pltpu.VMEM((nz, 2, LANES), jnp.float32),
            pltpu.SemaphoreType.DMA((3,)),
            pltpu.SemaphoreType.DMA((len(ROUNDS), 8)),
            pltpu.SemaphoreType.DMA((len(ROUNDS), 8)),
            pltpu.SemaphoreType.DMA((2, 8)),
            pltpu.SemaphoreType.DMA((2, 8)),
            pltpu.SemaphoreType.DMA,
            pltpu.SemaphoreType.DMA,
            pltpu.SemaphoreType.DMA,
            pltpu.SemaphoreType.DMA,
        ],
        compiler_params=pltpu.CompilerParams(
            collective_id=0, has_side_effects=True, vmem_limit_bytes=32 * 1024 * 1024
        ),
    )(rhs_local.reshape(nodes, elems), stretch)
    return out.reshape(rhs_local.shape)


def solution(mesh):
    placed = (P(None, None, None, ("gz", "row")), P(None, ("gz", "row")))
    return jax.shard_map(
        per_device,
        mesh=mesh,
        in_specs=placed,
        out_specs=P(None, None, None, ("gz", "row")),
        check_vma=False,
    )
```

```python
import functools

import numpy as np

import jax
import jax.numpy as jnp
from jax import lax
from jax.experimental import pallas as pl
from jax.experimental.pallas import tpu as pltpu
from jax.sharding import PartitionSpec as P

ORDER = 7
MID = 3
ITERS = 5
EZ = 4
EA = 4
ER = 16
LANES = 128

LOW_BOUND = 0.4
HIGH_BOUND = 4.0
THETA = 0.5 * (HIGH_BOUND + LOW_BOUND)
DELTA = 0.5 * (HIGH_BOUND - LOW_BOUND)
RHO = DELTA / THETA
RHO2 = 1.0 / (2.0 * THETA / DELTA - RHO)

DIRS = ((0, 1), (0, -1), (1, 0), (-1, 0), (1, 1), (1, -1), (-1, 1), (-1, -1))
FAR_DIRS = tuple((z, a) for z in (2, -2, 1, -1, 0) for a in (2, -2, 1, -1, 0) if (z, a) != (0, 0))
ROUNDS = ((8, 8, 4), (8,), (4,), (4,), (4,) * 6, (4,), (8,), (8,))
SCALE = 16.0
TINY = 1e-13


def points_of(order):
    return -np.cos(np.pi * np.arange(order + 1) / order)


def tables_of(order):
    x = points_of(order)
    n = order + 1
    place = np.arange(n)
    running = np.ones(n)
    for j in range(1, order // 2 + 1):
        b = 1.0 if 2 * j == order else 2.0
        running = running - b * np.cos(2 * np.pi * j * place / order) / (4 * j * j - 1)
    weights = np.where((place == 0) | (place == order), 1.0, 2.0) / order * running
    gap = x[:, None] - x[None, :] + np.eye(n)
    bary = 1.0 / np.prod(gap, axis=1)
    deriv = bary[None, :] / bary[:, None] / gap * (1.0 - np.eye(n))
    deriv = deriv - np.diag(deriv.sum(axis=1))
    stiff = deriv.T @ (weights[:, None] * deriv)
    return weights, stiff / weights[:, None]


def interpolation(fine_order, coarse_order):
    x = points_of(fine_order)
    y = points_of(coarse_order)
    table = np.ones((fine_order + 1, coarse_order + 1))
    for j in range(coarse_order + 1):
        for k in range(coarse_order + 1):
            if k != j:
                table[:, j] *= (x - y[k]) / (y[j] - y[k])
    return table


WK = {n: tables_of(n - 1) for n in (8, 4, 2)}
UP = {(4, 8): interpolation(7, 3), (2, 4): interpolation(3, 1)}
DOWN = {(8, 4): UP[4, 8].T, (4, 2): UP[2, 4].T}
PAIRS = [(i, j) for i in range(ITERS) for j in range(i, ITERS)] + [(i, ITERS) for i in range(ITERS)]


def column_blocks(table):
    blocks = np.zeros((table.shape[1], 8))
    blocks[:, : table.shape[0]] = table.T
    return blocks


def constant_table():
    blocks, where = [], {}

    def put(name, rows):
        where[name] = sum(len(b) for b in blocks)
        blocks.append(rows)

    for n in (8, 4, 2):
        w, k = WK[n]
        put(("k", n), column_blocks(k))
        put(("w", n), column_blocks(np.outer(w, w)))
        put(("d", n), column_blocks(np.diag(k)[:, None]))
    for key, table in list(UP.items()) + list(DOWN.items()):
        put(("j",) + key, column_blocks(table))
    return np.concatenate(blocks).astype(np.float32), where


CONST, WHERE = constant_table()


def line(table, values, pairs=None):
    rows, cols = table.shape
    half = cols // 2
    even = [values[k] + values[cols - 1 - k] for k in range(half)]
    odd = [values[k] - values[cols - 1 - k] for k in range(half)]
    out = [None] * rows
    for i in range(rows // 2) if pairs is None else pairs:
        e = o = None
        for k in range(half):
            te = float(np.float32(0.5 * (table[i, k] + table[i, cols - 1 - k])))
            to = float(np.float32(0.5 * (table[i, k] - table[i, cols - 1 - k])))
            e = te * even[k] if e is None else e + te * even[k]
            o = to * odd[k] if o is None else o + to * odd[k]
        out[i] = e + o
        out[rows - 1 - i] = e - o
    return out


def rows8(start):
    if isinstance(start, int):
        return pl.ds(start, 8)
    return pl.ds(pl.multiple_of(start, 8), 8)


def roll(value, shift):
    shift = shift % LANES
    return value if shift == 0 else pltpu.roll(value, shift, 1)


def loop(count, body, unroll_all):
    if unroll_all:
        for i in range(count):
            body(i)
    else:
        pl.loop(0, count)(body)


def split(i, size):
    if isinstance(i, int):
        return i // size, i % size
    return lax.div(i, size), lax.rem(i, size)


def two_sum(a, b):
    s = a + b
    t = s - a
    return s, (a - (s - t)) + (b - t)


def halves(a):
    t = 4097.0 * a
    hi = t - (t - a)
    return a, hi, a - hi


def two_prod(x, y):
    a, ah, al = x
    b, bh, bl = y
    p = a * b
    return p, ((ah * bh - p) + ah * bl + al * bh) + al * bl


def add2(x, y):
    s, e = two_sum(x[0], y[0])
    return two_sum(s, e + (x[1] + y[1]))


def mul2(x, y):
    p, e = two_prod(halves(x[0]), halves(y[0]))
    return two_sum(p, e + (x[0] * y[1] + x[1] * y[0]))


def inverse2(x):
    r = 1.0 / x[0]
    p, e = two_prod(halves(x[0]), halves(r))
    return two_sum(r, r * (((1.0 - p) - e) - x[1] * r))


def kernel(
    nz, nr, rhs, stretch_in, out, stretch, tab,
    x7, d7, r7, inv7, o7, t1, t2, x3, d3, r3, inv3, o3, t3, x1, r1, coef,
    vertex, lifted, images, send, recv, send_diag, recv_diag, send_block, recv_block, send_point, recv_point, row_box, gz_box,
    load_sem, send_sem, recv_sem, block_send, block_recv, point_send, point_recv, row_send, row_recv, gz_send, gz_recv,
):
    gz = lax.axis_index("gz")
    row = lax.axis_index("row")
    mesh_ids = pl.DeviceIdType.MESH
    shape = (8, LANES)
    lane = lax.broadcasted_iota(jnp.int32, shape, 1)
    sub = lax.broadcasted_iota(jnp.int32, shape, 0)
    in_r = lane % ER
    in_a = (lane // ER) % EA
    low_half = lane < 64

    def as_float(cond):
        return jnp.where(cond, 1.0, 0.0).astype(jnp.float32)

    def at_device(dz, da):
        return (lax.rem(gz + (dz + nz), nz), lax.rem(row + (da + nr), nr))

    barrier = pltpu.get_barrier_semaphore()

    @pl.loop(1, nr)
    def _(o):
        pl.semaphore_signal(barrier, inc=1, device_id=(gz, lax.rem(row + o, nr)), device_id_type=mesh_ids)

    @pl.loop(1, nz)
    def _(o):
        pl.semaphore_signal(barrier, inc=1, device_id=(lax.rem(gz + o, nz), row), device_id_type=mesh_ids)

    askew = [d for d in FAR_DIRS if d[0] != 0 and d[1] != 0]
    for dz, da in askew:
        pl.semaphore_signal(barrier, inc=1, device_id=at_device(dz, da), device_id_type=mesh_ids)

    loads = [pltpu.make_async_copy(stretch_in, stretch, load_sem.at[2])]
    for g in range(2):
        loads.append(
            pltpu.make_async_copy(rhs.at[:, pl.ds(g * LANES, LANES)], r7.at[pl.ds(g * 512, 512)], load_sem.at[g])
        )
    for load in loads:
        load.start()

    for b, values in enumerate(CONST):
        block = jnp.full(shape, float(values[0]), jnp.float32)
        for i in range(1, 8):
            block = jnp.where(sub == i, float(values[i]), block)
        tab[rows8(b * 8), :] = block
    loads[0].wait()

    def const(name, j=0):
        return tab[rows8((WHERE[name] + j) * 8), :]

    def live(n):
        wall = ((sub == 0) & (in_r == 0)) | ((sub == n - 1) & (in_r == ER - 1))
        return jnp.logical_not(wall) & (sub < n)

    for g in range(2):
        for k in range(3):
            coef[rows8((g * 3 + k) * 8), :] = jnp.broadcast_to(
                stretch[pl.ds(k, 1), pl.ds(g * LANES, LANES)], shape
            )

    def coeff(g, k):
        return coef[rows8((g * 3 + k) * 8), :]

    def add_r(field, n, base, stride=8, inner=False):
        lo_at = pl.ds(base, 8, stride=stride)
        hi_at = pl.ds(base + n - 1, 8, stride=stride)
        lo, hi = field[lo_at, :], field[hi_at, :]
        keep = (sub > 0) & (sub < 7) if inner else sub >= 0
        field[lo_at, :] = lo + jnp.where(keep & (in_r > 0), roll(hi, 1), 0.0)
        field[hi_at, :] = hi + jnp.where(keep & (in_r < ER - 1), roll(lo, -1), 0.0)

    def with_r(value):
        from_below = roll(pltpu.roll(value, 1, 0), 1)
        from_above = roll(pltpu.roll(value, 7, 0), -1)
        value = value + jnp.where((sub == 0) & (in_r > 0), from_below, 0.0)
        return value + jnp.where((sub == 7) & (in_r < ER - 1), from_above, 0.0)

    def add_a(field, n, base):
        lo_at, hi_at = rows8(base), rows8(base + (n - 1) * 8)
        lo, hi = field[lo_at, :], field[hi_at, :]
        field[lo_at, :] = lo + jnp.where(in_a > 0, roll(hi, ER), 0.0)
        field[hi_at, :] = hi + jnp.where(in_a < EA - 1, roll(lo, -ER), 0.0)

    def block_at(n, g, iz, ia):
        return rows8(((g * n + iz) * n + ia) * 8)

    def add_z(field, n, which=None):
        for ia in range(n) if which is None else which:
            at = [block_at(n, g, iz, ia) for g, iz in ((0, 0), (1, 0), (0, n - 1), (1, n - 1))]
            lo0, lo1, hi0, hi1 = [field[a, :] for a in at]
            up0, up1, dn0, dn1 = [roll(v, 64) for v in (hi0, hi1, lo0, lo1)]
            field[at[0], :] = lo0 + jnp.where(low_half, 0.0, up0)
            field[at[1], :] = lo1 + jnp.where(low_half, up0, up1)
            field[at[2], :] = hi0 + jnp.where(low_half, dn0, dn1)
            field[at[3], :] = hi1 + jnp.where(low_half, dn1, 0.0)

    def device_sum(field, n):
        loop(2 * n * n // 8, lambda i: add_r(field, n, i * 64), n < 8)
        loop(2 * n, lambda i: add_a(field, n, i * n * 8), n < 8)
        add_z(field, n)

    def shared(iz, ia, n):
        along = jnp.where((sub == 0) | (sub == n - 1), 0.5, 1.0)
        if ia in (0, n - 1):
            along = 0.5 * along
        if isinstance(iz, int):
            return 0.5 * along if iz in (0, n - 1) else along
        return jnp.where((iz == 0) | (iz == n - 1), 0.5, 1.0) * along

    def along_z(field, image, n, g, ia):
        base = g * (n * n * 8) + ia * 8
        got = line(WK[n][1], [field[rows8(base + iz * n * 8), :] for iz in range(n)])
        c0 = coef[rows8(g * 24), :]
        for iz in range(n):
            image[rows8(base + iz * n * 8), :] = c0 * got[iz]

    def rest_values(field, image, n, g, iz, pairs):
        w, k = WK[n]
        base = (g * n + iz) * (n * 8)
        got = line(k, [field[rows8(base + ia * 8), :] for ia in range(n)], pairs)
        c1 = coef[rows8(g * 24 + 8), :]
        c2 = coef[rows8(g * 24 + 16), :]
        scale = tab[rows8((WHERE["w", n] + iz) * 8), :]
        values = []
        for ia in sorted(list(pairs) + [n - 1 - p for p in pairs]):
            at = base + ia * 8
            part = None
            for j in range(n):
                term = const(("k", n), j) * field[pl.ds(at + j, 1), :]
                part = term if part is None else part + term
            values.append((ia, (float(w[ia]) * scale) * (image[rows8(at), :] + c1 * got[ia] + c2 * part)))
        return values

    def element(field, image, n, sums, left=None):
        loop(2 * n, lambda i: along_z(field, image, n, *split(i, n)), n < 8)

        def along_rest(i):
            g, iz = split(i, n)
            for ia, value in rest_values(field, image, n, g, iz, range(n // 2)):
                at = rows8(i * (n * 8) + ia * 8)
                image[at, :] = value if left is None else shared(iz, ia, n) * left[at, :] - value

        loop(2 * n, along_rest, n < 8)
        if sums:
            device_sum(image, n)

    def diagonal(field, n):
        w, k = WK[n]

        def body(i):
            g, iz = split(i, n)
            c0 = coef[rows8(g * 24), :]
            c1 = coef[rows8(g * 24 + 8), :]
            c2 = coef[rows8(g * 24 + 16), :]
            scale = tab[rows8((WHERE["w", n] + iz) * 8), :]
            kz = jnp.broadcast_to(tab[pl.ds(WHERE["d", n] * 8 + iz, 1), :], shape)
            fixed = c0 * kz + c2 * const(("d", n))
            for ia in range(n):
                field[rows8(i * (n * 8) + ia * 8), :] = (float(w[ia]) * scale) * (fixed + float(k[ia, ia]) * c1)

        loop(2 * n, body, n < 8)

    quarter = in_a

    def pack_a(field, n, at):
        half = n // 2
        for m in range(half):
            rows = rows8(at + m * 8)
            to_up = to_down = None
            for k in range(4):
                g, iz = divmod(m + k * half, n)
                up = roll(field[block_at(n, g, iz, n - 1), :], 80 + 16 * k)
                down = roll(field[block_at(n, g, iz, 0), :], 16 * k)
                to_up = up if k == 0 else jnp.where(quarter == k, up, to_up)
                to_down = down if k == 0 else jnp.where(quarter == k, down, to_down)
            send[0, rows, :] = to_up
            send[1, rows, :] = to_down

    def pack_z(field, n, at):
        half = n // 2
        for m in range(half):
            rows = rows8(at + m * 8)
            hi = [field[block_at(n, 1, n - 1, ia), :] for ia in (m, m + half)]
            lo = [field[block_at(n, 0, 0, ia), :] for ia in (m, m + half)]
            send[2, rows, :] = jnp.where(low_half, roll(hi[0], 64), hi[1])
            send[3, rows, :] = jnp.where(low_half, lo[0], roll(lo[1], 64))

    def pack(field, n, at, at_diag):
        pack_a(field, n, at)
        pack_z(field, n, at)
        for d, (g, iz, ia) in enumerate(corners(n)):
            send_diag[d, rows8(at_diag), :] = field[block_at(n, g, iz, ia), :]

    def corners(n):
        return ((1, n - 1, n - 1), (1, n - 1, 0), (0, 0, n - 1), (0, 0, 0))

    def unpack(field, n, at, at_diag):
        half = n // 2

        def add(where, keep, value):
            field[where, :] = field[where, :] + jnp.where(keep, value, 0.0)

        for m in range(half):
            rows = rows8(at + m * 8)
            got = [recv[d, rows, :] for d in range(4)]
            for k in range(4):
                g, iz = divmod(m + k * half, n)
                add(block_at(n, g, iz, 0), in_a == 0, roll(got[0], -16 * k))
                add(block_at(n, g, iz, n - 1), in_a == EA - 1, roll(got[1], 48 - 16 * k))
        for m in range(half):
            rows = rows8(at + m * 8)
            got = [recv[d, rows, :] for d in range(4)]
            for k in range(2):
                add(block_at(n, 0, 0, m + k * half), low_half, roll(got[2], 64 * k))
                add(block_at(n, 1, n - 1, m + k * half), jnp.logical_not(low_half), roll(got[3], 64 - 64 * k))
        rows = rows8(at_diag)
        add(block_at(n, 0, 0, 0), lane < 16, roll(recv_diag[0, rows, :], 16))
        add(block_at(n, 0, 0, n - 1), (lane >= 48) & (lane < 64), roll(recv_diag[1, rows, :], -16))
        add(block_at(n, 1, n - 1, 0), (lane >= 64) & (lane < 80), roll(recv_diag[2, rows, :], 16))
        add(block_at(n, 1, n - 1, n - 1), lane >= 112, roll(recv_diag[3, rows, :], -16))

    offsets, diag_offsets = [0], [0]
    for counts in ROUNDS:
        offsets.append(offsets[-1] + sum(counts) * 4)
        diag_offsets.append(diag_offsets[-1] + len(counts) * 8)
    state = {"next": 0}

    class Round:
        def __init__(self, *fields):
            self.turn = state["next"]
            state["next"] += 1
            self.counts = ROUNDS[self.turn]
            self.at, self.at_diag = offsets[self.turn], diag_offsets[self.turn]
            self.fields = fields
            self.copies = []

        def places(self):
            at, at_diag = self.at, self.at_diag
            for field, n in zip(self.fields, self.counts):
                yield field, n, at, at_diag
                at += n * 4
                at_diag += 8

        def pack(self):
            for place in self.places():
                pack(*place)

        def start(self, which):
            for d in which:
                dz, da = DIRS[d]
                if d < 4:
                    rows = pl.ds(self.at, sum(self.counts) * 4)
                    src, dst = send.at[d, rows], recv.at[d, rows]
                else:
                    rows = pl.ds(self.at_diag, len(self.counts) * 8)
                    src, dst = send_diag.at[d - 4, rows], recv_diag.at[d - 4, rows]
                copy = pltpu.make_async_remote_copy(
                    src_ref=src, dst_ref=dst, send_sem=send_sem.at[self.turn, d], recv_sem=recv_sem.at[self.turn, d],
                    device_id=at_device(dz, da), device_id_type=mesh_ids,
                )
                copy.start()
                self.copies.append(copy)

        def finish(self):
            for copy in self.copies:
                copy.wait()
            for place in self.places():
                unpack(*place)

    LATE_FIRST = (4, 5, 6, 7, 0, 1, 2, 3)

    def send_all(dirs, src, dst, sends, recvs):
        copies = []
        for d, (dz, da) in enumerate(dirs):
            copy = pltpu.make_async_remote_copy(
                src_ref=src, dst_ref=dst.at[d], send_sem=sends.at[d], recv_sem=recvs.at[d],
                device_id=at_device(dz, da), device_id_type=mesh_ids,
            )
            copy.start()
            copies.append(copy)
        return copies

    def wide(at):
        def block(dz, da):
            if (dz, da) == (0, 0):
                return send_block[rows8(at), :]
            return recv_block[DIRS.index((-dz, -da)), rows8(at), :]

        def left_part(dz):
            return jnp.where(low_half, block(dz, -1), roll(block(dz, 0), 64))

        def below(low, own):
            return jnp.where(sub < 4, low, pltpu.roll(own, 4, 0))

        top = jnp.concatenate([below(left_part(-1), left_part(0)), below(block(-1, 1), block(0, 1))], axis=1)
        bottom = jnp.concatenate([left_part(1), block(1, 1)], axis=1)
        return jnp.concatenate([top, bottom], axis=0)

    def exchange(*fields):
        turn = Round(*fields)
        turn.pack()
        turn.start(LATE_FIRST)
        turn.finish()

    def apply(field, image, n):
        if n == 8:
            apply_fine(field, image)
        else:
            element(field, image, n, True)
            exchange(image)

    def apply_fine(field, image):
        turn = Round(image)
        for g in range(2):
            for ia in (0, 7):
                along_z(field, image, 8, g, ia)
        for d, (g, iz) in enumerate(((1, 7), (0, 0))):
            (_, first), (_, last) = rest_values(field, image, 8, g, iz, (0,))
            send_diag[2 * d, rows8(turn.at_diag), :] = with_r(last)
            send_diag[2 * d + 1, rows8(turn.at_diag), :] = with_r(first)
        turn.start((4, 5, 6, 7))

        @pl.loop(0, 16)
        def _(i):
            g, iz = split(i, 8)
            for ia, value in rest_values(field, image, 8, g, iz, (0,)):
                image[rows8(i * 64 + ia * 8), :] = value

        for g in range(2):
            for ia in (0, 7):
                add_r(image, 8, g * 512 + ia * 8, 64)
        for i in range(16):
            add_a(image, 8, i * 64)
        add_z(image, 8, (0, 7))
        pack_a(image, 8, turn.at)
        turn.start((0, 1))

        @pl.loop(0, 12)
        def _(i):
            g, ia = split(i, 6)
            along_z(field, image, 8, g, ia + 1)

        def inner(i):
            g, iz = split(i, 8)
            for ia, value in rest_values(field, image, 8, g, iz, (1, 2, 3)):
                image[rows8(i * 64 + ia * 8), :] = value
            add_r(image, 8, i * 64, 8, True)

        inner(0)
        inner(15)
        pack_z(image, 8, turn.at)
        turn.start((2, 3))
        pl.loop(1, 15)(inner)
        add_z(image, 8, range(1, 7))
        turn.finish()

    def blocks(n, body):
        def step(i):
            if isinstance(i, int):
                body(pl.ds(i * 64, 64))
            else:
                body(pl.ds(pl.multiple_of(i * 64, 64), 64))

        loop(2 * n * n // 8, step, n < 8)

    def masked(n, value):
        keep = jnp.concatenate([as_float(live(n))] * 8, axis=0)
        return keep * value

    for load in loads[1:]:
        load.wait()
    device_sum(r7, 8)
    diagonal(inv7, 8)
    device_sum(inv7, 8)
    diagonal(inv3, 4)
    device_sum(inv3, 4)
    for k in range(3):
        rows = jnp.where(sub < 2, coeff(0, k), coeff(1, k))
        send_block[rows8(k * 8), :] = jnp.where(sub % 2 == 0, rows, roll(rows, 64))
    first_round = Round(r7, inv7, inv3)
    first_round.pack()
    pl.semaphore_wait(barrier, (nr - 1) + (nz - 1) + len(askew))
    first_round.start(LATE_FIRST)
    stretch_copies = send_all(DIRS, send_block, recv_block, block_send, block_recv)
    first_round.finish()

    def invert(inv, n):
        keep = jnp.concatenate([live(n)] * 8, axis=0)

        def body(at):
            inv[at, :] = jnp.where(keep, 1.0 / jnp.where(keep, inv[at, :], 1.0), 0.0)

        blocks(n, body)

    invert(inv7, 8)
    invert(inv3, 4)

    def smooth_first(inv, r, d, n):
        def body(at):
            d[at, :] = (1.0 / THETA) * (inv[at, :] * r[at, :])

        blocks(n, body)

    def smooth_second(inv, r, d, x, image, n, add, keep_r=True):
        def body(at):
            step = d[at, :]
            left = r[at, :] - image[at, :]
            second = (RHO2 * RHO) * step + (2.0 * RHO2 / DELTA) * (inv[at, :] * left)
            x[at, :] = (x[at, :] + (step + second)) if add else step + second
            if keep_r:
                d[at, :] = second
                r[at, :] = left

        blocks(n, body)

    def r_line(name, field, at, count):
        part = None
        for j in range(count):
            term = const(name, j) * field[pl.ds(at + j, 1), :]
            part = term if part is None else part + term
        return part

    def restrict(fine, nf, nc, coarse, tz, ta):
        table = DOWN[nf, nc]

        def along_z(i):
            g, ia = split(i, nf)
            got = line(table, [fine[rows8((g * nf + iz) * (nf * 8) + ia * 8), :] for iz in range(nf)])
            for c in range(nc):
                tz[rows8((g * nc + c) * (nf * 8) + ia * 8), :] = got[c]

        def along_a(i):
            got = line(table, [tz[rows8(i * (nf * 8) + ia * 8), :] for ia in range(nf)])
            for c in range(nc):
                ta[rows8(i * (nc * 8) + c * 8), :] = got[c]
            for c in range(nc):
                at = i * (nc * 8) + c * 8
                coarse[rows8(at), :] = r_line(("j", nf, nc), ta, at, nf)

        loop(2 * nf, along_z, nf < 8)
        loop(2 * nc, along_a, nf < 8)

    def prolong(coarse, nc, nf, fields, tz, ta, add=True):
        table = UP[nc, nf]

        def along_a(i):
            for c in range(nc):
                at = i * (nc * 8) + c * 8
                ta[rows8(at), :] = r_line(("j", nc, nf), coarse, at, nc)
            got = line(table, [ta[rows8(i * (nc * 8) + c * 8), :] for c in range(nc)])
            for ia in range(nf):
                tz[rows8(i * (nf * 8) + ia * 8), :] = got[ia]

        def along_z(i):
            g, ia = split(i, nf)
            got = line(table, [tz[rows8((g * nc + c) * (nf * 8) + ia * 8), :] for c in range(nc)])
            for iz in range(nf):
                at = rows8((g * nf + iz) * (nf * 8) + ia * 8)
                for field in fields:
                    field[at, :] = field[at, :] + got[iz] if add else got[iz]

        loop(2 * nc, along_a, nf < 8)
        loop(2 * nf, along_z, nf < 8)

    smooth_first(inv7, r7, d7, 8)
    apply(d7, o7, 8)
    smooth_second(inv7, r7, d7, x7, o7, 8, False)
    element(d7, o7, 8, False, left=r7)

    restrict(o7, 8, 4, r3, t1, t2)
    device_sum(r3, 4)
    exchange(r3)
    smooth_first(inv3, r3, d3, 4)
    apply(d3, o3, 4)
    smooth_second(inv3, r3, d3, x3, o3, 4, False)
    element(d3, o3, 4, False, left=r3)

    restrict(o3, 4, 2, r1, t3, t2)
    per_z = []
    for iz in range(2):
        per_a = []
        for ia in range(2):
            at = [((g * 2 + iz) * 2 + ia) * 8 for g in range(2)]
            per_r = []
            for ir in range(2):
                rows = jnp.where(sub < 2, r1[pl.ds(at[0] + ir, 1), :], r1[pl.ds(at[1] + ir, 1), :])
                rows = jnp.where(sub % 2 == 0, rows, roll(rows, 64))
                per_r.append(jnp.where((sub < 4) & low_half, rows, 0.0))
            per_a.append(per_r[0] + roll(per_r[1], 1))
        per_z.append(per_a[0] + roll(per_a[1], ER))
    send_point[...] = per_z[0] + pltpu.roll(per_z[1], 1, 0)
    point_copies = send_all(FAR_DIRS, send_point, recv_point, point_send, point_recv)

    for copy in stretch_copies:
        copy.wait()
    lane_wide = lax.broadcasted_iota(jnp.int32, (16, 256), 1)
    inside = lane_wide % ER > 0

    def step(value, axis, amount):
        if axis == 0:
            return pltpu.roll(value, amount % 16, 0)
        return pltpu.roll(value, (amount * (ER if axis == 1 else 1)) % 256, 1)

    edges = []
    for axis in range(3):
        total = wide(axis * 8)
        for other in range(3):
            if other != axis:
                total = total + step(total, other, 1)
        edges.append(0.5 * total)

    def differences(value):
        return [value - step(value, axis, -1) for axis in range(3)]

    def vertex_image(slopes):
        total = None
        for axis in range(3):
            flux = edges[axis] * slopes[axis]
            flux = flux - step(flux, axis, 1)
            total = flux if total is None else total + flux
        return jnp.where(inside, (1.0 / SCALE) * total, 0.0)

    def summed_points():
        def from_device(dz, da):
            if (dz, da) == (0, 0):
                return send_point[...]
            return recv_point[FAR_DIRS.index((-dz, -da))]

        left, right = [], []
        for dz in (-2, -1, 0, 1, 2):
            far_left, near_left, mine, near_right, far_right = [from_device(dz, da) for da in (-2, -1, 0, 1, 2)]
            turned = roll(mine, 64)
            left.append(near_left + jnp.where(low_half, jnp.where(lane < ER, roll(far_left, 64), 0.0), turned))
            far_right = jnp.where((lane >= 64) & (lane < 64 + ER), roll(far_right, 64), 0.0)
            right.append(near_right + jnp.where(lane < ER, turned, far_right))
        halves_of = []
        for far_low, near_low, mine, near_high, far_high in (left, right):
            turned, far_low, far_high = [pltpu.roll(v, 4, 0) for v in (mine, far_low, far_high)]
            top = near_low + jnp.where(sub >= 4, turned, jnp.where(sub == 0, far_low, 0.0))
            bottom = near_high + jnp.where(sub == 0, turned, jnp.where(sub == 4, far_high, 0.0))
            halves_of.append(jnp.concatenate([top, bottom], axis=0))
        return jnp.where(inside, jnp.concatenate(halves_of, axis=1), 0.0)

    for copy in point_copies:
        copy.wait()
    basis = [summed_points()]
    slopes = [differences(basis[0])]
    for k in range(1, ITERS):
        basis.append(vertex_image(slopes[-1]))
        slopes.append(differences(basis[-1]))
    for k in range(ITERS):
        vertex[k] = basis[k]

    own = (sub >= 4) & jnp.logical_not(low_half)
    roots = [jnp.where(own, jnp.sqrt(edge[0:8, 0:LANES]), 0.0) for edge in edges]
    flows = [[halves(roots[axis] * slope[axis][0:8, 0:LANES]) for axis in range(3)] for slope in slopes]
    points = [halves(jnp.where(own, value[0:8, 0:LANES], 0.0)) for value in basis]

    tiles = [None] * 6
    for e, (i, j) in enumerate(PAIRS):
        if j < ITERS:
            total = two_prod(flows[i][0], flows[j][0])
            for axis in (1, 2):
                total = add2(total, two_prod(flows[i][axis], flows[j][axis]))
        else:
            total = two_prod(points[i], points[0])
        for amount in (2, 1):
            total = add2(total, tuple(pltpu.roll(part, amount, 0) for part in total))
        for half in range(2):
            row_of = jnp.broadcast_to(total[half][7:8, :], shape)
            slot = 2 * (e // 8) + half
            tiles[slot] = row_of if e % 8 == 0 else jnp.where(sub == e % 8, row_of, tiles[slot])
    sent = [0.0, 0.0]
    for t in range(3):
        total = (tiles[2 * t], tiles[2 * t + 1])
        for amount in (64, 32, 16, 8, 4, 2, 1):
            total = add2(total, tuple(roll(part, amount) for part in total))
        pick = sub < 0
        for e in range(8 * t, min(8 * t + 8, len(PAIRS))):
            i, j = PAIRS[e]
            spot = lane == 8 * i + j
            if j < ITERS:
                spot = spot | (lane == 8 * j + i)
            pick = pick | ((sub == e % 8) & spot)
        for half in range(2):
            sent[half] = sent[half] + jnp.sum(jnp.where(pick, total[half], 0.0), axis=0, keepdims=True)
    for half in range(2):
        row_box[0, pl.ds(half, 1), :] = sent[half]

    @pl.loop(1, nr)
    def _(o):
        pltpu.make_async_remote_copy(
            src_ref=row_box.at[0], dst_ref=row_box.at[o], send_sem=row_send, recv_sem=row_recv,
            device_id=(gz, lax.rem(row + o, nr)), device_id_type=mesh_ids,
        ).start()

    def wait_for(box, count, sem):
        rest = box.at[pl.ds(1, count - 1)]
        pltpu.make_async_copy(rest, rest, sem).wait()

    def total_of(box, count):
        parts = [(box[o, pl.ds(0, 1), :], box[o, pl.ds(1, 1), :]) for o in range(count)]
        while len(parts) > 1:
            half = len(parts) // 2
            parts = [add2(parts[k], parts[k + half]) for k in range(half)] + parts[2 * half :]
        return parts[0]

    @pl.loop(0, ITERS)
    def _(k):
        value = vertex[k]
        for ia in range(2):
            at_node = []
            for ir in range(2):
                back = 64 + ER * ia + ir
                at_node.append([pltpu.roll(value, (shift - back) % 256, 1)[:, 0:LANES] for shift in (0, 64)])
            for g in range(2):
                for iz in range(2):
                    row_at = 4 + 2 * g + iz
                    pair = [
                        jnp.where(
                            low_half,
                            jnp.broadcast_to(v[0][row_at : row_at + 1], shape),
                            jnp.broadcast_to(v[1][row_at + 1 : row_at + 2], shape),
                        )
                        for v in at_node
                    ]
                    x1[block_at(2, g, iz, ia), :] = jnp.where(sub == 0, pair[0], jnp.where(sub == 1, pair[1], 0.0))
        prolong(x1, 2, 4, (lifted.at[k],), t3, t2, False)

    lifted[ITERS] = d3[...]

    @pl.loop(0, ITERS + 1)
    def _(k):
        element(lifted.at[k], images.at[k], 4, True)

    lifted_round = Round(*[images.at[k] for k in range(ITERS + 1)])
    lifted_round.pack()
    lifted_round.start(LATE_FIRST)

    wait_for(row_box, nr, row_recv)
    total = total_of(row_box, nr)
    for half in range(2):
        gz_box[0, pl.ds(half, 1), :] = total[half]

    @pl.loop(1, nz)
    def _(o):
        pltpu.make_async_remote_copy(
            src_ref=gz_box.at[0], dst_ref=gz_box.at[o], send_sem=gz_send, recv_sem=gz_recv,
            device_id=(lax.rem(gz + o, nz), row), device_id_type=mesh_ids,
        ).start()

    lifted_round.finish()
    wait_for(gz_box, nz, gz_recv)
    total = total_of(gz_box, nz)
    wait_for(row_box, nr, row_send)
    wait_for(gz_box, nz, gz_send)

    system = []
    for half in range(2):
        wide_row = jnp.broadcast_to(total[half], shape)
        part = jnp.zeros(shape, jnp.float32)
        for i in range(ITERS):
            part = jnp.where(sub == i, roll(wide_row, -8 * i), part)
        system.append(jnp.where(lane <= ITERS, part, 0.0))
    start = system[0]
    for p in range(ITERS):
        column = [jnp.broadcast_to(part[:, p : p + 1], shape) for part in system]
        line_p = [jnp.broadcast_to(part[p : p + 1, :], shape) for part in system]
        pivot = [jnp.broadcast_to(part[p : p + 1, :], shape) for part in column]
        least = TINY * jnp.broadcast_to(jnp.broadcast_to(start[p : p + 1, :], shape)[:, p : p + 1], shape)
        usable = pivot[0] > least
        inverse = inverse2((jnp.where(usable, pivot[0], 1.0), jnp.where(usable, pivot[1], 0.0)))
        scaled = mul2(line_p, tuple(jnp.where(usable, part, 0.0) for part in inverse))
        taken = mul2(column, scaled)
        rest = add2(system, (-taken[0], -taken[1]))
        system = [jnp.where(sub == p, scaled[half], rest[half]) for half in range(2)]

    factors = []
    for k in range(ITERS):
        factor = jnp.broadcast_to(system[0][k : k + 1, :], shape)[:, ITERS : ITERS + 1]
        factors.append(jnp.concatenate([jnp.broadcast_to(factor, shape)] * 8, axis=0))

    def correct(at):
        gain, image = x3[at, :], images[ITERS, at, :]
        for k in range(ITERS):
            gain = gain + factors[k] * lifted[k, at, :]
            image = image + factors[k] * images[k, at, :]
        x3[at, :] = gain
        r3[at, :] = r3[at, :] - image

    blocks(4, correct)
    smooth_first(inv3, r3, d3, 4)
    apply(d3, o3, 4)
    smooth_second(inv3, r3, d3, x3, o3, 4, True, False)

    prolong(x3, 4, 8, (d7, x7), t1, t2)
    apply(d7, o7, 8)

    def before_last(at):
        left = r7[at, :] - o7[at, :]
        r7[at, :] = left
        d7[at, :] = (1.0 / THETA) * (inv7[at, :] * left)

    blocks(8, before_last)
    apply(d7, o7, 8)
    smooth_second(inv7, r7, d7, x7, o7, 8, True, False)

    @pl.loop(0, 8)
    def _(i):
        rows = pl.ds(pl.multiple_of(i * 64, 64), 64)
        for g in range(2):
            out[rows, pl.ds(g * LANES, LANES)] = x7[pl.ds(pl.multiple_of(g * 512 + i * 64, 64), 64), :]


def per_device(rhs_local, stretch):
    nz = lax.axis_size("gz")
    nr = lax.axis_size("row")
    nodes = (ORDER + 1) ** 3
    elems = EZ * EA * ER
    face_rows = sum(sum(c) * 4 for c in ROUNDS)
    diag_rows = sum(len(c) * 8 for c in ROUNDS)

    def field(rows):
        return pltpu.VMEM((rows, LANES), jnp.float32)

    out = pl.pallas_call(
        functools.partial(kernel, nz, nr),
        out_shape=jax.ShapeDtypeStruct((nodes, elems), jnp.float32),
        in_specs=[pl.BlockSpec(memory_space=pltpu.HBM)] * 2,
        out_specs=pl.BlockSpec(memory_space=pltpu.VMEM),
        scratch_shapes=[pltpu.VMEM((3, elems), jnp.float32), field(CONST.shape[0] * 8)]
        + [field(1024)] * 5
        + [field(512), field(256)]
        + [field(256)] * 5
        + [field(128)]
        + [field(64)] * 2
        + [field(48)]
        + [
            pltpu.VMEM((ITERS, 16, 256), jnp.float32),
            pltpu.VMEM((ITERS + 1, 256, LANES), jnp.float32),
            pltpu.VMEM((ITERS + 1, 256, LANES), jnp.float32),
            pltpu.VMEM((4, face_rows, LANES), jnp.float32),
            pltpu.VMEM((4, face_rows, LANES), jnp.float32),
            pltpu.VMEM((4, diag_rows, LANES), jnp.float32),
            pltpu.VMEM((4, diag_rows, LANES), jnp.float32),
            pltpu.VMEM((24, LANES), jnp.float32),
            pltpu.VMEM((8, 24, LANES), jnp.float32),
            pltpu.VMEM((8, LANES), jnp.float32),
            pltpu.VMEM((len(FAR_DIRS), 8, LANES), jnp.float32),
            pltpu.VMEM((nr, 2, LANES), jnp.float32),
            pltpu.VMEM((nz, 2, LANES), jnp.float32),
            pltpu.SemaphoreType.DMA((3,)),
            pltpu.SemaphoreType.DMA((len(ROUNDS), 8)),
            pltpu.SemaphoreType.DMA((len(ROUNDS), 8)),
            pltpu.SemaphoreType.DMA((8,)),
            pltpu.SemaphoreType.DMA((8,)),
            pltpu.SemaphoreType.DMA((len(FAR_DIRS),)),
            pltpu.SemaphoreType.DMA((len(FAR_DIRS),)),
            pltpu.SemaphoreType.DMA,
            pltpu.SemaphoreType.DMA,
            pltpu.SemaphoreType.DMA,
            pltpu.SemaphoreType.DMA,
        ],
        compiler_params=pltpu.CompilerParams(
            collective_id=0, has_side_effects=True, vmem_limit_bytes=32 * 1024 * 1024
        ),
    )(rhs_local.reshape(nodes, elems), stretch)
    return out.reshape(rhs_local.shape)


def solution(mesh):
    placed = (P(None, None, None, ("gz", "row")), P(None, ("gz", "row")))
    return jax.shard_map(
        per_device,
        mesh=mesh,
        in_specs=placed,
        out_specs=P(None, None, None, ("gz", "row")),
        check_vma=False,
    )
```

```python
import functools

import numpy as np

import jax
import jax.numpy as jnp
from jax import lax
from jax.experimental import pallas as pl
from jax.experimental.pallas import tpu as pltpu
from jax.sharding import PartitionSpec as P

ORDER = 7
MID = 3
ITERS = 5
EZ = 4
EA = 4
ER = 16
LANES = 128

LOW_BOUND = 0.4
HIGH_BOUND = 4.0
THETA = 0.5 * (HIGH_BOUND + LOW_BOUND)
DELTA = 0.5 * (HIGH_BOUND - LOW_BOUND)
RHO = DELTA / THETA
RHO2 = 1.0 / (2.0 * THETA / DELTA - RHO)

DIRS = ((0, 1), (0, -1), (1, 0), (-1, 0), (1, 1), (1, -1), (-1, 1), (-1, -1))
FAR_DIRS = tuple((z, a) for z in (2, -2, 1, -1, 0) for a in (2, -2, 1, -1, 0) if (z, a) != (0, 0))
ROUNDS = ((8, 8, 4), (8,), (4,), (4,), (4,) * 6, (4,), (8,), (8,))
SCALE = 16.0
TINY = 1e-13


def points_of(order):
    return -np.cos(np.pi * np.arange(order + 1) / order)


def tables_of(order):
    x = points_of(order)
    n = order + 1
    place = np.arange(n)
    running = np.ones(n)
    for j in range(1, order // 2 + 1):
        b = 1.0 if 2 * j == order else 2.0
        running = running - b * np.cos(2 * np.pi * j * place / order) / (4 * j * j - 1)
    weights = np.where((place == 0) | (place == order), 1.0, 2.0) / order * running
    gap = x[:, None] - x[None, :] + np.eye(n)
    bary = 1.0 / np.prod(gap, axis=1)
    deriv = bary[None, :] / bary[:, None] / gap * (1.0 - np.eye(n))
    deriv = deriv - np.diag(deriv.sum(axis=1))
    stiff = deriv.T @ (weights[:, None] * deriv)
    return weights, stiff / weights[:, None]


def interpolation(fine_order, coarse_order):
    x = points_of(fine_order)
    y = points_of(coarse_order)
    table = np.ones((fine_order + 1, coarse_order + 1))
    for j in range(coarse_order + 1):
        for k in range(coarse_order + 1):
            if k != j:
                table[:, j] *= (x - y[k]) / (y[j] - y[k])
    return table


WK = {n: tables_of(n - 1) for n in (8, 4, 2)}
UP = {(4, 8): interpolation(7, 3), (2, 4): interpolation(3, 1)}
DOWN = {(8, 4): UP[4, 8].T, (4, 2): UP[2, 4].T}
PAIRS = [(i, j) for i in range(ITERS) for j in range(i, ITERS)] + [(i, ITERS) for i in range(ITERS)]


def column_blocks(table):
    blocks = np.zeros((table.shape[1], 8))
    blocks[:, : table.shape[0]] = table.T
    return blocks


def constant_table():
    blocks, where = [], {}

    def put(name, rows):
        where[name] = sum(len(b) for b in blocks)
        blocks.append(rows)

    for n in (8, 4, 2):
        w, k = WK[n]
        put(("k", n), column_blocks(k))
        put(("w", n), column_blocks(np.outer(w, w)))
        put(("d", n), column_blocks(np.diag(k)[:, None]))
    for key, table in list(UP.items()) + list(DOWN.items()):
        put(("j",) + key, column_blocks(table))
    return np.concatenate(blocks).astype(np.float32), where


CONST, WHERE = constant_table()


def line(table, values, pairs=None):
    rows, cols = table.shape
    half = cols // 2
    even = [values[k] + values[cols - 1 - k] for k in range(half)]
    odd = [values[k] - values[cols - 1 - k] for k in range(half)]
    out = [None] * rows
    for i in range(rows // 2) if pairs is None else pairs:
        e = o = None
        for k in range(half):
            te = float(np.float32(0.5 * (table[i, k] + table[i, cols - 1 - k])))
            to = float(np.float32(0.5 * (table[i, k] - table[i, cols - 1 - k])))
            e = te * even[k] if e is None else e + te * even[k]
            o = to * odd[k] if o is None else o + to * odd[k]
        out[i] = e + o
        out[rows - 1 - i] = e - o
    return out


def rows8(start):
    if isinstance(start, int):
        return pl.ds(start, 8)
    return pl.ds(pl.multiple_of(start, 8), 8)


def roll(value, shift):
    shift = shift % LANES
    return value if shift == 0 else pltpu.roll(value, shift, 1)


def loop(count, body, unroll_all):
    if unroll_all:
        for i in range(count):
            body(i)
    else:
        pl.loop(0, count, unroll=2)(body)


def split(i, size):
    if isinstance(i, int):
        return i // size, i % size
    return lax.div(i, size), lax.rem(i, size)


def two_sum(a, b):
    s = a + b
    t = s - a
    return s, (a - (s - t)) + (b - t)


def halves(a):
    t = 4097.0 * a
    hi = t - (t - a)
    return a, hi, a - hi


def two_prod(x, y):
    a, ah, al = x
    b, bh, bl = y
    p = a * b
    return p, ((ah * bh - p) + ah * bl + al * bh) + al * bl


def add2(x, y):
    s, e = two_sum(x[0], y[0])
    return two_sum(s, e + (x[1] + y[1]))


def mul2(x, y):
    p, e = two_prod(halves(x[0]), halves(y[0]))
    return two_sum(p, e + (x[0] * y[1] + x[1] * y[0]))


def inverse2(x):
    r = 1.0 / x[0]
    p, e = two_prod(halves(x[0]), halves(r))
    return two_sum(r, r * (((1.0 - p) - e) - x[1] * r))


def kernel(
    nz, nr, rhs, stretch_in, out, stretch, tab,
    x7, d7, r7, inv7, o7, t1, t2, x3, d3, r3, inv3, o3, t3, x1, r1, coef,
    vertex, lifted, images, send, recv, send_diag, recv_diag, send_block, recv_block, send_point, recv_point, row_box, gz_box,
    load_sem, send_sem, recv_sem, block_send, block_recv, point_send, point_recv, row_send, row_recv, gz_send, gz_recv,
):
    gz = lax.axis_index("gz")
    row = lax.axis_index("row")
    mesh_ids = pl.DeviceIdType.MESH
    shape = (8, LANES)
    lane = lax.broadcasted_iota(jnp.int32, shape, 1)
    sub = lax.broadcasted_iota(jnp.int32, shape, 0)
    in_r = lane % ER
    in_a = (lane // ER) % EA
    low_half = lane < 64

    def as_float(cond):
        return jnp.where(cond, 1.0, 0.0).astype(jnp.float32)

    def at_device(dz, da):
        return (lax.rem(gz + (dz + nz), nz), lax.rem(row + (da + nr), nr))

    barrier = pltpu.get_barrier_semaphore()

    @pl.loop(1, nr)
    def _(o):
        pl.semaphore_signal(barrier, inc=1, device_id=(gz, lax.rem(row + o, nr)), device_id_type=mesh_ids)

    @pl.loop(1, nz)
    def _(o):
        pl.semaphore_signal(barrier, inc=1, device_id=(lax.rem(gz + o, nz), row), device_id_type=mesh_ids)

    askew = [d for d in FAR_DIRS if d[0] != 0 and d[1] != 0]
    for dz, da in askew:
        pl.semaphore_signal(barrier, inc=1, device_id=at_device(dz, da), device_id_type=mesh_ids)

    loads = [pltpu.make_async_copy(stretch_in, stretch, load_sem.at[2])]
    for g in range(2):
        loads.append(
            pltpu.make_async_copy(rhs.at[:, pl.ds(g * LANES, LANES)], r7.at[pl.ds(g * 512, 512)], load_sem.at[g])
        )
    for load in loads:
        load.start()

    for b, values in enumerate(CONST):
        block = jnp.full(shape, float(values[0]), jnp.float32)
        for i in range(1, 8):
            block = jnp.where(sub == i, float(values[i]), block)
        tab[rows8(b * 8), :] = block
    loads[0].wait()

    def const(name, j=0):
        return tab[rows8((WHERE[name] + j) * 8), :]

    def live(n):
        wall = ((sub == 0) & (in_r == 0)) | ((sub == n - 1) & (in_r == ER - 1))
        return jnp.logical_not(wall) & (sub < n)

    for g in range(2):
        for k in range(3):
            coef[rows8((g * 3 + k) * 8), :] = jnp.broadcast_to(
                stretch[pl.ds(k, 1), pl.ds(g * LANES, LANES)], shape
            )

    def coeff(g, k):
        return coef[rows8((g * 3 + k) * 8), :]

    def add_r(field, n, base, stride=8, inner=False):
        lo_at = pl.ds(base, 8, stride=stride)
        hi_at = pl.ds(base + n - 1, 8, stride=stride)
        lo, hi = field[lo_at, :], field[hi_at, :]
        keep = (sub % n > 0) & (sub % n < n - 1) if inner else sub >= 0
        field[lo_at, :] = lo + jnp.where(keep & (in_r > 0), roll(hi, 1), 0.0)
        field[hi_at, :] = hi + jnp.where(keep & (in_r < ER - 1), roll(lo, -1), 0.0)

    def with_r(value, n):
        from_below = roll(pltpu.roll(value, 9 - n, 0), 1)
        from_above = roll(pltpu.roll(value, n - 1, 0), -1)
        value = value + jnp.where((sub == 0) & (in_r > 0), from_below, 0.0)
        return value + jnp.where((sub == n - 1) & (in_r < ER - 1), from_above, 0.0)

    def add_a(field, n, base):
        lo_at, hi_at = rows8(base), rows8(base + (n - 1) * 8)
        lo, hi = field[lo_at, :], field[hi_at, :]
        field[lo_at, :] = lo + jnp.where(in_a > 0, roll(hi, ER), 0.0)
        field[hi_at, :] = hi + jnp.where(in_a < EA - 1, roll(lo, -ER), 0.0)

    def block_at(n, g, iz, ia):
        return rows8(((g * n + iz) * n + ia) * 8)

    def add_z(field, n, which=None):
        for ia in range(n) if which is None else which:
            at = [block_at(n, g, iz, ia) for g, iz in ((0, 0), (1, 0), (0, n - 1), (1, n - 1))]
            lo0, lo1, hi0, hi1 = [field[a, :] for a in at]
            up0, up1, dn0, dn1 = [roll(v, 64) for v in (hi0, hi1, lo0, lo1)]
            field[at[0], :] = lo0 + jnp.where(low_half, 0.0, up0)
            field[at[1], :] = lo1 + jnp.where(low_half, up0, up1)
            field[at[2], :] = hi0 + jnp.where(low_half, dn0, dn1)
            field[at[3], :] = hi1 + jnp.where(low_half, dn1, 0.0)

    def device_sum(field, n):
        loop(2 * n * n // 8, lambda i: add_r(field, n, i * 64), n < 8)
        loop(2 * n, lambda i: add_a(field, n, i * n * 8), n < 8)
        add_z(field, n)

    def shared(iz, ia, n):
        along = jnp.where((sub == 0) | (sub == n - 1), 0.5, 1.0)
        if ia in (0, n - 1):
            along = 0.5 * along
        if isinstance(iz, int):
            return 0.5 * along if iz in (0, n - 1) else along
        return jnp.where((iz == 0) | (iz == n - 1), 0.5, 1.0) * along

    def along_z(field, image, n, g, ia):
        base = g * (n * n * 8) + ia * 8
        got = line(WK[n][1], [field[rows8(base + iz * n * 8), :] for iz in range(n)])
        c0 = coef[rows8(g * 24), :]
        for iz in range(n):
            image[rows8(base + iz * n * 8), :] = c0 * got[iz]

    def rest_values(field, image, n, g, iz, pairs):
        w, k = WK[n]
        base = (g * n + iz) * (n * 8)
        got = line(k, [field[rows8(base + ia * 8), :] for ia in range(n)], pairs)
        c1 = coef[rows8(g * 24 + 8), :]
        c2 = coef[rows8(g * 24 + 16), :]
        scale = tab[rows8((WHERE["w", n] + iz) * 8), :]
        values = []
        for ia in sorted(list(pairs) + [n - 1 - p for p in pairs]):
            at = base + ia * 8
            part = None
            for j in range(n):
                term = const(("k", n), j) * field[pl.ds(at + j, 1), :]
                part = term if part is None else part + term
            values.append((ia, (float(w[ia]) * scale) * (image[rows8(at), :] + c1 * got[ia] + c2 * part)))
        return values

    def element(field, image, n, sums, left=None):
        loop(2 * n, lambda i: along_z(field, image, n, *split(i, n)), n < 8)

        def along_rest(i):
            g, iz = split(i, n)
            for ia, value in rest_values(field, image, n, g, iz, range(n // 2)):
                at = rows8(i * (n * 8) + ia * 8)
                image[at, :] = value if left is None else shared(iz, ia, n) * left[at, :] - value

        loop(2 * n, along_rest, n < 8)
        if sums:
            device_sum(image, n)

    def diagonal(field, n):
        w, k = WK[n]

        def body(i):
            g, iz = split(i, n)
            c0 = coef[rows8(g * 24), :]
            c1 = coef[rows8(g * 24 + 8), :]
            c2 = coef[rows8(g * 24 + 16), :]
            scale = tab[rows8((WHERE["w", n] + iz) * 8), :]
            kz = jnp.broadcast_to(tab[pl.ds(WHERE["d", n] * 8 + iz, 1), :], shape)
            fixed = c0 * kz + c2 * const(("d", n))
            for ia in range(n):
                field[rows8(i * (n * 8) + ia * 8), :] = (float(w[ia]) * scale) * (fixed + float(k[ia, ia]) * c1)

        loop(2 * n, body, n < 8)

    quarter = in_a

    def pack_a(field, n, at):
        half = n // 2
        for m in range(half):
            rows = rows8(at + m * 8)
            to_up = to_down = None
            for k in range(4):
                g, iz = divmod(m + k * half, n)
                up = roll(field[block_at(n, g, iz, n - 1), :], 80 + 16 * k)
                down = roll(field[block_at(n, g, iz, 0), :], 16 * k)
                to_up = up if k == 0 else jnp.where(quarter == k, up, to_up)
                to_down = down if k == 0 else jnp.where(quarter == k, down, to_down)
            send[0, rows, :] = to_up
            send[1, rows, :] = to_down

    def pack_z(field, n, at):
        half = n // 2
        for m in range(half):
            rows = rows8(at + m * 8)
            hi = [field[block_at(n, 1, n - 1, ia), :] for ia in (m, m + half)]
            lo = [field[block_at(n, 0, 0, ia), :] for ia in (m, m + half)]
            send[2, rows, :] = jnp.where(low_half, roll(hi[0], 64), hi[1])
            send[3, rows, :] = jnp.where(low_half, lo[0], roll(lo[1], 64))

    def pack(field, n, at, at_diag):
        pack_a(field, n, at)
        pack_z(field, n, at)
        for d, (g, iz, ia) in enumerate(corners(n)):
            send_diag[d, rows8(at_diag), :] = field[block_at(n, g, iz, ia), :]

    def corners(n):
        return ((1, n - 1, n - 1), (1, n - 1, 0), (0, 0, n - 1), (0, 0, 0))

    def unpack(field, n, at, at_diag, fix=None):
        half = n // 2

        def add(place, keep, value):
            value = jnp.where(keep, value, 0.0)
            if fix is not None:
                fix(place, value)
            else:
                where = block_at(n, *place)
                field[where, :] = field[where, :] + value

        for m in range(half):
            rows = rows8(at + m * 8)
            got = [recv[d, rows, :] for d in range(4)]
            for k in range(4):
                g, iz = divmod(m + k * half, n)
                add((g, iz, 0), in_a == 0, roll(got[0], -16 * k))
                add((g, iz, n - 1), in_a == EA - 1, roll(got[1], 48 - 16 * k))
        for m in range(half):
            rows = rows8(at + m * 8)
            got = [recv[d, rows, :] for d in range(4)]
            for k in range(2):
                add((0, 0, m + k * half), low_half, roll(got[2], 64 * k))
                add((1, n - 1, m + k * half), jnp.logical_not(low_half), roll(got[3], 64 - 64 * k))
        rows = rows8(at_diag)
        add((0, 0, 0), lane < 16, roll(recv_diag[0, rows, :], 16))
        add((0, 0, n - 1), (lane >= 48) & (lane < 64), roll(recv_diag[1, rows, :], -16))
        add((1, n - 1, 0), (lane >= 64) & (lane < 80), roll(recv_diag[2, rows, :], 16))
        add((1, n - 1, n - 1), lane >= 112, roll(recv_diag[3, rows, :], -16))

    offsets, diag_offsets = [0], [0]
    for counts in ROUNDS:
        offsets.append(offsets[-1] + sum(counts) * 4)
        diag_offsets.append(diag_offsets[-1] + len(counts) * 8)
    state = {"next": 0}

    class Round:
        def __init__(self, *fields):
            self.turn = state["next"]
            state["next"] += 1
            self.counts = ROUNDS[self.turn]
            self.at, self.at_diag = offsets[self.turn], diag_offsets[self.turn]
            self.fields = fields
            self.copies = []

        def places(self):
            at, at_diag = self.at, self.at_diag
            for field, n in zip(self.fields, self.counts):
                yield field, n, at, at_diag
                at += n * 4
                at_diag += 8

        def pack(self):
            for place in self.places():
                pack(*place)

        def start(self, which):
            for d in which:
                dz, da = DIRS[d]
                if d < 4:
                    rows = pl.ds(self.at, sum(self.counts) * 4)
                    src, dst = send.at[d, rows], recv.at[d, rows]
                else:
                    rows = pl.ds(self.at_diag, len(self.counts) * 8)
                    src, dst = send_diag.at[d - 4, rows], recv_diag.at[d - 4, rows]
                copy = pltpu.make_async_remote_copy(
                    src_ref=src, dst_ref=dst, send_sem=send_sem.at[self.turn, d], recv_sem=recv_sem.at[self.turn, d],
                    device_id=at_device(dz, da), device_id_type=mesh_ids,
                )
                copy.start()
                self.copies.append(copy)

        def finish(self, fix=None):
            for copy in self.copies:
                copy.wait()
            for place in self.places():
                unpack(*place, fix)

    LATE_FIRST = (4, 5, 6, 7, 0, 1, 2, 3)

    def send_all(dirs, src, dst, sends, recvs):
        copies = []
        for d, (dz, da) in enumerate(dirs):
            copy = pltpu.make_async_remote_copy(
                src_ref=src, dst_ref=dst.at[d], send_sem=sends.at[d], recv_sem=recvs.at[d],
                device_id=at_device(dz, da), device_id_type=mesh_ids,
            )
            copy.start()
            copies.append(copy)
        return copies

    def wide(at):
        def block(dz, da):
            if (dz, da) == (0, 0):
                return send_block[rows8(at), :]
            return recv_block[DIRS.index((-dz, -da)), rows8(at), :]

        def left_part(dz):
            return jnp.where(low_half, block(dz, -1), roll(block(dz, 0), 64))

        def below(low, own):
            return jnp.where(sub < 4, low, pltpu.roll(own, 4, 0))

        top = jnp.concatenate([below(left_part(-1), left_part(0)), below(block(-1, 1), block(0, 1))], axis=1)
        bottom = jnp.concatenate([left_part(1), block(1, 1)], axis=1)
        return jnp.concatenate([top, bottom], axis=0)

    def exchange(*fields):
        turn = Round(*fields)
        turn.pack()
        turn.start(LATE_FIRST)
        turn.finish()

    def apply(field, image, n, during, fix):
        turn = Round(image)
        ends = (0, n - 1)
        for g in range(2):
            for ia in ends:
                along_z(field, image, n, g, ia)
        for d, (g, iz) in enumerate(((1, n - 1), (0, 0))):
            (_, first), (_, last) = rest_values(field, image, n, g, iz, (0,))
            send_diag[2 * d, rows8(turn.at_diag), :] = with_r(last, n)
            send_diag[2 * d + 1, rows8(turn.at_diag), :] = with_r(first, n)
        turn.start((4, 5, 6, 7))

        def outer(i):
            g, iz = split(i, n)
            for ia, value in rest_values(field, image, n, g, iz, (0,)):
                image[rows8(i * (n * 8) + ia * 8), :] = value

        loop(2 * n, outer, n < 8)
        for q in range(2 * n // 8):
            for ia in ends:
                add_r(image, n, q * (n * 64) + ia * 8, n * 8)
        for i in range(2 * n):
            add_a(image, n, i * n * 8)
        add_z(image, n, ends)
        pack_a(image, n, turn.at)
        turn.start((0, 1))

        def inner_z(i):
            g, ia = split(i, n - 2)
            along_z(field, image, n, g, ia + 1)

        loop(2 * (n - 2), inner_z, n < 8)

        def inner(q):
            for part in range(8 // n):
                i = q * (8 // n) + part
                g, iz = split(i, n)
                for ia, value in rest_values(field, image, n, g, iz, range(1, n // 2)):
                    image[rows8(i * (n * 8) + ia * 8), :] = value
            add_r(image, n, q * 64, 8, True)

        groups = 2 * n * n // 8
        inner(0)
        inner(groups - 1)
        pack_z(image, n, turn.at)
        turn.start((2, 3))
        loop(groups - 2, lambda q: inner(q + 1), n < 8)
        add_z(image, n, range(1, n - 1))
        during()
        turn.finish(fix)

    def blocks(n, body):
        def step(i):
            if isinstance(i, int):
                body(pl.ds(i * 64, 64))
            else:
                body(pl.ds(pl.multiple_of(i * 64, 64), 64))

        loop(2 * n * n // 8, step, n < 8)

    def masked(n, value):
        keep = jnp.concatenate([as_float(live(n))] * 8, axis=0)
        return keep * value

    for load in loads[1:]:
        load.wait()
    device_sum(r7, 8)
    diagonal(inv7, 8)
    device_sum(inv7, 8)
    diagonal(inv3, 4)
    device_sum(inv3, 4)
    for k in range(3):
        rows = jnp.where(sub < 2, coeff(0, k), coeff(1, k))
        send_block[rows8(k * 8), :] = jnp.where(sub % 2 == 0, rows, roll(rows, 64))
    first_round = Round(r7, inv7, inv3)
    first_round.pack()
    pl.semaphore_wait(barrier, (nr - 1) + (nz - 1) + len(askew))
    first_round.start(LATE_FIRST)
    stretch_copies = send_all(DIRS, send_block, recv_block, block_send, block_recv)
    first_round.finish()

    def invert(inv, n):
        keep = jnp.concatenate([live(n)] * 8, axis=0)

        def body(at):
            inv[at, :] = jnp.where(keep, 1.0 / jnp.where(keep, inv[at, :], 1.0), 0.0)

        blocks(n, body)

    invert(inv7, 8)
    invert(inv3, 4)

    def smooth_first(inv, r, d, n):
        def body(at):
            d[at, :] = (1.0 / THETA) * (inv[at, :] * r[at, :])

        blocks(n, body)

    def smooth_second(inv, r, d, x, image, n, result=None):
        def body(at):
            step = d[at, :]
            left = r[at, :] - image[at, :]
            second = (RHO2 * RHO) * step + (2.0 * RHO2 / DELTA) * (inv[at, :] * left)
            if result is None:
                x[at, :] = step + second
                d[at, :] = second
                r[at, :] = left
            else:
                result(at, x[at, :] + (step + second))

        def fix(place, value):
            at = block_at(n, *place)
            change = (2.0 * RHO2 / DELTA) * (inv[at, :] * value)
            if result is None:
                r[at, :] = r[at, :] - value
                d[at, :] = d[at, :] - change
                x[at, :] = x[at, :] - change
            elif n == 8:
                g, iz, ia = place
                spot = rows8((iz * 8 + ia) * 8), pl.ds(g * LANES, LANES)
                out[spot] = out[spot] - change
            else:
                x[at, :] = x[at, :] - change

        apply(d, image, n, lambda: blocks(n, body), fix)

    def r_line(name, field, at, count):
        part = None
        for j in range(count):
            term = const(name, j) * field[pl.ds(at + j, 1), :]
            part = term if part is None else part + term
        return part

    def restrict(fine, nf, nc, coarse, tz, ta):
        table = DOWN[nf, nc]

        def along_z(i):
            g, ia = split(i, nf)
            got = line(table, [fine[rows8((g * nf + iz) * (nf * 8) + ia * 8), :] for iz in range(nf)])
            for c in range(nc):
                tz[rows8((g * nc + c) * (nf * 8) + ia * 8), :] = got[c]

        def along_a(i):
            got = line(table, [tz[rows8(i * (nf * 8) + ia * 8), :] for ia in range(nf)])
            for c in range(nc):
                ta[rows8(i * (nc * 8) + c * 8), :] = got[c]
            for c in range(nc):
                at = i * (nc * 8) + c * 8
                coarse[rows8(at), :] = r_line(("j", nf, nc), ta, at, nf)

        loop(2 * nf, along_z, nf < 8)
        loop(2 * nc, along_a, nf < 8)

    def prolong(coarse, nc, nf, fields, tz, ta, add=True):
        table = UP[nc, nf]

        def along_a(i):
            for c in range(nc):
                at = i * (nc * 8) + c * 8
                ta[rows8(at), :] = r_line(("j", nc, nf), coarse, at, nc)
            got = line(table, [ta[rows8(i * (nc * 8) + c * 8), :] for c in range(nc)])
            for ia in range(nf):
                tz[rows8(i * (nf * 8) + ia * 8), :] = got[ia]

        def along_z(i):
            g, ia = split(i, nf)
            got = line(table, [tz[rows8((g * nc + c) * (nf * 8) + ia * 8), :] for c in range(nc)])
            for iz in range(nf):
                at = rows8((g * nf + iz) * (nf * 8) + ia * 8)
                for field in fields:
                    field[at, :] = field[at, :] + got[iz] if add else got[iz]

        loop(2 * nc, along_a, nf < 8)
        loop(2 * nf, along_z, nf < 8)

    smooth_first(inv7, r7, d7, 8)
    smooth_second(inv7, r7, d7, x7, o7, 8)
    element(d7, o7, 8, False, left=r7)

    restrict(o7, 8, 4, r3, t1, t2)
    device_sum(r3, 4)
    exchange(r3)
    smooth_first(inv3, r3, d3, 4)
    smooth_second(inv3, r3, d3, x3, o3, 4)
    element(d3, o3, 4, False, left=r3)

    restrict(o3, 4, 2, r1, t3, t2)
    per_z = []
    for iz in range(2):
        per_a = []
        for ia in range(2):
            at = [((g * 2 + iz) * 2 + ia) * 8 for g in range(2)]
            per_r = []
            for ir in range(2):
                rows = jnp.where(sub < 2, r1[pl.ds(at[0] + ir, 1), :], r1[pl.ds(at[1] + ir, 1), :])
                rows = jnp.where(sub % 2 == 0, rows, roll(rows, 64))
                per_r.append(jnp.where((sub < 4) & low_half, rows, 0.0))
            per_a.append(per_r[0] + roll(per_r[1], 1))
        per_z.append(per_a[0] + roll(per_a[1], ER))
    send_point[...] = per_z[0] + pltpu.roll(per_z[1], 1, 0)
    point_copies = send_all(FAR_DIRS, send_point, recv_point, point_send, point_recv)

    for copy in stretch_copies:
        copy.wait()
    lane_wide = lax.broadcasted_iota(jnp.int32, (16, 256), 1)
    inside = lane_wide % ER > 0

    def step(value, axis, amount):
        if axis == 0:
            return pltpu.roll(value, amount % 16, 0)
        return pltpu.roll(value, (amount * (ER if axis == 1 else 1)) % 256, 1)

    edges = []
    for axis in range(3):
        total = wide(axis * 8)
        for other in range(3):
            if other != axis:
                total = total + step(total, other, 1)
        edges.append(0.5 * total)

    def differences(value):
        return [value - step(value, axis, -1) for axis in range(3)]

    def vertex_image(slopes):
        total = None
        for axis in range(3):
            flux = edges[axis] * slopes[axis]
            flux = flux - step(flux, axis, 1)
            total = flux if total is None else total + flux
        return jnp.where(inside, (1.0 / SCALE) * total, 0.0)

    def summed_points():
        def from_device(dz, da):
            if (dz, da) == (0, 0):
                return send_point[...]
            return recv_point[FAR_DIRS.index((-dz, -da))]

        left, right = [], []
        for dz in (-2, -1, 0, 1, 2):
            far_left, near_left, mine, near_right, far_right = [from_device(dz, da) for da in (-2, -1, 0, 1, 2)]
            turned = roll(mine, 64)
            left.append(near_left + jnp.where(low_half, jnp.where(lane < ER, roll(far_left, 64), 0.0), turned))
            far_right = jnp.where((lane >= 64) & (lane < 64 + ER), roll(far_right, 64), 0.0)
            right.append(near_right + jnp.where(lane < ER, turned, far_right))
        halves_of = []
        for far_low, near_low, mine, near_high, far_high in (left, right):
            turned, far_low, far_high = [pltpu.roll(v, 4, 0) for v in (mine, far_low, far_high)]
            top = near_low + jnp.where(sub >= 4, turned, jnp.where(sub == 0, far_low, 0.0))
            bottom = near_high + jnp.where(sub == 0, turned, jnp.where(sub == 4, far_high, 0.0))
            halves_of.append(jnp.concatenate([top, bottom], axis=0))
        return jnp.where(inside, jnp.concatenate(halves_of, axis=1), 0.0)

    for copy in point_copies:
        copy.wait()
    basis = [summed_points()]
    slopes = [differences(basis[0])]
    for k in range(1, ITERS):
        basis.append(vertex_image(slopes[-1]))
        slopes.append(differences(basis[-1]))
    for k in range(ITERS):
        vertex[k] = basis[k]

    own = (sub >= 4) & jnp.logical_not(low_half)
    roots = [jnp.where(own, jnp.sqrt(edge[0:8, 0:LANES]), 0.0) for edge in edges]
    flows = [[halves(roots[axis] * slope[axis][0:8, 0:LANES]) for axis in range(3)] for slope in slopes]
    points = [halves(jnp.where(own, value[0:8, 0:LANES], 0.0)) for value in basis]

    tiles = [None] * 6
    for e, (i, j) in enumerate(PAIRS):
        if j < ITERS:
            total = two_prod(flows[i][0], flows[j][0])
            for axis in (1, 2):
                total = add2(total, two_prod(flows[i][axis], flows[j][axis]))
        else:
            total = two_prod(points[i], points[0])
        for amount in (2, 1):
            total = add2(total, tuple(pltpu.roll(part, amount, 0) for part in total))
        for half in range(2):
            row_of = jnp.broadcast_to(total[half][7:8, :], shape)
            slot = 2 * (e // 8) + half
            tiles[slot] = row_of if e % 8 == 0 else jnp.where(sub == e % 8, row_of, tiles[slot])
    sent = [0.0, 0.0]
    for t in range(3):
        total = (tiles[2 * t], tiles[2 * t + 1])
        for amount in (64, 32, 16, 8, 4, 2, 1):
            total = add2(total, tuple(roll(part, amount) for part in total))
        pick = sub < 0
        for e in range(8 * t, min(8 * t + 8, len(PAIRS))):
            i, j = PAIRS[e]
            spot = lane == 8 * i + j
            if j < ITERS:
                spot = spot | (lane == 8 * j + i)
            pick = pick | ((sub == e % 8) & spot)
        for half in range(2):
            sent[half] = sent[half] + jnp.sum(jnp.where(pick, total[half], 0.0), axis=0, keepdims=True)
    for half in range(2):
        row_box[0, pl.ds(half, 1), :] = sent[half]

    @pl.loop(1, nr)
    def _(o):
        pltpu.make_async_remote_copy(
            src_ref=row_box.at[0], dst_ref=row_box.at[o], send_sem=row_send, recv_sem=row_recv,
            device_id=(gz, lax.rem(row + o, nr)), device_id_type=mesh_ids,
        ).start()

    def wait_for(box, count, sem):
        rest = box.at[pl.ds(1, count - 1)]
        pltpu.make_async_copy(rest, rest, sem).wait()

    def total_of(box, count):
        parts = [(box[o, pl.ds(0, 1), :], box[o, pl.ds(1, 1), :]) for o in range(count)]
        while len(parts) > 1:
            half = len(parts) // 2
            parts = [add2(parts[k], parts[k + half]) for k in range(half)] + parts[2 * half :]
        return parts[0]

    @pl.loop(0, ITERS)
    def _(k):
        value = vertex[k]
        for ia in range(2):
            at_node = []
            for ir in range(2):
                back = 64 + ER * ia + ir
                at_node.append([pltpu.roll(value, (shift - back) % 256, 1)[:, 0:LANES] for shift in (0, 64)])
            for g in range(2):
                for iz in range(2):
                    row_at = 4 + 2 * g + iz
                    pair = [
                        jnp.where(
                            low_half,
                            jnp.broadcast_to(v[0][row_at : row_at + 1], shape),
                            jnp.broadcast_to(v[1][row_at + 1 : row_at + 2], shape),
                        )
                        for v in at_node
                    ]
                    x1[block_at(2, g, iz, ia), :] = jnp.where(sub == 0, pair[0], jnp.where(sub == 1, pair[1], 0.0))
        prolong(x1, 2, 4, (lifted.at[k],), t3, t2, False)

    lifted[ITERS] = d3[...]

    @pl.loop(0, ITERS + 1)
    def _(k):
        element(lifted.at[k], images.at[k], 4, True)

    lifted_round = Round(*[images.at[k] for k in range(ITERS + 1)])
    lifted_round.pack()
    lifted_round.start(LATE_FIRST)

    wait_for(row_box, nr, row_recv)
    total = total_of(row_box, nr)
    for half in range(2):
        gz_box[0, pl.ds(half, 1), :] = total[half]

    @pl.loop(1, nz)
    def _(o):
        pltpu.make_async_remote_copy(
            src_ref=gz_box.at[0], dst_ref=gz_box.at[o], send_sem=gz_send, recv_sem=gz_recv,
            device_id=(lax.rem(gz + o, nz), row), device_id_type=mesh_ids,
        ).start()

    lifted_round.finish()
    wait_for(gz_box, nz, gz_recv)
    total = total_of(gz_box, nz)
    wait_for(row_box, nr, row_send)
    wait_for(gz_box, nz, gz_send)

    system = []
    for half in range(2):
        wide_row = jnp.broadcast_to(total[half], shape)
        part = jnp.zeros(shape, jnp.float32)
        for i in range(ITERS):
            part = jnp.where(sub == i, roll(wide_row, -8 * i), part)
        system.append(jnp.where(lane <= ITERS, part, 0.0))
    start = system[0]
    for p in range(ITERS):
        column = [jnp.broadcast_to(part[:, p : p + 1], shape) for part in system]
        line_p = [jnp.broadcast_to(part[p : p + 1, :], shape) for part in system]
        pivot = [jnp.broadcast_to(part[p : p + 1, :], shape) for part in column]
        least = TINY * jnp.broadcast_to(jnp.broadcast_to(start[p : p + 1, :], shape)[:, p : p + 1], shape)
        usable = pivot[0] > least
        inverse = inverse2((jnp.where(usable, pivot[0], 1.0), jnp.where(usable, pivot[1], 0.0)))
        scaled = mul2(line_p, tuple(jnp.where(usable, part, 0.0) for part in inverse))
        taken = mul2(column, scaled)
        rest = add2(system, (-taken[0], -taken[1]))
        system = [jnp.where(sub == p, scaled[half], rest[half]) for half in range(2)]

    factors = []
    for k in range(ITERS):
        factor = jnp.broadcast_to(system[0][k : k + 1, :], shape)[:, ITERS : ITERS + 1]
        factors.append(jnp.concatenate([jnp.broadcast_to(factor, shape)] * 8, axis=0))

    def correct(at):
        gain, image = x3[at, :], images[ITERS, at, :]
        for k in range(ITERS):
            gain = gain + factors[k] * lifted[k, at, :]
            image = image + factors[k] * images[k, at, :]
        x3[at, :] = gain
        r3[at, :] = r3[at, :] - image

    blocks(4, correct)
    smooth_first(inv3, r3, d3, 4)

    def keep_x3(at, value):
        x3[at, :] = value

    smooth_second(inv3, r3, d3, x3, o3, 4, keep_x3)

    prolong(x3, 4, 8, (d7, x7), t1, t2)

    def before_last(at):
        left = r7[at, :] - o7[at, :]
        r7[at, :] = left
        d7[at, :] = (1.0 / THETA) * (inv7[at, :] * left)

    def fix_before_last(place, value):
        at = block_at(8, *place)
        r7[at, :] = r7[at, :] - value
        d7[at, :] = d7[at, :] - (1.0 / THETA) * (inv7[at, :] * value)

    apply(d7, o7, 8, lambda: blocks(8, before_last), fix_before_last)

    def write(at, value):
        i = lax.div(at.start, 64)
        rows = pl.ds(pl.multiple_of(lax.rem(i, 8) * 64, 64), 64)
        out[rows, pl.ds(pl.multiple_of(lax.div(i, 8) * LANES, LANES), LANES)] = value

    smooth_second(inv7, r7, d7, x7, o7, 8, write)


def per_device(rhs_local, stretch):
    nz = lax.axis_size("gz")
    nr = lax.axis_size("row")
    nodes = (ORDER + 1) ** 3
    elems = EZ * EA * ER
    face_rows = sum(sum(c) * 4 for c in ROUNDS)
    diag_rows = sum(len(c) * 8 for c in ROUNDS)

    def field(rows):
        return pltpu.VMEM((rows, LANES), jnp.float32)

    out = pl.pallas_call(
        functools.partial(kernel, nz, nr),
        out_shape=jax.ShapeDtypeStruct((nodes, elems), jnp.float32),
        in_specs=[pl.BlockSpec(memory_space=pltpu.HBM)] * 2,
        out_specs=pl.BlockSpec(memory_space=pltpu.VMEM),
        scratch_shapes=[pltpu.VMEM((3, elems), jnp.float32), field(CONST.shape[0] * 8)]
        + [field(1024)] * 5
        + [field(512), field(256)]
        + [field(256)] * 5
        + [field(128)]
        + [field(64)] * 2
        + [field(48)]
        + [
            pltpu.VMEM((ITERS, 16, 256), jnp.float32),
            pltpu.VMEM((ITERS + 1, 256, LANES), jnp.float32),
            pltpu.VMEM((ITERS + 1, 256, LANES), jnp.float32),
            pltpu.VMEM((4, face_rows, LANES), jnp.float32),
            pltpu.VMEM((4, face_rows, LANES), jnp.float32),
            pltpu.VMEM((4, diag_rows, LANES), jnp.float32),
            pltpu.VMEM((4, diag_rows, LANES), jnp.float32),
            pltpu.VMEM((24, LANES), jnp.float32),
            pltpu.VMEM((8, 24, LANES), jnp.float32),
            pltpu.VMEM((8, LANES), jnp.float32),
            pltpu.VMEM((len(FAR_DIRS), 8, LANES), jnp.float32),
            pltpu.VMEM((nr, 2, LANES), jnp.float32),
            pltpu.VMEM((nz, 2, LANES), jnp.float32),
            pltpu.SemaphoreType.DMA((3,)),
            pltpu.SemaphoreType.DMA((len(ROUNDS), 8)),
            pltpu.SemaphoreType.DMA((len(ROUNDS), 8)),
            pltpu.SemaphoreType.DMA((8,)),
            pltpu.SemaphoreType.DMA((8,)),
            pltpu.SemaphoreType.DMA((len(FAR_DIRS),)),
            pltpu.SemaphoreType.DMA((len(FAR_DIRS),)),
            pltpu.SemaphoreType.DMA,
            pltpu.SemaphoreType.DMA,
            pltpu.SemaphoreType.DMA,
            pltpu.SemaphoreType.DMA,
        ],
        compiler_params=pltpu.CompilerParams(
            collective_id=0, has_side_effects=True, vmem_limit_bytes=32 * 1024 * 1024
        ),
    )(pltpu.with_memory_space_constraint(rhs_local.reshape(nodes, elems), pltpu.HBM), pltpu.with_memory_space_constraint(stretch, pltpu.HBM))
    return out.reshape(rhs_local.shape)


def solution(mesh):
    placed = (P(None, None, None, ("gz", "row")), P(None, ("gz", "row")))
    return jax.shard_map(
        per_device,
        mesh=mesh,
        in_specs=placed,
        out_specs=P(None, None, None, ("gz", "row")),
        check_vma=False,
    )
```

```python
import functools

import numpy as np

import jax
import jax.numpy as jnp
from jax import lax
from jax.experimental import pallas as pl
from jax.experimental.pallas import tpu as pltpu
from jax.sharding import PartitionSpec as P

ORDER = 7
MID = 3
ITERS = 5
EZ = 4
EA = 4
ER = 16
LANES = 128

LOW_BOUND = 0.4
HIGH_BOUND = 4.0
THETA = 0.5 * (HIGH_BOUND + LOW_BOUND)
DELTA = 0.5 * (HIGH_BOUND - LOW_BOUND)
RHO = DELTA / THETA
RHO2 = 1.0 / (2.0 * THETA / DELTA - RHO)

DIRS = ((0, 1), (0, -1), (1, 0), (-1, 0), (1, 1), (1, -1), (-1, 1), (-1, -1))
FAR_DIRS = tuple((z, a) for z in (2, -2, 1, -1, 0) for a in (2, -2, 1, -1, 0) if (z, a) != (0, 0))
ROUNDS = ((8, 8, 4), (8,), (4,), (4,), (4,) * 6, (4,), (8,), (8,))
SCALE = 16.0
TINY = 1e-13


def points_of(order):
    return -np.cos(np.pi * np.arange(order + 1) / order)


def tables_of(order):
    x = points_of(order)
    n = order + 1
    place = np.arange(n)
    running = np.ones(n)
    for j in range(1, order // 2 + 1):
        b = 1.0 if 2 * j == order else 2.0
        running = running - b * np.cos(2 * np.pi * j * place / order) / (4 * j * j - 1)
    weights = np.where((place == 0) | (place == order), 1.0, 2.0) / order * running
    gap = x[:, None] - x[None, :] + np.eye(n)
    bary = 1.0 / np.prod(gap, axis=1)
    deriv = bary[None, :] / bary[:, None] / gap * (1.0 - np.eye(n))
    deriv = deriv - np.diag(deriv.sum(axis=1))
    stiff = deriv.T @ (weights[:, None] * deriv)
    return weights, stiff / weights[:, None]


def interpolation(fine_order, coarse_order):
    x = points_of(fine_order)
    y = points_of(coarse_order)
    table = np.ones((fine_order + 1, coarse_order + 1))
    for j in range(coarse_order + 1):
        for k in range(coarse_order + 1):
            if k != j:
                table[:, j] *= (x - y[k]) / (y[j] - y[k])
    return table


WK = {n: tables_of(n - 1) for n in (8, 4, 2)}
UP = {(4, 8): interpolation(7, 3), (2, 4): interpolation(3, 1)}
DOWN = {(8, 4): UP[4, 8].T, (4, 2): UP[2, 4].T}
PAIRS = [(i, j) for i in range(ITERS) for j in range(i, ITERS)] + [(i, ITERS) for i in range(ITERS)]


def column_blocks(table):
    blocks = np.zeros((table.shape[1], 8))
    blocks[:, : table.shape[0]] = table.T
    return blocks


def constant_table():
    blocks, where = [], {}

    def put(name, rows):
        where[name] = sum(len(b) for b in blocks)
        blocks.append(rows)

    for n in (8, 4, 2):
        w, k = WK[n]
        put(("k", n), column_blocks(k))
        put(("w", n), column_blocks(np.outer(w, w)))
        put(("d", n), column_blocks(np.diag(k)[:, None]))
    for key, table in list(UP.items()) + list(DOWN.items()):
        put(("j",) + key, column_blocks(table))
    return np.concatenate(blocks).astype(np.float32), where


CONST, WHERE = constant_table()


def line(table, values, pairs=None):
    rows, cols = table.shape
    half = cols // 2
    even = [values[k] + values[cols - 1 - k] for k in range(half)]
    odd = [values[k] - values[cols - 1 - k] for k in range(half)]
    out = [None] * rows
    for i in range(rows // 2) if pairs is None else pairs:
        e = o = None
        for k in range(half):
            te = float(np.float32(0.5 * (table[i, k] + table[i, cols - 1 - k])))
            to = float(np.float32(0.5 * (table[i, k] - table[i, cols - 1 - k])))
            e = te * even[k] if e is None else e + te * even[k]
            o = to * odd[k] if o is None else o + to * odd[k]
        out[i] = e + o
        out[rows - 1 - i] = e - o
    return out


def rows8(start):
    if isinstance(start, int):
        return pl.ds(start, 8)
    return pl.ds(pl.multiple_of(start, 8), 8)


def roll(value, shift):
    shift = shift % LANES
    return value if shift == 0 else pltpu.roll(value, shift, 1)


def loop(count, body, unroll_all):
    if unroll_all:
        for i in range(count):
            body(i)
    else:
        pl.loop(0, count, unroll=2)(body)


def split(i, size):
    if isinstance(i, int):
        return i // size, i % size
    return lax.div(i, size), lax.rem(i, size)


def two_sum(a, b):
    s = a + b
    t = s - a
    return s, (a - (s - t)) + (b - t)


def halves(a):
    t = 4097.0 * a
    hi = t - (t - a)
    return a, hi, a - hi


def two_prod(x, y):
    a, ah, al = x
    b, bh, bl = y
    p = a * b
    return p, ((ah * bh - p) + ah * bl + al * bh) + al * bl


def add2(x, y):
    s, e = two_sum(x[0], y[0])
    return two_sum(s, e + (x[1] + y[1]))


def mul2(x, y):
    p, e = two_prod(halves(x[0]), halves(y[0]))
    return two_sum(p, e + (x[0] * y[1] + x[1] * y[0]))


def inverse2(x):
    r = 1.0 / x[0]
    p, e = two_prod(halves(x[0]), halves(r))
    return two_sum(r, r * (((1.0 - p) - e) - x[1] * r))


def kernel(
    nz, nr, rhs, stretch_in, out, stretch, tab,
    x7, d7, r7, inv7, o7, t1, t2, x3, d3, r3, inv3, o3, t3, x1, r1, coef,
    vertex, lifted, images, send, recv, send_diag, recv_diag, send_block, recv_block, send_point, recv_point, row_box, gz_box,
    load_sem, send_sem, recv_sem, block_send, block_recv, point_send, point_recv, row_send, row_recv, gz_send, gz_recv,
):
    gz = lax.axis_index("gz")
    row = lax.axis_index("row")
    mesh_ids = pl.DeviceIdType.MESH
    shape = (8, LANES)
    lane = lax.broadcasted_iota(jnp.int32, shape, 1)
    sub = lax.broadcasted_iota(jnp.int32, shape, 0)
    in_r = lane % ER
    in_a = (lane // ER) % EA
    low_half = lane < 64

    def as_float(cond):
        return jnp.where(cond, 1.0, 0.0).astype(jnp.float32)

    def at_device(dz, da):
        return (lax.rem(gz + (dz + nz), nz), lax.rem(row + (da + nr), nr))

    barrier = pltpu.get_barrier_semaphore()

    @pl.loop(1, nr)
    def _(o):
        pl.semaphore_signal(barrier, inc=1, device_id=(gz, lax.rem(row + o, nr)), device_id_type=mesh_ids)

    @pl.loop(1, nz)
    def _(o):
        pl.semaphore_signal(barrier, inc=1, device_id=(lax.rem(gz + o, nz), row), device_id_type=mesh_ids)

    askew = [d for d in FAR_DIRS if d[0] != 0 and d[1] != 0]
    for dz, da in askew:
        pl.semaphore_signal(barrier, inc=1, device_id=at_device(dz, da), device_id_type=mesh_ids)

    loads = [pltpu.make_async_copy(stretch_in, stretch, load_sem.at[2])]
    for g in range(2):
        loads.append(
            pltpu.make_async_copy(rhs.at[:, pl.ds(g * LANES, LANES)], r7.at[pl.ds(g * 512, 512)], load_sem.at[g])
        )
    for load in loads:
        load.start()

    for b, values in enumerate(CONST):
        block = jnp.full(shape, float(values[0]), jnp.float32)
        for i in range(1, 8):
            block = jnp.where(sub == i, float(values[i]), block)
        tab[rows8(b * 8), :] = block
    loads[0].wait()

    def row_targets():
        if nr != 32:
            return [(o, lax.rem(row + o, nr)) for o in range(1, nr)]
        y, x, core = lax.div(row, 8), lax.rem(lax.div(row, 2), 4), lax.rem(row, 2)
        ys, xs, cores = [lax.rem(y + k, 4) * 8 for k in range(4)], [lax.rem(x + k, 4) * 2 for k in range(4)], [core, 1 - core]
        order = sorted(range(1, 32), key=lambda o: -(min(o // 8, 4 - o // 8) + min(o // 2 % 4, 4 - o // 2 % 4)))
        return [(o, ys[o // 8] + xs[o // 2 % 4] + cores[o % 2]) for o in order]

    def const(name, j=0):
        return tab[rows8((WHERE[name] + j) * 8), :]

    def live(n):
        wall = ((sub == 0) & (in_r == 0)) | ((sub == n - 1) & (in_r == ER - 1))
        return jnp.logical_not(wall) & (sub < n)

    for g in range(2):
        for k in range(3):
            coef[rows8((g * 3 + k) * 8), :] = jnp.broadcast_to(
                stretch[pl.ds(k, 1), pl.ds(g * LANES, LANES)], shape
            )

    def coeff(g, k):
        return coef[rows8((g * 3 + k) * 8), :]

    def add_r(field, n, base, stride=8, inner=False):
        lo_at = pl.ds(base, 8, stride=stride)
        hi_at = pl.ds(base + n - 1, 8, stride=stride)
        lo, hi = field[lo_at, :], field[hi_at, :]
        keep = (sub % n > 0) & (sub % n < n - 1) if inner else sub >= 0
        field[lo_at, :] = lo + jnp.where(keep & (in_r > 0), roll(hi, 1), 0.0)
        field[hi_at, :] = hi + jnp.where(keep & (in_r < ER - 1), roll(lo, -1), 0.0)

    def with_r(value, n):
        from_below = roll(pltpu.roll(value, 9 - n, 0), 1)
        from_above = roll(pltpu.roll(value, n - 1, 0), -1)
        value = value + jnp.where((sub == 0) & (in_r > 0), from_below, 0.0)
        return value + jnp.where((sub == n - 1) & (in_r < ER - 1), from_above, 0.0)

    def add_a(field, n, base):
        lo_at, hi_at = rows8(base), rows8(base + (n - 1) * 8)
        lo, hi = field[lo_at, :], field[hi_at, :]
        field[lo_at, :] = lo + jnp.where(in_a > 0, roll(hi, ER), 0.0)
        field[hi_at, :] = hi + jnp.where(in_a < EA - 1, roll(lo, -ER), 0.0)

    def block_at(n, g, iz, ia):
        return rows8(((g * n + iz) * n + ia) * 8)

    def add_z(field, n, which=None):
        for ia in range(n) if which is None else which:
            at = [block_at(n, g, iz, ia) for g, iz in ((0, 0), (1, 0), (0, n - 1), (1, n - 1))]
            lo0, lo1, hi0, hi1 = [field[a, :] for a in at]
            up0, up1, dn0, dn1 = [roll(v, 64) for v in (hi0, hi1, lo0, lo1)]
            field[at[0], :] = lo0 + jnp.where(low_half, 0.0, up0)
            field[at[1], :] = lo1 + jnp.where(low_half, up0, up1)
            field[at[2], :] = hi0 + jnp.where(low_half, dn0, dn1)
            field[at[3], :] = hi1 + jnp.where(low_half, dn1, 0.0)

    def device_sum(field, n):
        loop(2 * n * n // 8, lambda i: add_r(field, n, i * 64), n < 8)
        loop(2 * n, lambda i: add_a(field, n, i * n * 8), n < 8)
        add_z(field, n)

    def shared(iz, ia, n):
        along = jnp.where((sub == 0) | (sub == n - 1), 0.5, 1.0)
        if ia in (0, n - 1):
            along = 0.5 * along
        if isinstance(iz, int):
            return 0.5 * along if iz in (0, n - 1) else along
        return jnp.where((iz == 0) | (iz == n - 1), 0.5, 1.0) * along

    def along_z(field, image, n, g, ia):
        base = g * (n * n * 8) + ia * 8
        got = line(WK[n][1], [field[rows8(base + iz * n * 8), :] for iz in range(n)])
        c0 = coef[rows8(g * 24), :]
        for iz in range(n):
            image[rows8(base + iz * n * 8), :] = c0 * got[iz]

    def rest_values(field, image, n, g, iz, pairs, along=None):
        w, k = WK[n]
        base = (g * n + iz) * (n * 8)
        got = line(k, [field[rows8(base + ia * 8), :] for ia in range(n)], pairs)
        c1 = coef[rows8(g * 24 + 8), :]
        c2 = coef[rows8(g * 24 + 16), :]
        scale = tab[rows8((WHERE["w", n] + iz) * 8), :]
        values = []
        for ia in sorted(list(pairs) + [n - 1 - p for p in pairs]):
            at = base + ia * 8
            part = None
            for j in range(n):
                term = const(("k", n), j) * field[pl.ds(at + j, 1), :]
                part = term if part is None else part + term
            first = image[rows8(at), :] if along is None else along[ia]
            values.append((ia, (float(w[ia]) * scale) * (first + c1 * got[ia] + c2 * part)))
        return values

    def element(field, image, n, sums, left=None):
        loop(2 * n, lambda i: along_z(field, image, n, *split(i, n)), n < 8)

        def along_rest(i):
            g, iz = split(i, n)
            for ia, value in rest_values(field, image, n, g, iz, range(n // 2)):
                at = rows8(i * (n * 8) + ia * 8)
                image[at, :] = value if left is None else shared(iz, ia, n) * left[at, :] - value

        loop(2 * n, along_rest, n < 8)
        if sums:
            device_sum(image, n)

    def diagonal(field, n):
        w, k = WK[n]

        def body(i):
            g, iz = split(i, n)
            c0 = coef[rows8(g * 24), :]
            c1 = coef[rows8(g * 24 + 8), :]
            c2 = coef[rows8(g * 24 + 16), :]
            scale = tab[rows8((WHERE["w", n] + iz) * 8), :]
            kz = jnp.broadcast_to(tab[pl.ds(WHERE["d", n] * 8 + iz, 1), :], shape)
            fixed = c0 * kz + c2 * const(("d", n))
            for ia in range(n):
                field[rows8(i * (n * 8) + ia * 8), :] = (float(w[ia]) * scale) * (fixed + float(k[ia, ia]) * c1)

        loop(2 * n, body, n < 8)

    quarter = in_a

    def pack_a(field, n, at):
        half = n // 2
        for m in range(half):
            rows = rows8(at + m * 8)
            to_up = to_down = None
            for k in range(4):
                g, iz = divmod(m + k * half, n)
                up = roll(field[block_at(n, g, iz, n - 1), :], 80 + 16 * k)
                down = roll(field[block_at(n, g, iz, 0), :], 16 * k)
                to_up = up if k == 0 else jnp.where(quarter == k, up, to_up)
                to_down = down if k == 0 else jnp.where(quarter == k, down, to_down)
            send[0, rows, :] = to_up
            send[1, rows, :] = to_down

    def pack_z(field, n, at):
        half = n // 2
        for m in range(half):
            rows = rows8(at + m * 8)
            hi = [field[block_at(n, 1, n - 1, ia), :] for ia in (m, m + half)]
            lo = [field[block_at(n, 0, 0, ia), :] for ia in (m, m + half)]
            send[2, rows, :] = jnp.where(low_half, roll(hi[0], 64), hi[1])
            send[3, rows, :] = jnp.where(low_half, lo[0], roll(lo[1], 64))

    def pack(field, n, at, at_diag):
        pack_a(field, n, at)
        pack_z(field, n, at)
        for d, (g, iz, ia) in enumerate(corners(n)):
            send_diag[d, rows8(at_diag), :] = field[block_at(n, g, iz, ia), :]

    def corners(n):
        return ((1, n - 1, n - 1), (1, n - 1, 0), (0, 0, n - 1), (0, 0, 0))

    def unpack(field, n, at, at_diag, fix=None):
        half = n // 2

        def add(place, keep, value):
            value = jnp.where(keep, value, 0.0)
            if fix is not None:
                fix(place, value)
            else:
                where = block_at(n, *place)
                field[where, :] = field[where, :] + value

        for m in range(half):
            rows = rows8(at + m * 8)
            got = [recv[d, rows, :] for d in range(4)]
            for k in range(4):
                g, iz = divmod(m + k * half, n)
                add((g, iz, 0), in_a == 0, roll(got[0], -16 * k))
                add((g, iz, n - 1), in_a == EA - 1, roll(got[1], 48 - 16 * k))
        for m in range(half):
            rows = rows8(at + m * 8)
            got = [recv[d, rows, :] for d in range(4)]
            for k in range(2):
                add((0, 0, m + k * half), low_half, roll(got[2], 64 * k))
                add((1, n - 1, m + k * half), jnp.logical_not(low_half), roll(got[3], 64 - 64 * k))
        rows = rows8(at_diag)
        add((0, 0, 0), lane < 16, roll(recv_diag[0, rows, :], 16))
        add((0, 0, n - 1), (lane >= 48) & (lane < 64), roll(recv_diag[1, rows, :], -16))
        add((1, n - 1, 0), (lane >= 64) & (lane < 80), roll(recv_diag[2, rows, :], 16))
        add((1, n - 1, n - 1), lane >= 112, roll(recv_diag[3, rows, :], -16))

    offsets, diag_offsets = [0], [0]
    for counts in ROUNDS:
        offsets.append(offsets[-1] + sum(counts) * 4)
        diag_offsets.append(diag_offsets[-1] + len(counts) * 8)
    state = {"next": 0}

    class Round:
        def __init__(self, *fields):
            self.turn = state["next"]
            state["next"] += 1
            self.counts = ROUNDS[self.turn]
            self.at, self.at_diag = offsets[self.turn], diag_offsets[self.turn]
            self.fields = fields
            self.copies = []

        def places(self):
            at, at_diag = self.at, self.at_diag
            for field, n in zip(self.fields, self.counts):
                yield field, n, at, at_diag
                at += n * 4
                at_diag += 8

        def pack(self):
            for place in self.places():
                pack(*place)

        def start(self, which):
            for d in which:
                dz, da = DIRS[d]
                if d < 4:
                    rows = pl.ds(self.at, sum(self.counts) * 4)
                    src, dst = send.at[d, rows], recv.at[d, rows]
                else:
                    rows = pl.ds(self.at_diag, len(self.counts) * 8)
                    src, dst = send_diag.at[d - 4, rows], recv_diag.at[d - 4, rows]
                copy = pltpu.make_async_remote_copy(
                    src_ref=src, dst_ref=dst, send_sem=send_sem.at[self.turn, d], recv_sem=recv_sem.at[self.turn, d],
                    device_id=at_device(dz, da), device_id_type=mesh_ids,
                )
                copy.start()
                self.copies.append(copy)

        def finish(self, fix=None):
            for copy in self.copies:
                copy.wait()
            for place in self.places():
                unpack(*place, fix)

    LATE_FIRST = (4, 5, 6, 7, 0, 1, 2, 3)

    def send_all(dirs, src, dst, sends, recvs):
        copies = []
        for d, (dz, da) in enumerate(dirs):
            copy = pltpu.make_async_remote_copy(
                src_ref=src, dst_ref=dst.at[d], send_sem=sends.at[d], recv_sem=recvs.at[d],
                device_id=at_device(dz, da), device_id_type=mesh_ids,
            )
            copy.start()
            copies.append(copy)
        return copies

    def wide(at):
        def block(dz, da):
            if (dz, da) == (0, 0):
                return send_block[rows8(at), :]
            return recv_block[DIRS.index((-dz, -da)), rows8(at), :]

        def left_part(dz):
            return jnp.where(low_half, block(dz, -1), roll(block(dz, 0), 64))

        def below(low, own):
            return jnp.where(sub < 4, low, pltpu.roll(own, 4, 0))

        top = jnp.concatenate([below(left_part(-1), left_part(0)), below(block(-1, 1), block(0, 1))], axis=1)
        bottom = jnp.concatenate([left_part(1), block(1, 1)], axis=1)
        return jnp.concatenate([top, bottom], axis=0)

    def assemble(field, n):
        turn = Round(field)
        for d, place in enumerate(corners(n)):
            send_diag[d, rows8(turn.at_diag), :] = with_r(field[block_at(n, *place), :], n)
        turn.start((4, 5, 6, 7))
        device_sum(field, n)
        pack_a(field, n, turn.at)
        turn.start((0, 1))
        pack_z(field, n, turn.at)
        turn.start((2, 3))
        turn.finish()

    def apply(field, image, n, during, fix):
        turn = Round(image)
        ends = (0, n - 1)
        for d, (g, iz) in enumerate(((1, n - 1), (0, 0))):
            along = {}
            for ia in ends:
                got = line(WK[n][1], [field[block_at(n, g, j, ia), :] for j in range(n)], (0,))
                along[ia] = coef[rows8(g * 24), :] * got[iz]
            (_, first), (_, last) = rest_values(field, image, n, g, iz, (0,), along)
            send_diag[2 * d, rows8(turn.at_diag), :] = with_r(last, n)
            send_diag[2 * d + 1, rows8(turn.at_diag), :] = with_r(first, n)
        turn.start((4, 5, 6, 7))
        for g in range(2):
            for ia in ends:
                along_z(field, image, n, g, ia)

        def outer(i):
            g, iz = split(i, n)
            for ia, value in rest_values(field, image, n, g, iz, (0,)):
                image[rows8(i * (n * 8) + ia * 8), :] = value

        loop(2 * n, outer, n < 8)
        for q in range(2 * n // 8):
            for ia in ends:
                add_r(image, n, q * (n * 64) + ia * 8, n * 8)
        for i in range(2 * n):
            add_a(image, n, i * n * 8)
        add_z(image, n, ends)
        pack_a(image, n, turn.at)
        turn.start((0, 1))

        def inner_z(i):
            g, ia = split(i, n - 2)
            along_z(field, image, n, g, ia + 1)

        loop(2 * (n - 2), inner_z, n < 8)

        def inner(q):
            for part in range(8 // n):
                i = q * (8 // n) + part
                g, iz = split(i, n)
                for ia, value in rest_values(field, image, n, g, iz, range(1, n // 2)):
                    image[rows8(i * (n * 8) + ia * 8), :] = value
            add_r(image, n, q * 64, 8, True)

        groups = 2 * n * n // 8
        inner(0)
        inner(groups - 1)
        pack_z(image, n, turn.at)
        turn.start((2, 3))
        loop(groups - 2, lambda q: inner(q + 1), n < 8)
        add_z(image, n, range(1, n - 1))
        during()
        turn.finish(fix)

    def blocks(n, body):
        def step(i):
            if isinstance(i, int):
                body(pl.ds(i * 64, 64))
            else:
                body(pl.ds(pl.multiple_of(i * 64, 64), 64))

        loop(2 * n * n // 8, step, n < 8)

    def masked(n, value):
        keep = jnp.concatenate([as_float(live(n))] * 8, axis=0)
        return keep * value

    for load in loads[1:]:
        load.wait()
    device_sum(r7, 8)
    diagonal(inv7, 8)
    device_sum(inv7, 8)
    diagonal(inv3, 4)
    device_sum(inv3, 4)
    for k in range(3):
        rows = jnp.where(sub < 2, coeff(0, k), coeff(1, k))
        send_block[rows8(k * 8), :] = jnp.where(sub % 2 == 0, rows, roll(rows, 64))
    first_round = Round(r7, inv7, inv3)
    first_round.pack()
    pl.semaphore_wait(barrier, (nr - 1) + (nz - 1) + len(askew))
    first_round.start(LATE_FIRST)
    stretch_copies = send_all(DIRS, send_block, recv_block, block_send, block_recv)
    first_round.finish()

    def invert(inv, n):
        keep = jnp.concatenate([live(n)] * 8, axis=0)

        def body(at):
            inv[at, :] = jnp.where(keep, 1.0 / jnp.where(keep, inv[at, :], 1.0), 0.0)

        blocks(n, body)

    invert(inv7, 8)
    invert(inv3, 4)

    def smooth_first(inv, r, d, n):
        def body(at):
            d[at, :] = (1.0 / THETA) * (inv[at, :] * r[at, :])

        blocks(n, body)

    def smooth_second(inv, r, d, x, image, n, result=None):
        def body(at):
            step = d[at, :]
            left = r[at, :] - image[at, :]
            second = (RHO2 * RHO) * step + (2.0 * RHO2 / DELTA) * (inv[at, :] * left)
            if result is None:
                x[at, :] = step + second
                d[at, :] = second
                r[at, :] = left
            else:
                result(at, x[at, :] + (step + second))

        def fix(place, value):
            at = block_at(n, *place)
            change = (2.0 * RHO2 / DELTA) * (inv[at, :] * value)
            if result is None:
                r[at, :] = r[at, :] - value
                d[at, :] = d[at, :] - change
                x[at, :] = x[at, :] - change
            elif n == 8:
                g, iz, ia = place
                spot = rows8((iz * 8 + ia) * 8), pl.ds(g * LANES, LANES)
                out[spot] = out[spot] - change
            else:
                x[at, :] = x[at, :] - change

        apply(d, image, n, lambda: blocks(n, body), fix)

    def r_line(name, field, at, count):
        part = None
        for j in range(count):
            term = const(name, j) * field[pl.ds(at + j, 1), :]
            part = term if part is None else part + term
        return part

    def restrict(fine, nf, nc, coarse, tz, ta):
        table = DOWN[nf, nc]

        def along_z(i):
            g, ia = split(i, nf)
            got = line(table, [fine[rows8((g * nf + iz) * (nf * 8) + ia * 8), :] for iz in range(nf)])
            for c in range(nc):
                tz[rows8((g * nc + c) * (nf * 8) + ia * 8), :] = got[c]

        def along_a(i):
            got = line(table, [tz[rows8(i * (nf * 8) + ia * 8), :] for ia in range(nf)])
            for c in range(nc):
                ta[rows8(i * (nc * 8) + c * 8), :] = got[c]
            for c in range(nc):
                at = i * (nc * 8) + c * 8
                coarse[rows8(at), :] = r_line(("j", nf, nc), ta, at, nf)

        loop(2 * nf, along_z, nf < 8)
        loop(2 * nc, along_a, nf < 8)

    def prolong(coarse, nc, nf, fields, tz, ta, add=True):
        table = UP[nc, nf]

        def along_a(i):
            for c in range(nc):
                at = i * (nc * 8) + c * 8
                ta[rows8(at), :] = r_line(("j", nc, nf), coarse, at, nc)
            got = line(table, [ta[rows8(i * (nc * 8) + c * 8), :] for c in range(nc)])
            for ia in range(nf):
                tz[rows8(i * (nf * 8) + ia * 8), :] = got[ia]

        def along_z(i):
            g, ia = split(i, nf)
            got = line(table, [tz[rows8((g * nc + c) * (nf * 8) + ia * 8), :] for c in range(nc)])
            for iz in range(nf):
                at = rows8((g * nf + iz) * (nf * 8) + ia * 8)
                for field in fields:
                    field[at, :] = field[at, :] + got[iz] if add else got[iz]

        loop(2 * nc, along_a, nf < 8)
        loop(2 * nf, along_z, nf < 8)

    smooth_first(inv7, r7, d7, 8)
    smooth_second(inv7, r7, d7, x7, o7, 8)
    element(d7, o7, 8, False, left=r7)

    restrict(o7, 8, 4, r3, t1, t2)
    assemble(r3, 4)
    smooth_first(inv3, r3, d3, 4)
    smooth_second(inv3, r3, d3, x3, o3, 4)
    element(d3, o3, 4, False, left=r3)

    restrict(o3, 4, 2, r1, t3, t2)
    per_z = []
    for iz in range(2):
        per_a = []
        for ia in range(2):
            at = [((g * 2 + iz) * 2 + ia) * 8 for g in range(2)]
            per_r = []
            for ir in range(2):
                rows = jnp.where(sub < 2, r1[pl.ds(at[0] + ir, 1), :], r1[pl.ds(at[1] + ir, 1), :])
                rows = jnp.where(sub % 2 == 0, rows, roll(rows, 64))
                per_r.append(jnp.where((sub < 4) & low_half, rows, 0.0))
            per_a.append(per_r[0] + roll(per_r[1], 1))
        per_z.append(per_a[0] + roll(per_a[1], ER))
    send_point[...] = per_z[0] + pltpu.roll(per_z[1], 1, 0)
    point_copies = send_all(FAR_DIRS, send_point, recv_point, point_send, point_recv)

    for copy in stretch_copies:
        copy.wait()
    lane_wide = lax.broadcasted_iota(jnp.int32, (16, 256), 1)
    inside = lane_wide % ER > 0

    def step(value, axis, amount):
        if axis == 0:
            return pltpu.roll(value, amount % 16, 0)
        return pltpu.roll(value, (amount * (ER if axis == 1 else 1)) % 256, 1)

    edges = []
    for axis in range(3):
        total = wide(axis * 8)
        for other in range(3):
            if other != axis:
                total = total + step(total, other, 1)
        edges.append(0.5 * total)

    def differences(value):
        return [value - step(value, axis, -1) for axis in range(3)]

    def vertex_image(slopes):
        total = None
        for axis in range(3):
            flux = edges[axis] * slopes[axis]
            flux = flux - step(flux, axis, 1)
            total = flux if total is None else total + flux
        return jnp.where(inside, (1.0 / SCALE) * total, 0.0)

    def summed_points():
        def from_device(dz, da):
            if (dz, da) == (0, 0):
                return send_point[...]
            return recv_point[FAR_DIRS.index((-dz, -da))]

        left, right = [], []
        for dz in (-2, -1, 0, 1, 2):
            far_left, near_left, mine, near_right, far_right = [from_device(dz, da) for da in (-2, -1, 0, 1, 2)]
            turned = roll(mine, 64)
            left.append(near_left + jnp.where(low_half, jnp.where(lane < ER, roll(far_left, 64), 0.0), turned))
            far_right = jnp.where((lane >= 64) & (lane < 64 + ER), roll(far_right, 64), 0.0)
            right.append(near_right + jnp.where(lane < ER, turned, far_right))
        halves_of = []
        for far_low, near_low, mine, near_high, far_high in (left, right):
            turned, far_low, far_high = [pltpu.roll(v, 4, 0) for v in (mine, far_low, far_high)]
            top = near_low + jnp.where(sub >= 4, turned, jnp.where(sub == 0, far_low, 0.0))
            bottom = near_high + jnp.where(sub == 0, turned, jnp.where(sub == 4, far_high, 0.0))
            halves_of.append(jnp.concatenate([top, bottom], axis=0))
        return jnp.where(inside, jnp.concatenate(halves_of, axis=1), 0.0)

    for copy in point_copies:
        copy.wait()
    basis = [summed_points()]
    slopes = [differences(basis[0])]
    for k in range(1, ITERS):
        basis.append(vertex_image(slopes[-1]))
        slopes.append(differences(basis[-1]))
    for k in range(ITERS):
        vertex[k] = basis[k]

    own = (sub >= 4) & jnp.logical_not(low_half)
    roots = [jnp.where(own, jnp.sqrt(edge[0:8, 0:LANES]), 0.0) for edge in edges]
    flows = [[halves(roots[axis] * slope[axis][0:8, 0:LANES]) for axis in range(3)] for slope in slopes]
    points = [halves(jnp.where(own, value[0:8, 0:LANES], 0.0)) for value in basis]

    tiles = [None] * 6
    for e, (i, j) in enumerate(PAIRS):
        if j < ITERS:
            total = two_prod(flows[i][0], flows[j][0])
            for axis in (1, 2):
                total = add2(total, two_prod(flows[i][axis], flows[j][axis]))
        else:
            total = two_prod(points[i], points[0])
        for amount in (2, 1):
            total = add2(total, tuple(pltpu.roll(part, amount, 0) for part in total))
        for half in range(2):
            row_of = jnp.broadcast_to(total[half][7:8, :], shape)
            slot = 2 * (e // 8) + half
            tiles[slot] = row_of if e % 8 == 0 else jnp.where(sub == e % 8, row_of, tiles[slot])
    sent = [0.0, 0.0]
    for t in range(3):
        total = (tiles[2 * t], tiles[2 * t + 1])
        for amount in (64, 32, 16, 8, 4, 2, 1):
            total = add2(total, tuple(roll(part, amount) for part in total))
        pick = sub < 0
        for e in range(8 * t, min(8 * t + 8, len(PAIRS))):
            i, j = PAIRS[e]
            spot = lane == 8 * i + j
            if j < ITERS:
                spot = spot | (lane == 8 * j + i)
            pick = pick | ((sub == e % 8) & spot)
        for half in range(2):
            sent[half] = sent[half] + jnp.sum(jnp.where(pick, total[half], 0.0), axis=0, keepdims=True)
    for half in range(2):
        row_box[0, pl.ds(half, 1), :] = sent[half]

    for o, target in row_targets():
        pltpu.make_async_remote_copy(
            src_ref=row_box.at[0], dst_ref=row_box.at[o], send_sem=row_send, recv_sem=row_recv,
            device_id=(gz, target), device_id_type=mesh_ids,
        ).start()

    def wait_for(box, count, sem):
        rest = box.at[pl.ds(1, count - 1)]
        pltpu.make_async_copy(rest, rest, sem).wait()

    def total_of(box, count):
        parts = [(box[o, pl.ds(0, 1), :], box[o, pl.ds(1, 1), :]) for o in range(count)]
        while len(parts) > 1:
            half = len(parts) // 2
            parts = [add2(parts[k], parts[k + half]) for k in range(half)] + parts[2 * half :]
        return parts[0]

    @pl.loop(0, ITERS)
    def _(k):
        value = vertex[k]
        for ia in range(2):
            at_node = []
            for ir in range(2):
                back = 64 + ER * ia + ir
                at_node.append([pltpu.roll(value, (shift - back) % 256, 1)[:, 0:LANES] for shift in (0, 64)])
            for g in range(2):
                for iz in range(2):
                    row_at = 4 + 2 * g + iz
                    pair = [
                        jnp.where(
                            low_half,
                            jnp.broadcast_to(v[0][row_at : row_at + 1], shape),
                            jnp.broadcast_to(v[1][row_at + 1 : row_at + 2], shape),
                        )
                        for v in at_node
                    ]
                    x1[block_at(2, g, iz, ia), :] = jnp.where(sub == 0, pair[0], jnp.where(sub == 1, pair[1], 0.0))
        prolong(x1, 2, 4, (lifted.at[k],), t3, t2, False)

    lifted[ITERS] = d3[...]

    @pl.loop(0, ITERS + 1)
    def _(k):
        element(lifted.at[k], images.at[k], 4, True)

    lifted_round = Round(*[images.at[k] for k in range(ITERS + 1)])
    lifted_round.pack()
    lifted_round.start(LATE_FIRST)

    wait_for(row_box, nr, row_recv)
    total = total_of(row_box, nr)
    for half in range(2):
        gz_box[0, pl.ds(half, 1), :] = total[half]

    @pl.loop(1, nz)
    def _(o):
        pltpu.make_async_remote_copy(
            src_ref=gz_box.at[0], dst_ref=gz_box.at[o], send_sem=gz_send, recv_sem=gz_recv,
            device_id=(lax.rem(gz + o, nz), row), device_id_type=mesh_ids,
        ).start()

    lifted_round.finish()
    wait_for(gz_box, nz, gz_recv)
    total = total_of(gz_box, nz)
    wait_for(row_box, nr, row_send)
    wait_for(gz_box, nz, gz_send)

    system = []
    for half in range(2):
        wide_row = jnp.broadcast_to(total[half], shape)
        part = jnp.zeros(shape, jnp.float32)
        for i in range(ITERS):
            part = jnp.where(sub == i, roll(wide_row, -8 * i), part)
        system.append(jnp.where(lane <= ITERS, part, 0.0))
    start = system[0]
    for p in range(ITERS):
        column = [jnp.broadcast_to(part[:, p : p + 1], shape) for part in system]
        line_p = [jnp.broadcast_to(part[p : p + 1, :], shape) for part in system]
        pivot = [jnp.broadcast_to(part[p : p + 1, :], shape) for part in column]
        least = TINY * jnp.broadcast_to(jnp.broadcast_to(start[p : p + 1, :], shape)[:, p : p + 1], shape)
        usable = pivot[0] > least
        inverse = inverse2((jnp.where(usable, pivot[0], 1.0), jnp.where(usable, pivot[1], 0.0)))
        scaled = mul2(line_p, tuple(jnp.where(usable, part, 0.0) for part in inverse))
        taken = mul2(column, scaled)
        rest = add2(system, (-taken[0], -taken[1]))
        system = [jnp.where(sub == p, scaled[half], rest[half]) for half in range(2)]

    factors = []
    for k in range(ITERS):
        factor = jnp.broadcast_to(system[0][k : k + 1, :], shape)[:, ITERS : ITERS + 1]
        factors.append(jnp.concatenate([jnp.broadcast_to(factor, shape)] * 8, axis=0))

    def correct(at):
        gain, image = x3[at, :], images[ITERS, at, :]
        for k in range(ITERS):
            gain = gain + factors[k] * lifted[k, at, :]
            image = image + factors[k] * images[k, at, :]
        x3[at, :] = gain
        r3[at, :] = r3[at, :] - image

    blocks(4, correct)
    smooth_first(inv3, r3, d3, 4)

    def keep_x3(at, value):
        x3[at, :] = value

    smooth_second(inv3, r3, d3, x3, o3, 4, keep_x3)

    prolong(x3, 4, 8, (d7, x7), t1, t2)

    def before_last(at):
        left = r7[at, :] - o7[at, :]
        r7[at, :] = left
        d7[at, :] = (1.0 / THETA) * (inv7[at, :] * left)

    def fix_before_last(place, value):
        at = block_at(8, *place)
        r7[at, :] = r7[at, :] - value
        d7[at, :] = d7[at, :] - (1.0 / THETA) * (inv7[at, :] * value)

    apply(d7, o7, 8, lambda: blocks(8, before_last), fix_before_last)

    def write(at, value):
        i = lax.div(at.start, 64)
        rows = pl.ds(pl.multiple_of(lax.rem(i, 8) * 64, 64), 64)
        out[rows, pl.ds(pl.multiple_of(lax.div(i, 8) * LANES, LANES), LANES)] = value

    smooth_second(inv7, r7, d7, x7, o7, 8, write)


def per_device(rhs_local, stretch):
    nz = lax.axis_size("gz")
    nr = lax.axis_size("row")
    nodes = (ORDER + 1) ** 3
    elems = EZ * EA * ER
    face_rows = sum(sum(c) * 4 for c in ROUNDS)
    diag_rows = sum(len(c) * 8 for c in ROUNDS)

    def field(rows):
        return pltpu.VMEM((rows, LANES), jnp.float32)

    out = pl.pallas_call(
        functools.partial(kernel, nz, nr),
        out_shape=jax.ShapeDtypeStruct((nodes, elems), jnp.float32),
        in_specs=[pl.BlockSpec(memory_space=pltpu.HBM)] * 2,
        out_specs=pl.BlockSpec(memory_space=pltpu.VMEM),
        scratch_shapes=[pltpu.VMEM((3, elems), jnp.float32), field(CONST.shape[0] * 8)]
        + [field(1024)] * 5
        + [field(512), field(256)]
        + [field(256)] * 5
        + [field(128)]
        + [field(64)] * 2
        + [field(48)]
        + [
            pltpu.VMEM((ITERS, 16, 256), jnp.float32),
            pltpu.VMEM((ITERS + 1, 256, LANES), jnp.float32),
            pltpu.VMEM((ITERS + 1, 256, LANES), jnp.float32),
            pltpu.VMEM((4, face_rows, LANES), jnp.float32),
            pltpu.VMEM((4, face_rows, LANES), jnp.float32),
            pltpu.VMEM((4, diag_rows, LANES), jnp.float32),
            pltpu.VMEM((4, diag_rows, LANES), jnp.float32),
            pltpu.VMEM((24, LANES), jnp.float32),
            pltpu.VMEM((8, 24, LANES), jnp.float32),
            pltpu.VMEM((8, LANES), jnp.float32),
            pltpu.VMEM((len(FAR_DIRS), 8, LANES), jnp.float32),
            pltpu.VMEM((nr, 2, LANES), jnp.float32),
            pltpu.VMEM((nz, 2, LANES), jnp.float32),
            pltpu.SemaphoreType.DMA((3,)),
            pltpu.SemaphoreType.DMA((len(ROUNDS), 8)),
            pltpu.SemaphoreType.DMA((len(ROUNDS), 8)),
            pltpu.SemaphoreType.DMA((8,)),
            pltpu.SemaphoreType.DMA((8,)),
            pltpu.SemaphoreType.DMA((len(FAR_DIRS),)),
            pltpu.SemaphoreType.DMA((len(FAR_DIRS),)),
            pltpu.SemaphoreType.DMA,
            pltpu.SemaphoreType.DMA,
            pltpu.SemaphoreType.DMA,
            pltpu.SemaphoreType.DMA,
        ],
        compiler_params=pltpu.CompilerParams(
            collective_id=0, has_side_effects=True, vmem_limit_bytes=32 * 1024 * 1024
        ),
    )(pltpu.with_memory_space_constraint(rhs_local.reshape(nodes, elems), pltpu.HBM), pltpu.with_memory_space_constraint(stretch, pltpu.HBM))
    return out.reshape(rhs_local.shape)


def solution(mesh):
    placed = (P(None, None, None, ("gz", "row")), P(None, ("gz", "row")))
    return jax.shard_map(
        per_device,
        mesh=mesh,
        in_specs=placed,
        out_specs=P(None, None, None, ("gz", "row")),
        check_vma=False,
    )
```

```python
import functools

import numpy as np

import jax
import jax.numpy as jnp
from jax import lax
from jax.experimental import pallas as pl
from jax.experimental.pallas import tpu as pltpu
from jax.sharding import PartitionSpec as P

ORDER = 7
MID = 3
ITERS = 5
EZ = 4
EA = 4
ER = 16
LANES = 128

LOW_BOUND = 0.4
HIGH_BOUND = 4.0
THETA = 0.5 * (HIGH_BOUND + LOW_BOUND)
DELTA = 0.5 * (HIGH_BOUND - LOW_BOUND)
RHO = DELTA / THETA
RHO2 = 1.0 / (2.0 * THETA / DELTA - RHO)

DIRS = ((0, 1), (0, -1), (1, 0), (-1, 0), (1, 1), (1, -1), (-1, 1), (-1, -1))
FAR_DIRS = tuple((z, a) for z in (2, -2, 1, -1, 0) for a in (2, -2, 1, -1, 0) if (z, a) != (0, 0))
ROUNDS = ((8, 8, 4), (8,), (4,), (4,), (4,) * 6, (4,), (8,), (8,))
SCALE = 16.0
TINY = 1e-13


def points_of(order):
    return -np.cos(np.pi * np.arange(order + 1) / order)


def tables_of(order):
    x = points_of(order)
    n = order + 1
    place = np.arange(n)
    running = np.ones(n)
    for j in range(1, order // 2 + 1):
        b = 1.0 if 2 * j == order else 2.0
        running = running - b * np.cos(2 * np.pi * j * place / order) / (4 * j * j - 1)
    weights = np.where((place == 0) | (place == order), 1.0, 2.0) / order * running
    gap = x[:, None] - x[None, :] + np.eye(n)
    bary = 1.0 / np.prod(gap, axis=1)
    deriv = bary[None, :] / bary[:, None] / gap * (1.0 - np.eye(n))
    deriv = deriv - np.diag(deriv.sum(axis=1))
    stiff = deriv.T @ (weights[:, None] * deriv)
    return weights, stiff / weights[:, None]


def interpolation(fine_order, coarse_order):
    x = points_of(fine_order)
    y = points_of(coarse_order)
    table = np.ones((fine_order + 1, coarse_order + 1))
    for j in range(coarse_order + 1):
        for k in range(coarse_order + 1):
            if k != j:
                table[:, j] *= (x - y[k]) / (y[j] - y[k])
    return table


WK = {n: tables_of(n - 1) for n in (8, 4, 2)}
UP = {(4, 8): interpolation(7, 3), (2, 4): interpolation(3, 1)}
DOWN = {(8, 4): UP[4, 8].T, (4, 2): UP[2, 4].T}
PAIRS = [(i, j) for i in range(ITERS) for j in range(i, ITERS)] + [(i, ITERS) for i in range(ITERS)]


def column_blocks(table):
    blocks = np.zeros((table.shape[1], 8))
    blocks[:, : table.shape[0]] = table.T
    return blocks


def constant_table():
    blocks, where = [], {}

    def put(name, rows):
        where[name] = sum(len(b) for b in blocks)
        blocks.append(rows)

    for n in (8, 4, 2):
        w, k = WK[n]
        put(("k", n), column_blocks(k))
        put(("w", n), column_blocks(np.outer(w, w)))
        put(("d", n), column_blocks(np.diag(k)[:, None]))
    for key, table in list(UP.items()) + list(DOWN.items()):
        put(("j",) + key, column_blocks(table))
    return np.concatenate(blocks).astype(np.float32), where


CONST, WHERE = constant_table()


def line(table, values, pairs=None):
    rows, cols = table.shape
    half = cols // 2
    even = [values[k] + values[cols - 1 - k] for k in range(half)]
    odd = [values[k] - values[cols - 1 - k] for k in range(half)]
    out = [None] * rows
    for i in range(rows // 2) if pairs is None else pairs:
        e = o = None
        for k in range(half):
            te = float(np.float32(0.5 * (table[i, k] + table[i, cols - 1 - k])))
            to = float(np.float32(0.5 * (table[i, k] - table[i, cols - 1 - k])))
            e = te * even[k] if e is None else e + te * even[k]
            o = to * odd[k] if o is None else o + to * odd[k]
        out[i] = e + o
        out[rows - 1 - i] = e - o
    return out


def rows8(start):
    if isinstance(start, int):
        return pl.ds(start, 8)
    return pl.ds(pl.multiple_of(start, 8), 8)


def roll(value, shift):
    shift = shift % LANES
    return value if shift == 0 else pltpu.roll(value, shift, 1)


def loop(count, body, unroll_all):
    if unroll_all:
        for i in range(count):
            body(i)
    else:
        pl.loop(0, count, unroll=2)(body)


def split(i, size):
    if isinstance(i, int):
        return i // size, i % size
    return lax.div(i, size), lax.rem(i, size)


def two_sum(a, b):
    s = a + b
    t = s - a
    return s, (a - (s - t)) + (b - t)


def halves(a):
    t = 4097.0 * a
    hi = t - (t - a)
    return a, hi, a - hi


def two_prod(x, y):
    a, ah, al = x
    b, bh, bl = y
    p = a * b
    return p, ((ah * bh - p) + ah * bl + al * bh) + al * bl


def add2(x, y):
    s, e = two_sum(x[0], y[0])
    return two_sum(s, e + (x[1] + y[1]))


def mul2(x, y):
    p, e = two_prod(halves(x[0]), halves(y[0]))
    return two_sum(p, e + (x[0] * y[1] + x[1] * y[0]))


def inverse2(x):
    r = 1.0 / x[0]
    p, e = two_prod(halves(x[0]), halves(r))
    return two_sum(r, r * (((1.0 - p) - e) - x[1] * r))


def kernel(
    nz, nr, rhs, stretch_in, out, stretch, tab,
    x7, d7, r7, inv7, o7, t1, t2, x3, d3, r3, inv3, o3, t3, x1, r1, coef,
    vertex, lifted, images, send, recv, send_diag, recv_diag, send_block, recv_block, send_point, recv_point, row_box, gz_box,
    load_sem, send_sem, recv_sem, block_send, block_recv, point_send, point_recv, row_met, gz_met, row_send, row_recv, gz_send, gz_recv,
):
    gz = lax.axis_index("gz")
    row = lax.axis_index("row")
    mesh_ids = pl.DeviceIdType.MESH
    shape = (8, LANES)
    lane = lax.broadcasted_iota(jnp.int32, shape, 1)
    sub = lax.broadcasted_iota(jnp.int32, shape, 0)
    in_r = lane % ER
    in_a = (lane // ER) % EA
    low_half = lane < 64

    def as_float(cond):
        return jnp.where(cond, 1.0, 0.0).astype(jnp.float32)

    def at_device(dz, da):
        return (lax.rem(gz + dz % nz, nz), lax.rem(row + da % nr, nr))

    barrier = pltpu.get_barrier_semaphore()
    for dz, da in DIRS:
        pl.semaphore_signal(barrier, inc=1, device_id=at_device(dz, da), device_id_type=mesh_ids)

    def greet(sem, dz, da):
        for sign in (1, -1):
            pl.semaphore_signal(sem, inc=1, device_id=at_device(sign * dz, sign * da), device_id_type=mesh_ids)

    loads = [pltpu.make_async_copy(stretch_in, stretch, load_sem.at[2])]
    for g in range(2):
        loads.append(
            pltpu.make_async_copy(rhs.at[:, pl.ds(g * LANES, LANES)], r7.at[pl.ds(g * 512, 512)], load_sem.at[g])
        )
    for load in loads:
        load.start()

    for b, values in enumerate(CONST):
        block = jnp.full(shape, float(values[0]), jnp.float32)
        for i in range(1, 8):
            block = jnp.where(sub == i, float(values[i]), block)
        tab[rows8(b * 8), :] = block
    loads[0].wait()

    def row_targets():
        if nr != 32:
            return [(o, lax.rem(row + o, nr)) for o in range(1, nr)]
        y, x, core = lax.div(row, 8), lax.rem(lax.div(row, 2), 4), lax.rem(row, 2)
        ys, xs, cores = [lax.rem(y + k, 4) * 8 for k in range(4)], [lax.rem(x + k, 4) * 2 for k in range(4)], [core, 1 - core]
        order = sorted(range(1, 32), key=lambda o: -(min(o // 8, 4 - o // 8) + min(o // 2 % 4, 4 - o // 2 % 4)))
        return [(o, ys[o // 8] + xs[o // 2 % 4] + cores[o % 2]) for o in order]

    def const(name, j=0):
        return tab[rows8((WHERE[name] + j) * 8), :]

    def live(n):
        wall = ((sub == 0) & (in_r == 0)) | ((sub == n - 1) & (in_r == ER - 1))
        return jnp.logical_not(wall) & (sub < n)

    for g in range(2):
        for k in range(3):
            coef[rows8((g * 3 + k) * 8), :] = jnp.broadcast_to(
                stretch[pl.ds(k, 1), pl.ds(g * LANES, LANES)], shape
            )

    def coeff(g, k):
        return coef[rows8((g * 3 + k) * 8), :]

    def add_r(field, n, base, stride=8, inner=False):
        lo_at = pl.ds(base, 8, stride=stride)
        hi_at = pl.ds(base + n - 1, 8, stride=stride)
        lo, hi = field[lo_at, :], field[hi_at, :]
        keep = (sub % n > 0) & (sub % n < n - 1) if inner else sub >= 0
        field[lo_at, :] = lo + jnp.where(keep & (in_r > 0), roll(hi, 1), 0.0)
        field[hi_at, :] = hi + jnp.where(keep & (in_r < ER - 1), roll(lo, -1), 0.0)

    def with_r(value, n):
        from_below = roll(pltpu.roll(value, 9 - n, 0), 1)
        from_above = roll(pltpu.roll(value, n - 1, 0), -1)
        value = value + jnp.where((sub == 0) & (in_r > 0), from_below, 0.0)
        return value + jnp.where((sub == n - 1) & (in_r < ER - 1), from_above, 0.0)

    def add_a(field, n, base):
        lo_at, hi_at = rows8(base), rows8(base + (n - 1) * 8)
        lo, hi = field[lo_at, :], field[hi_at, :]
        field[lo_at, :] = lo + jnp.where(in_a > 0, roll(hi, ER), 0.0)
        field[hi_at, :] = hi + jnp.where(in_a < EA - 1, roll(lo, -ER), 0.0)

    def block_at(n, g, iz, ia):
        return rows8(((g * n + iz) * n + ia) * 8)

    def add_z(field, n, which=None):
        for ia in range(n) if which is None else which:
            at = [block_at(n, g, iz, ia) for g, iz in ((0, 0), (1, 0), (0, n - 1), (1, n - 1))]
            lo0, lo1, hi0, hi1 = [field[a, :] for a in at]
            up0, up1, dn0, dn1 = [roll(v, 64) for v in (hi0, hi1, lo0, lo1)]
            field[at[0], :] = lo0 + jnp.where(low_half, 0.0, up0)
            field[at[1], :] = lo1 + jnp.where(low_half, up0, up1)
            field[at[2], :] = hi0 + jnp.where(low_half, dn0, dn1)
            field[at[3], :] = hi1 + jnp.where(low_half, dn1, 0.0)

    def device_sum(field, n):
        loop(2 * n * n // 8, lambda i: add_r(field, n, i * 64), n < 8)
        loop(2 * n, lambda i: add_a(field, n, i * n * 8), n < 8)
        add_z(field, n)

    def shared(iz, ia, n):
        along = jnp.where((sub == 0) | (sub == n - 1), 0.5, 1.0)
        if ia in (0, n - 1):
            along = 0.5 * along
        if isinstance(iz, int):
            return 0.5 * along if iz in (0, n - 1) else along
        return jnp.where((iz == 0) | (iz == n - 1), 0.5, 1.0) * along

    def along_z(field, image, n, g, ia):
        base = g * (n * n * 8) + ia * 8
        got = line(WK[n][1], [field[rows8(base + iz * n * 8), :] for iz in range(n)])
        c0 = coef[rows8(g * 24), :]
        for iz in range(n):
            image[rows8(base + iz * n * 8), :] = c0 * got[iz]

    def rest_values(field, image, n, g, iz, pairs, along=None):
        w, k = WK[n]
        base = (g * n + iz) * (n * 8)
        got = line(k, [field[rows8(base + ia * 8), :] for ia in range(n)], pairs)
        c1 = coef[rows8(g * 24 + 8), :]
        c2 = coef[rows8(g * 24 + 16), :]
        scale = tab[rows8((WHERE["w", n] + iz) * 8), :]
        values = []
        for ia in sorted(list(pairs) + [n - 1 - p for p in pairs]):
            at = base + ia * 8
            part = None
            for j in range(n):
                term = const(("k", n), j) * field[pl.ds(at + j, 1), :]
                part = term if part is None else part + term
            first = image[rows8(at), :] if along is None else along[ia]
            values.append((ia, (float(w[ia]) * scale) * (first + c1 * got[ia] + c2 * part)))
        return values

    def element(field, image, n, sums, left=None):
        loop(2 * n, lambda i: along_z(field, image, n, *split(i, n)), n < 8)

        def along_rest(i):
            g, iz = split(i, n)
            for ia, value in rest_values(field, image, n, g, iz, range(n // 2)):
                at = rows8(i * (n * 8) + ia * 8)
                image[at, :] = value if left is None else shared(iz, ia, n) * left[at, :] - value

        loop(2 * n, along_rest, n < 8)
        if sums:
            device_sum(image, n)

    def diagonal(field, n):
        w, k = WK[n]

        def body(i):
            g, iz = split(i, n)
            c0 = coef[rows8(g * 24), :]
            c1 = coef[rows8(g * 24 + 8), :]
            c2 = coef[rows8(g * 24 + 16), :]
            scale = tab[rows8((WHERE["w", n] + iz) * 8), :]
            kz = jnp.broadcast_to(tab[pl.ds(WHERE["d", n] * 8 + iz, 1), :], shape)
            fixed = c0 * kz + c2 * const(("d", n))
            for ia in range(n):
                field[rows8(i * (n * 8) + ia * 8), :] = (float(w[ia]) * scale) * (fixed + float(k[ia, ia]) * c1)

        loop(2 * n, body, n < 8)

    quarter = in_a

    def pack_a(field, n, at):
        half = n // 2
        for m in range(half):
            rows = rows8(at + m * 8)
            to_up = to_down = None
            for k in range(4):
                g, iz = divmod(m + k * half, n)
                up = roll(field[block_at(n, g, iz, n - 1), :], 80 + 16 * k)
                down = roll(field[block_at(n, g, iz, 0), :], 16 * k)
                to_up = up if k == 0 else jnp.where(quarter == k, up, to_up)
                to_down = down if k == 0 else jnp.where(quarter == k, down, to_down)
            send[0, rows, :] = to_up
            send[1, rows, :] = to_down

    def pack_z(field, n, at):
        half = n // 2
        for m in range(half):
            rows = rows8(at + m * 8)
            hi = [field[block_at(n, 1, n - 1, ia), :] for ia in (m, m + half)]
            lo = [field[block_at(n, 0, 0, ia), :] for ia in (m, m + half)]
            send[2, rows, :] = jnp.where(low_half, roll(hi[0], 64), hi[1])
            send[3, rows, :] = jnp.where(low_half, lo[0], roll(lo[1], 64))

    def pack(field, n, at, at_diag):
        pack_a(field, n, at)
        pack_z(field, n, at)
        for d, (g, iz, ia) in enumerate(corners(n)):
            send_diag[d, rows8(at_diag), :] = field[block_at(n, g, iz, ia), :]

    def corners(n):
        return ((1, n - 1, n - 1), (1, n - 1, 0), (0, 0, n - 1), (0, 0, 0))

    def unpack(field, n, at, at_diag, fix=None):
        half = n // 2

        def add(place, keep, value):
            value = jnp.where(keep, value, 0.0)
            if fix is not None:
                fix(place, value)
            else:
                where = block_at(n, *place)
                field[where, :] = field[where, :] + value

        for m in range(half):
            rows = rows8(at + m * 8)
            got = [recv[d, rows, :] for d in range(4)]
            for k in range(4):
                g, iz = divmod(m + k * half, n)
                add((g, iz, 0), in_a == 0, roll(got[0], -16 * k))
                add((g, iz, n - 1), in_a == EA - 1, roll(got[1], 48 - 16 * k))
        for m in range(half):
            rows = rows8(at + m * 8)
            got = [recv[d, rows, :] for d in range(4)]
            for k in range(2):
                add((0, 0, m + k * half), low_half, roll(got[2], 64 * k))
                add((1, n - 1, m + k * half), jnp.logical_not(low_half), roll(got[3], 64 - 64 * k))
        rows = rows8(at_diag)
        add((0, 0, 0), lane < 16, roll(recv_diag[0, rows, :], 16))
        add((0, 0, n - 1), (lane >= 48) & (lane < 64), roll(recv_diag[1, rows, :], -16))
        add((1, n - 1, 0), (lane >= 64) & (lane < 80), roll(recv_diag[2, rows, :], 16))
        add((1, n - 1, n - 1), lane >= 112, roll(recv_diag[3, rows, :], -16))

    offsets, diag_offsets = [0], [0]
    for counts in ROUNDS:
        offsets.append(offsets[-1] + sum(counts) * 4)
        diag_offsets.append(diag_offsets[-1] + len(counts) * 8)
    state = {"next": 0}

    class Round:
        def __init__(self, *fields):
            self.turn = state["next"]
            state["next"] += 1
            self.counts = ROUNDS[self.turn]
            self.at, self.at_diag = offsets[self.turn], diag_offsets[self.turn]
            self.fields = fields
            self.copies = []

        def places(self):
            at, at_diag = self.at, self.at_diag
            for field, n in zip(self.fields, self.counts):
                yield field, n, at, at_diag
                at += n * 4
                at_diag += 8

        def pack(self):
            for place in self.places():
                pack(*place)

        def start(self, which):
            for d in which:
                dz, da = DIRS[d]
                if d < 4:
                    rows = pl.ds(self.at, sum(self.counts) * 4)
                    src, dst = send.at[d, rows], recv.at[d, rows]
                else:
                    rows = pl.ds(self.at_diag, len(self.counts) * 8)
                    src, dst = send_diag.at[d - 4, rows], recv_diag.at[d - 4, rows]
                copy = pltpu.make_async_remote_copy(
                    src_ref=src, dst_ref=dst, send_sem=send_sem.at[self.turn, d], recv_sem=recv_sem.at[self.turn, d],
                    device_id=at_device(dz, da), device_id_type=mesh_ids,
                )
                copy.start()
                self.copies.append(copy)

        def finish(self, fix=None):
            for copy in self.copies:
                copy.wait()
            for place in self.places():
                unpack(*place, fix)

    LATE_FIRST = (4, 5, 6, 7, 0, 1, 2, 3)

    def send_all(dirs, src, dst, sends, recvs):
        copies = []
        for d, (dz, da) in enumerate(dirs):
            copy = pltpu.make_async_remote_copy(
                src_ref=src, dst_ref=dst.at[d], send_sem=sends.at[d], recv_sem=recvs.at[d],
                device_id=at_device(dz, da), device_id_type=mesh_ids,
            )
            copy.start()
            copies.append(copy)
        return copies

    def wide(at):
        def block(dz, da):
            if (dz, da) == (0, 0):
                return send_block[rows8(at), :]
            return recv_block[DIRS.index((-dz, -da)), rows8(at), :]

        def left_part(dz):
            return jnp.where(low_half, block(dz, -1), roll(block(dz, 0), 64))

        def below(low, own):
            return jnp.where(sub < 4, low, pltpu.roll(own, 4, 0))

        top = jnp.concatenate([below(left_part(-1), left_part(0)), below(block(-1, 1), block(0, 1))], axis=1)
        bottom = jnp.concatenate([left_part(1), block(1, 1)], axis=1)
        return jnp.concatenate([top, bottom], axis=0)

    def assemble(field, n):
        turn = Round(field)
        for d, place in enumerate(corners(n)):
            send_diag[d, rows8(turn.at_diag), :] = with_r(field[block_at(n, *place), :], n)
        turn.start((4, 5, 6, 7))
        device_sum(field, n)
        pack_a(field, n, turn.at)
        turn.start((0, 1))
        pack_z(field, n, turn.at)
        turn.start((2, 3))
        turn.finish()

    def apply(field, image, n, during, fix):
        turn = Round(image)
        ends = (0, n - 1)
        for d, (g, iz) in enumerate(((1, n - 1), (0, 0))):
            along = {}
            for ia in ends:
                got = line(WK[n][1], [field[block_at(n, g, j, ia), :] for j in range(n)], (0,))
                along[ia] = coef[rows8(g * 24), :] * got[iz]
            (_, first), (_, last) = rest_values(field, image, n, g, iz, (0,), along)
            send_diag[2 * d, rows8(turn.at_diag), :] = with_r(last, n)
            send_diag[2 * d + 1, rows8(turn.at_diag), :] = with_r(first, n)
        turn.start((4, 5, 6, 7))
        for g in range(2):
            for ia in ends:
                along_z(field, image, n, g, ia)

        def outer(i):
            g, iz = split(i, n)
            for ia, value in rest_values(field, image, n, g, iz, (0,)):
                image[rows8(i * (n * 8) + ia * 8), :] = value

        loop(2 * n, outer, n < 8)
        for q in range(2 * n // 8):
            for ia in ends:
                add_r(image, n, q * (n * 64) + ia * 8, n * 8)
        for i in range(2 * n):
            add_a(image, n, i * n * 8)
        add_z(image, n, ends)
        pack_a(image, n, turn.at)
        turn.start((0, 1))

        def inner_z(i):
            g, ia = split(i, n - 2)
            along_z(field, image, n, g, ia + 1)

        loop(2 * (n - 2), inner_z, n < 8)

        def inner(q):
            for part in range(8 // n):
                i = q * (8 // n) + part
                g, iz = split(i, n)
                for ia, value in rest_values(field, image, n, g, iz, range(1, n // 2)):
                    image[rows8(i * (n * 8) + ia * 8), :] = value
            add_r(image, n, q * 64, 8, True)

        groups = 2 * n * n // 8
        inner(0)
        inner(groups - 1)
        pack_z(image, n, turn.at)
        turn.start((2, 3))
        loop(groups - 2, lambda q: inner(q + 1), n < 8)
        add_z(image, n, range(1, n - 1))
        during()
        turn.finish(fix)

    def blocks(n, body):
        def step(i):
            if isinstance(i, int):
                body(pl.ds(i * 64, 64))
            else:
                body(pl.ds(pl.multiple_of(i * 64, 64), 64))

        loop(2 * n * n // 8, step, n < 8)

    def masked(n, value):
        keep = jnp.concatenate([as_float(live(n))] * 8, axis=0)
        return keep * value

    for load in loads[1:]:
        load.wait()
    device_sum(r7, 8)
    diagonal(inv7, 8)
    device_sum(inv7, 8)
    diagonal(inv3, 4)
    device_sum(inv3, 4)
    for k in range(3):
        rows = jnp.where(sub < 2, coeff(0, k), coeff(1, k))
        send_block[rows8(k * 8), :] = jnp.where(sub % 2 == 0, rows, roll(rows, 64))
    first_round = Round(r7, inv7, inv3)
    first_round.pack()
    pl.semaphore_wait(barrier, len(DIRS))
    first_round.start(LATE_FIRST)
    stretch_copies = send_all(DIRS, send_block, recv_block, block_send, block_recv)
    first_round.finish()
    greet(row_met.at[0], 0, 2)
    greet(gz_met.at[0], 2, 0)

    def invert(inv, n):
        keep = jnp.concatenate([live(n)] * 8, axis=0)

        def body(at):
            inv[at, :] = jnp.where(keep, 1.0 / jnp.where(keep, inv[at, :], 1.0), 0.0)

        blocks(n, body)

    invert(inv7, 8)
    invert(inv3, 4)

    def smooth_first(inv, r, d, n):
        def body(at):
            d[at, :] = (1.0 / THETA) * (inv[at, :] * r[at, :])

        blocks(n, body)

    def smooth_second(inv, r, d, x, image, n, result=None):
        def body(at):
            step = d[at, :]
            left = r[at, :] - image[at, :]
            second = (RHO2 * RHO) * step + (2.0 * RHO2 / DELTA) * (inv[at, :] * left)
            if result is None:
                x[at, :] = step + second
                d[at, :] = second
                r[at, :] = left
            else:
                result(at, x[at, :] + (step + second))

        def fix(place, value):
            at = block_at(n, *place)
            change = (2.0 * RHO2 / DELTA) * (inv[at, :] * value)
            if result is None:
                r[at, :] = r[at, :] - value
                d[at, :] = d[at, :] - change
                x[at, :] = x[at, :] - change
            elif n == 8:
                g, iz, ia = place
                spot = rows8((iz * 8 + ia) * 8), pl.ds(g * LANES, LANES)
                out[spot] = out[spot] - change
            else:
                x[at, :] = x[at, :] - change

        apply(d, image, n, lambda: blocks(n, body), fix)

    def r_line(name, field, at, count):
        part = None
        for j in range(count):
            term = const(name, j) * field[pl.ds(at + j, 1), :]
            part = term if part is None else part + term
        return part

    def restrict(fine, nf, nc, coarse, tz, ta):
        table = DOWN[nf, nc]

        def along_z(i):
            g, ia = split(i, nf)
            got = line(table, [fine[rows8((g * nf + iz) * (nf * 8) + ia * 8), :] for iz in range(nf)])
            for c in range(nc):
                tz[rows8((g * nc + c) * (nf * 8) + ia * 8), :] = got[c]

        def along_a(i):
            got = line(table, [tz[rows8(i * (nf * 8) + ia * 8), :] for ia in range(nf)])
            for c in range(nc):
                ta[rows8(i * (nc * 8) + c * 8), :] = got[c]
            for c in range(nc):
                at = i * (nc * 8) + c * 8
                coarse[rows8(at), :] = r_line(("j", nf, nc), ta, at, nf)

        loop(2 * nf, along_z, nf < 8)
        loop(2 * nc, along_a, nf < 8)

    def prolong(coarse, nc, nf, fields, tz, ta, add=True):
        table = UP[nc, nf]

        def along_a(i):
            for c in range(nc):
                at = i * (nc * 8) + c * 8
                ta[rows8(at), :] = r_line(("j", nc, nf), coarse, at, nc)
            got = line(table, [ta[rows8(i * (nc * 8) + c * 8), :] for c in range(nc)])
            for ia in range(nf):
                tz[rows8(i * (nf * 8) + ia * 8), :] = got[ia]

        def along_z(i):
            g, ia = split(i, nf)
            got = line(table, [tz[rows8((g * nc + c) * (nf * 8) + ia * 8), :] for c in range(nc)])
            for iz in range(nf):
                at = rows8((g * nf + iz) * (nf * 8) + ia * 8)
                for field in fields:
                    field[at, :] = field[at, :] + got[iz] if add else got[iz]

        loop(2 * nc, along_a, nf < 8)
        loop(2 * nf, along_z, nf < 8)

    smooth_first(inv7, r7, d7, 8)
    smooth_second(inv7, r7, d7, x7, o7, 8)
    pl.semaphore_wait(row_met.at[0], 2)
    pl.semaphore_wait(gz_met.at[0], 2)
    greet(row_met.at[1], 0, 4)
    greet(gz_met.at[1], 4, 0)
    element(d7, o7, 8, False, left=r7)

    restrict(o7, 8, 4, r3, t1, t2)
    assemble(r3, 4)
    pl.semaphore_wait(row_met.at[1], 2)
    pl.semaphore_wait(gz_met.at[1], 2)
    greet(row_met.at[2], 0, 8)
    smooth_first(inv3, r3, d3, 4)
    smooth_second(inv3, r3, d3, x3, o3, 4)
    pl.semaphore_wait(row_met.at[2], 2)
    element(d3, o3, 4, False, left=r3)

    restrict(o3, 4, 2, r1, t3, t2)
    per_z = []
    for iz in range(2):
        per_a = []
        for ia in range(2):
            at = [((g * 2 + iz) * 2 + ia) * 8 for g in range(2)]
            per_r = []
            for ir in range(2):
                rows = jnp.where(sub < 2, r1[pl.ds(at[0] + ir, 1), :], r1[pl.ds(at[1] + ir, 1), :])
                rows = jnp.where(sub % 2 == 0, rows, roll(rows, 64))
                per_r.append(jnp.where((sub < 4) & low_half, rows, 0.0))
            per_a.append(per_r[0] + roll(per_r[1], 1))
        per_z.append(per_a[0] + roll(per_a[1], ER))
    send_point[...] = per_z[0] + pltpu.roll(per_z[1], 1, 0)
    point_copies = send_all(FAR_DIRS, send_point, recv_point, point_send, point_recv)

    for copy in stretch_copies:
        copy.wait()
    lane_wide = lax.broadcasted_iota(jnp.int32, (16, 256), 1)
    inside = lane_wide % ER > 0

    def step(value, axis, amount):
        if axis == 0:
            return pltpu.roll(value, amount % 16, 0)
        return pltpu.roll(value, (amount * (ER if axis == 1 else 1)) % 256, 1)

    edges = []
    for axis in range(3):
        total = wide(axis * 8)
        for other in range(3):
            if other != axis:
                total = total + step(total, other, 1)
        edges.append(0.5 * total)

    def differences(value):
        return [value - step(value, axis, -1) for axis in range(3)]

    def vertex_image(slopes):
        total = None
        for axis in range(3):
            flux = edges[axis] * slopes[axis]
            flux = flux - step(flux, axis, 1)
            total = flux if total is None else total + flux
        return jnp.where(inside, (1.0 / SCALE) * total, 0.0)

    def summed_points():
        def from_device(dz, da):
            if (dz, da) == (0, 0):
                return send_point[...]
            return recv_point[FAR_DIRS.index((-dz, -da))]

        left, right = [], []
        for dz in (-2, -1, 0, 1, 2):
            far_left, near_left, mine, near_right, far_right = [from_device(dz, da) for da in (-2, -1, 0, 1, 2)]
            turned = roll(mine, 64)
            left.append(near_left + jnp.where(low_half, jnp.where(lane < ER, roll(far_left, 64), 0.0), turned))
            far_right = jnp.where((lane >= 64) & (lane < 64 + ER), roll(far_right, 64), 0.0)
            right.append(near_right + jnp.where(lane < ER, turned, far_right))
        halves_of = []
        for far_low, near_low, mine, near_high, far_high in (left, right):
            turned, far_low, far_high = [pltpu.roll(v, 4, 0) for v in (mine, far_low, far_high)]
            top = near_low + jnp.where(sub >= 4, turned, jnp.where(sub == 0, far_low, 0.0))
            bottom = near_high + jnp.where(sub == 0, turned, jnp.where(sub == 4, far_high, 0.0))
            halves_of.append(jnp.concatenate([top, bottom], axis=0))
        return jnp.where(inside, jnp.concatenate(halves_of, axis=1), 0.0)

    for copy in point_copies:
        copy.wait()
    basis = [summed_points()]
    slopes = [differences(basis[0])]
    for k in range(1, ITERS):
        basis.append(vertex_image(slopes[-1]))
        slopes.append(differences(basis[-1]))
    for k in range(ITERS):
        vertex[k] = basis[k]

    own = (sub >= 4) & jnp.logical_not(low_half)
    roots = [jnp.where(own, jnp.sqrt(edge[0:8, 0:LANES]), 0.0) for edge in edges]
    flows = [[halves(roots[axis] * slope[axis][0:8, 0:LANES]) for axis in range(3)] for slope in slopes]
    points = [halves(jnp.where(own, value[0:8, 0:LANES], 0.0)) for value in basis]

    tiles = [None] * 6
    for e, (i, j) in enumerate(PAIRS):
        if j < ITERS:
            total = two_prod(flows[i][0], flows[j][0])
            for axis in (1, 2):
                total = add2(total, two_prod(flows[i][axis], flows[j][axis]))
        else:
            total = two_prod(points[i], points[0])
        for amount in (2, 1):
            total = add2(total, tuple(pltpu.roll(part, amount, 0) for part in total))
        for half in range(2):
            row_of = jnp.broadcast_to(total[half][7:8, :], shape)
            slot = 2 * (e // 8) + half
            tiles[slot] = row_of if e % 8 == 0 else jnp.where(sub == e % 8, row_of, tiles[slot])
    sent = [0.0, 0.0]
    for t in range(3):
        total = (tiles[2 * t], tiles[2 * t + 1])
        for amount in (64, 32, 16, 8, 4, 2, 1):
            total = add2(total, tuple(roll(part, amount) for part in total))
        pick = sub < 0
        for e in range(8 * t, min(8 * t + 8, len(PAIRS))):
            i, j = PAIRS[e]
            spot = lane == 8 * i + j
            if j < ITERS:
                spot = spot | (lane == 8 * j + i)
            pick = pick | ((sub == e % 8) & spot)
        for half in range(2):
            sent[half] = sent[half] + jnp.sum(jnp.where(pick, total[half], 0.0), axis=0, keepdims=True)
    for half in range(2):
        row_box[0, pl.ds(half, 1), :] = sent[half]

    for o, target in row_targets():
        pltpu.make_async_remote_copy(
            src_ref=row_box.at[0], dst_ref=row_box.at[o], send_sem=row_send, recv_sem=row_recv,
            device_id=(gz, target), device_id_type=mesh_ids,
        ).start()

    def wait_for(box, count, sem):
        rest = box.at[pl.ds(1, count - 1)]
        pltpu.make_async_copy(rest, rest, sem).wait()

    def total_of(box, count):
        parts = [(box[o, pl.ds(0, 1), :], box[o, pl.ds(1, 1), :]) for o in range(count)]
        while len(parts) > 1:
            half = len(parts) // 2
            parts = [add2(parts[k], parts[k + half]) for k in range(half)] + parts[2 * half :]
        return parts[0]

    @pl.loop(0, ITERS)
    def _(k):
        value = vertex[k]
        for ia in range(2):
            at_node = []
            for ir in range(2):
                back = 64 + ER * ia + ir
                at_node.append([pltpu.roll(value, (shift - back) % 256, 1)[:, 0:LANES] for shift in (0, 64)])
            for g in range(2):
                for iz in range(2):
                    row_at = 4 + 2 * g + iz
                    pair = [
                        jnp.where(
                            low_half,
                            jnp.broadcast_to(v[0][row_at : row_at + 1], shape),
                            jnp.broadcast_to(v[1][row_at + 1 : row_at + 2], shape),
                        )
                        for v in at_node
                    ]
                    x1[block_at(2, g, iz, ia), :] = jnp.where(sub == 0, pair[0], jnp.where(sub == 1, pair[1], 0.0))
        prolong(x1, 2, 4, (lifted.at[k],), t3, t2, False)

    lifted[ITERS] = d3[...]

    @pl.loop(0, ITERS + 1)
    def _(k):
        element(lifted.at[k], images.at[k], 4, True)

    lifted_round = Round(*[images.at[k] for k in range(ITERS + 1)])
    lifted_round.pack()
    lifted_round.start(LATE_FIRST)

    wait_for(row_box, nr, row_recv)
    total = total_of(row_box, nr)
    for half in range(2):
        gz_box[0, pl.ds(half, 1), :] = total[half]

    @pl.loop(1, nz)
    def _(o):
        pltpu.make_async_remote_copy(
            src_ref=gz_box.at[0], dst_ref=gz_box.at[o], send_sem=gz_send, recv_sem=gz_recv,
            device_id=(lax.rem(gz + o, nz), row), device_id_type=mesh_ids,
        ).start()

    lifted_round.finish()
    wait_for(gz_box, nz, gz_recv)
    total = total_of(gz_box, nz)
    wait_for(row_box, nr, row_send)
    wait_for(gz_box, nz, gz_send)

    system = []
    for half in range(2):
        wide_row = jnp.broadcast_to(total[half], shape)
        part = jnp.zeros(shape, jnp.float32)
        for i in range(ITERS):
            part = jnp.where(sub == i, roll(wide_row, -8 * i), part)
        system.append(jnp.where(lane <= ITERS, part, 0.0))
    start = system[0]
    for p in range(ITERS):
        column = [jnp.broadcast_to(part[:, p : p + 1], shape) for part in system]
        line_p = [jnp.broadcast_to(part[p : p + 1, :], shape) for part in system]
        pivot = [jnp.broadcast_to(part[p : p + 1, :], shape) for part in column]
        least = TINY * jnp.broadcast_to(jnp.broadcast_to(start[p : p + 1, :], shape)[:, p : p + 1], shape)
        usable = pivot[0] > least
        inverse = inverse2((jnp.where(usable, pivot[0], 1.0), jnp.where(usable, pivot[1], 0.0)))
        scaled = mul2(line_p, tuple(jnp.where(usable, part, 0.0) for part in inverse))
        taken = mul2(column, scaled)
        rest = add2(system, (-taken[0], -taken[1]))
        system = [jnp.where(sub == p, scaled[half], rest[half]) for half in range(2)]

    factors = []
    for k in range(ITERS):
        factor = jnp.broadcast_to(system[0][k : k + 1, :], shape)[:, ITERS : ITERS + 1]
        factors.append(jnp.concatenate([jnp.broadcast_to(factor, shape)] * 8, axis=0))

    def correct(at):
        gain, image = x3[at, :], images[ITERS, at, :]
        for k in range(ITERS):
            gain = gain + factors[k] * lifted[k, at, :]
            image = image + factors[k] * images[k, at, :]
        x3[at, :] = gain
        r3[at, :] = r3[at, :] - image

    blocks(4, correct)
    smooth_first(inv3, r3, d3, 4)

    def keep_x3(at, value):
        x3[at, :] = value

    smooth_second(inv3, r3, d3, x3, o3, 4, keep_x3)

    prolong(x3, 4, 8, (d7, x7), t1, t2)

    def before_last(at):
        left = r7[at, :] - o7[at, :]
        r7[at, :] = left
        d7[at, :] = (1.0 / THETA) * (inv7[at, :] * left)

    def fix_before_last(place, value):
        at = block_at(8, *place)
        r7[at, :] = r7[at, :] - value
        d7[at, :] = d7[at, :] - (1.0 / THETA) * (inv7[at, :] * value)

    apply(d7, o7, 8, lambda: blocks(8, before_last), fix_before_last)

    def write(at, value):
        i = lax.div(at.start, 64)
        rows = pl.ds(pl.multiple_of(lax.rem(i, 8) * 64, 64), 64)
        out[rows, pl.ds(pl.multiple_of(lax.div(i, 8) * LANES, LANES), LANES)] = value

    smooth_second(inv7, r7, d7, x7, o7, 8, write)


def per_device(rhs_local, stretch):
    nz = lax.axis_size("gz")
    nr = lax.axis_size("row")
    nodes = (ORDER + 1) ** 3
    elems = EZ * EA * ER
    face_rows = sum(sum(c) * 4 for c in ROUNDS)
    diag_rows = sum(len(c) * 8 for c in ROUNDS)

    def field(rows):
        return pltpu.VMEM((rows, LANES), jnp.float32)

    out = pl.pallas_call(
        functools.partial(kernel, nz, nr),
        out_shape=jax.ShapeDtypeStruct((nodes, elems), jnp.float32),
        in_specs=[pl.BlockSpec(memory_space=pltpu.HBM)] * 2,
        out_specs=pl.BlockSpec(memory_space=pltpu.VMEM),
        scratch_shapes=[pltpu.VMEM((3, elems), jnp.float32), field(CONST.shape[0] * 8)]
        + [field(1024)] * 5
        + [field(512), field(256)]
        + [field(256)] * 5
        + [field(128)]
        + [field(64)] * 2
        + [field(48)]
        + [
            pltpu.VMEM((ITERS, 16, 256), jnp.float32),
            pltpu.VMEM((ITERS + 1, 256, LANES), jnp.float32),
            pltpu.VMEM((ITERS + 1, 256, LANES), jnp.float32),
            pltpu.VMEM((4, face_rows, LANES), jnp.float32),
            pltpu.VMEM((4, face_rows, LANES), jnp.float32),
            pltpu.VMEM((4, diag_rows, LANES), jnp.float32),
            pltpu.VMEM((4, diag_rows, LANES), jnp.float32),
            pltpu.VMEM((24, LANES), jnp.float32),
            pltpu.VMEM((8, 24, LANES), jnp.float32),
            pltpu.VMEM((8, LANES), jnp.float32),
            pltpu.VMEM((len(FAR_DIRS), 8, LANES), jnp.float32),
            pltpu.VMEM((nr, 2, LANES), jnp.float32),
            pltpu.VMEM((nz, 2, LANES), jnp.float32),
            pltpu.SemaphoreType.DMA((3,)),
            pltpu.SemaphoreType.DMA((len(ROUNDS), 8)),
            pltpu.SemaphoreType.DMA((len(ROUNDS), 8)),
            pltpu.SemaphoreType.DMA((8,)),
            pltpu.SemaphoreType.DMA((8,)),
            pltpu.SemaphoreType.DMA((len(FAR_DIRS),)),
            pltpu.SemaphoreType.DMA((len(FAR_DIRS),)),
            pltpu.SemaphoreType.REGULAR((3,)),
            pltpu.SemaphoreType.REGULAR((2,)),
            pltpu.SemaphoreType.DMA,
            pltpu.SemaphoreType.DMA,
            pltpu.SemaphoreType.DMA,
            pltpu.SemaphoreType.DMA,
        ],
        compiler_params=pltpu.CompilerParams(
            collective_id=0, has_side_effects=True, vmem_limit_bytes=32 * 1024 * 1024
        ),
    )(pltpu.with_memory_space_constraint(rhs_local.reshape(nodes, elems), pltpu.HBM), pltpu.with_memory_space_constraint(stretch, pltpu.HBM))
    return out.reshape(rhs_local.shape)


def solution(mesh):
    placed = (P(None, None, None, ("gz", "row")), P(None, ("gz", "row")))
    return jax.shard_map(
        per_device,
        mesh=mesh,
        in_specs=placed,
        out_specs=P(None, None, None, ("gz", "row")),
        check_vma=False,
    )
```

```python
import functools

import numpy as np

import jax
import jax.numpy as jnp
from jax import lax
from jax.experimental import pallas as pl
from jax.experimental.pallas import tpu as pltpu
from jax.sharding import PartitionSpec as P

ORDER = 7
MID = 3
ITERS = 5
EZ = 4
EA = 4
ER = 16
LANES = 128

LOW_BOUND = 0.4
HIGH_BOUND = 4.0
THETA = 0.5 * (HIGH_BOUND + LOW_BOUND)
DELTA = 0.5 * (HIGH_BOUND - LOW_BOUND)
RHO = DELTA / THETA
RHO2 = 1.0 / (2.0 * THETA / DELTA - RHO)

DIRS = ((0, 1), (0, -1), (1, 0), (-1, 0), (1, 1), (1, -1), (-1, 1), (-1, -1))
FAR_DIRS = tuple((z, a) for z in (2, -2, 1, -1, 0) for a in (2, -2, 1, -1, 0) if (z, a) != (0, 0))
ROUNDS = ((8, 8, 4), (8,), (4,), (4,), (4,) * 6, (4,), (8,), (8,))
SCALE = 16.0
TINY = 1e-13


def points_of(order):
    return -np.cos(np.pi * np.arange(order + 1) / order)


def tables_of(order):
    x = points_of(order)
    n = order + 1
    place = np.arange(n)
    running = np.ones(n)
    for j in range(1, order // 2 + 1):
        b = 1.0 if 2 * j == order else 2.0
        running = running - b * np.cos(2 * np.pi * j * place / order) / (4 * j * j - 1)
    weights = np.where((place == 0) | (place == order), 1.0, 2.0) / order * running
    gap = x[:, None] - x[None, :] + np.eye(n)
    bary = 1.0 / np.prod(gap, axis=1)
    deriv = bary[None, :] / bary[:, None] / gap * (1.0 - np.eye(n))
    deriv = deriv - np.diag(deriv.sum(axis=1))
    stiff = deriv.T @ (weights[:, None] * deriv)
    return weights, stiff / weights[:, None]


def interpolation(fine_order, coarse_order):
    x = points_of(fine_order)
    y = points_of(coarse_order)
    table = np.ones((fine_order + 1, coarse_order + 1))
    for j in range(coarse_order + 1):
        for k in range(coarse_order + 1):
            if k != j:
                table[:, j] *= (x - y[k]) / (y[j] - y[k])
    return table


WK = {n: tables_of(n - 1) for n in (8, 4, 2)}
UP = {(4, 8): interpolation(7, 3), (2, 4): interpolation(3, 1)}
DOWN = {(8, 4): UP[4, 8].T, (4, 2): UP[2, 4].T}
PAIRS = [(i, j) for i in range(ITERS) for j in range(i, ITERS)] + [(i, ITERS) for i in range(ITERS)]


def column_blocks(table):
    blocks = np.zeros((table.shape[1], 8))
    blocks[:, : table.shape[0]] = table.T
    return blocks


def constant_table():
    blocks, where = [], {}

    def put(name, rows):
        where[name] = sum(len(b) for b in blocks)
        blocks.append(rows)

    for n in (8, 4, 2):
        w, k = WK[n]
        put(("k", n), column_blocks(k))
        put(("w", n), column_blocks(np.outer(w, w)))
        put(("d", n), column_blocks(np.diag(k)[:, None]))
    for key, table in list(UP.items()) + list(DOWN.items()):
        put(("j",) + key, column_blocks(table))
    return np.concatenate(blocks).astype(np.float32), where


CONST, WHERE = constant_table()


def line(table, values, pairs=None):
    rows, cols = table.shape
    half = cols // 2
    even = [values[k] + values[cols - 1 - k] for k in range(half)]
    odd = [values[k] - values[cols - 1 - k] for k in range(half)]
    out = [None] * rows
    for i in range(rows // 2) if pairs is None else pairs:
        e = o = None
        for k in range(half):
            te = float(np.float32(0.5 * (table[i, k] + table[i, cols - 1 - k])))
            to = float(np.float32(0.5 * (table[i, k] - table[i, cols - 1 - k])))
            e = te * even[k] if e is None else e + te * even[k]
            o = to * odd[k] if o is None else o + to * odd[k]
        out[i] = e + o
        out[rows - 1 - i] = e - o
    return out


def rows8(start):
    if isinstance(start, int):
        return pl.ds(start, 8)
    return pl.ds(pl.multiple_of(start, 8), 8)


def roll(value, shift):
    shift = shift % LANES
    return value if shift == 0 else pltpu.roll(value, shift, 1)


def loop(count, body, unroll_all):
    if unroll_all:
        for i in range(count):
            body(i)
    else:
        pl.loop(0, count, unroll=2)(body)


def split(i, size):
    if isinstance(i, int):
        return i // size, i % size
    return lax.div(i, size), lax.rem(i, size)


def two_sum(a, b):
    s = a + b
    t = s - a
    return s, (a - (s - t)) + (b - t)


def halves(a):
    t = 4097.0 * a
    hi = t - (t - a)
    return a, hi, a - hi


def two_prod(x, y):
    a, ah, al = x
    b, bh, bl = y
    p = a * b
    return p, ((ah * bh - p) + ah * bl + al * bh) + al * bl


def add2(x, y):
    s, e = two_sum(x[0], y[0])
    return two_sum(s, e + (x[1] + y[1]))


def mul2(x, y):
    p, e = two_prod(halves(x[0]), halves(y[0]))
    return two_sum(p, e + (x[0] * y[1] + x[1] * y[0]))


def inverse2(x):
    r = 1.0 / x[0]
    p, e = two_prod(halves(x[0]), halves(r))
    return two_sum(r, r * (((1.0 - p) - e) - x[1] * r))


def kernel(
    nz, nr, rhs, stretch_in, out, stretch, tab,
    x7, d7, r7, inv7, o7, t1, t2, x3, d3, r3, inv3, o3, t3, x1, r1, coef,
    vertex, lifted, images, send, recv, send_diag, recv_diag, send_block, recv_block, send_point, recv_point, row_box, gz_box,
    load_sem, send_sem, recv_sem, block_send, block_recv, point_send, point_recv, row_met, gz_met, row_send, row_recv, gz_send, gz_recv,
):
    gz = lax.axis_index("gz")
    row = lax.axis_index("row")
    mesh_ids = pl.DeviceIdType.MESH
    shape = (8, LANES)
    lane = lax.broadcasted_iota(jnp.int32, shape, 1)
    sub = lax.broadcasted_iota(jnp.int32, shape, 0)
    in_r = lane % ER
    in_a = (lane // ER) % EA
    low_half = lane < 64

    def as_float(cond):
        return jnp.where(cond, 1.0, 0.0).astype(jnp.float32)

    def at_device(dz, da):
        return (lax.rem(gz + dz % nz, nz), lax.rem(row + da % nr, nr))

    barrier = pltpu.get_barrier_semaphore()
    for dz, da in DIRS:
        pl.semaphore_signal(barrier, inc=1, device_id=at_device(dz, da), device_id_type=mesh_ids)

    def greet(sem, dz, da):
        for sign in (1, -1):
            pl.semaphore_signal(sem, inc=1, device_id=at_device(sign * dz, sign * da), device_id_type=mesh_ids)

    loads = [pltpu.make_async_copy(stretch_in, stretch, load_sem.at[2])]
    for g in range(2):
        loads.append(
            pltpu.make_async_copy(rhs.at[:, pl.ds(g * LANES, LANES)], r7.at[pl.ds(g * 512, 512)], load_sem.at[g])
        )
    for load in loads:
        load.start()

    for b, values in enumerate(CONST):
        block = jnp.full(shape, float(values[0]), jnp.float32)
        for i in range(1, 8):
            block = jnp.where(sub == i, float(values[i]), block)
        tab[rows8(b * 8), :] = block
    loads[0].wait()

    def row_targets():
        if nr != 32:
            return [(o, lax.rem(row + o, nr)) for o in range(1, nr)]
        y, x, core = lax.div(row, 8), lax.rem(lax.div(row, 2), 4), lax.rem(row, 2)
        ys, xs, cores = [lax.rem(y + k, 4) * 8 for k in range(4)], [lax.rem(x + k, 4) * 2 for k in range(4)], [core, 1 - core]
        order = sorted(range(1, 32), key=lambda o: -(min(o // 8, 4 - o // 8) + min(o // 2 % 4, 4 - o // 2 % 4)))
        return [(o, ys[o // 8] + xs[o // 2 % 4] + cores[o % 2]) for o in order]

    def const(name, j=0):
        return tab[rows8((WHERE[name] + j) * 8), :]

    def live(n):
        wall = ((sub == 0) & (in_r == 0)) | ((sub == n - 1) & (in_r == ER - 1))
        return jnp.logical_not(wall) & (sub < n)

    for g in range(2):
        for k in range(3):
            coef[rows8((g * 3 + k) * 8), :] = jnp.broadcast_to(
                stretch[pl.ds(k, 1), pl.ds(g * LANES, LANES)], shape
            )

    def coeff(g, k):
        return coef[rows8((g * 3 + k) * 8), :]

    def add_r(field, n, base, stride=8, inner=False):
        lo_at = pl.ds(base, 8, stride=stride)
        hi_at = pl.ds(base + n - 1, 8, stride=stride)
        lo, hi = field[lo_at, :], field[hi_at, :]
        keep = (sub % n > 0) & (sub % n < n - 1) if inner else sub >= 0
        field[lo_at, :] = lo + jnp.where(keep & (in_r > 0), roll(hi, 1), 0.0)
        field[hi_at, :] = hi + jnp.where(keep & (in_r < ER - 1), roll(lo, -1), 0.0)

    def with_r(value, n):
        from_below = roll(pltpu.roll(value, 9 - n, 0), 1)
        from_above = roll(pltpu.roll(value, n - 1, 0), -1)
        value = value + jnp.where((sub == 0) & (in_r > 0), from_below, 0.0)
        return value + jnp.where((sub == n - 1) & (in_r < ER - 1), from_above, 0.0)

    def add_a(field, n, base):
        lo_at, hi_at = rows8(base), rows8(base + (n - 1) * 8)
        lo, hi = field[lo_at, :], field[hi_at, :]
        field[lo_at, :] = lo + jnp.where(in_a > 0, roll(hi, ER), 0.0)
        field[hi_at, :] = hi + jnp.where(in_a < EA - 1, roll(lo, -ER), 0.0)

    def block_at(n, g, iz, ia):
        return rows8(((g * n + iz) * n + ia) * 8)

    def add_z(field, n, which=None):
        for ia in range(n) if which is None else which:
            at = [block_at(n, g, iz, ia) for g, iz in ((0, 0), (1, 0), (0, n - 1), (1, n - 1))]
            lo0, lo1, hi0, hi1 = [field[a, :] for a in at]
            up0, up1, dn0, dn1 = [roll(v, 64) for v in (hi0, hi1, lo0, lo1)]
            field[at[0], :] = lo0 + jnp.where(low_half, 0.0, up0)
            field[at[1], :] = lo1 + jnp.where(low_half, up0, up1)
            field[at[2], :] = hi0 + jnp.where(low_half, dn0, dn1)
            field[at[3], :] = hi1 + jnp.where(low_half, dn1, 0.0)

    def device_sum(field, n):
        loop(2 * n * n // 8, lambda i: add_r(field, n, i * 64), n < 8)
        loop(2 * n, lambda i: add_a(field, n, i * n * 8), n < 8)
        add_z(field, n)

    def shared(iz, ia, n):
        along = jnp.where((sub == 0) | (sub == n - 1), 0.5, 1.0)
        if ia in (0, n - 1):
            along = 0.5 * along
        if isinstance(iz, int):
            return 0.5 * along if iz in (0, n - 1) else along
        return jnp.where((iz == 0) | (iz == n - 1), 0.5, 1.0) * along

    def along_z(field, image, n, g, ia):
        base = g * (n * n * 8) + ia * 8
        got = line(WK[n][1], [field[rows8(base + iz * n * 8), :] for iz in range(n)])
        c0 = coef[rows8(g * 24), :]
        for iz in range(n):
            image[rows8(base + iz * n * 8), :] = c0 * got[iz]

    def rest_values(field, image, n, g, iz, pairs, along=None):
        w, k = WK[n]
        base = (g * n + iz) * (n * 8)
        got = line(k, [field[rows8(base + ia * 8), :] for ia in range(n)], pairs)
        c1 = coef[rows8(g * 24 + 8), :]
        c2 = coef[rows8(g * 24 + 16), :]
        scale = tab[rows8((WHERE["w", n] + iz) * 8), :]
        values = []
        for ia in sorted(list(pairs) + [n - 1 - p for p in pairs]):
            at = base + ia * 8
            part = None
            for j in range(n):
                term = const(("k", n), j) * field[pl.ds(at + j, 1), :]
                part = term if part is None else part + term
            first = image[rows8(at), :] if along is None else along[ia]
            values.append((ia, (float(w[ia]) * scale) * (first + c1 * got[ia] + c2 * part)))
        return values

    def element(field, image, n, sums, left=None):
        loop(2 * n, lambda i: along_z(field, image, n, *split(i, n)), n < 8)

        def along_rest(i):
            g, iz = split(i, n)
            for ia, value in rest_values(field, image, n, g, iz, range(n // 2)):
                at = rows8(i * (n * 8) + ia * 8)
                image[at, :] = value if left is None else shared(iz, ia, n) * left[at, :] - value

        loop(2 * n, along_rest, n < 8)
        if sums:
            device_sum(image, n)

    def diagonal(field, n):
        w, k = WK[n]

        def body(i):
            g, iz = split(i, n)
            c0 = coef[rows8(g * 24), :]
            c1 = coef[rows8(g * 24 + 8), :]
            c2 = coef[rows8(g * 24 + 16), :]
            scale = tab[rows8((WHERE["w", n] + iz) * 8), :]
            kz = jnp.broadcast_to(tab[pl.ds(WHERE["d", n] * 8 + iz, 1), :], shape)
            fixed = c0 * kz + c2 * const(("d", n))
            for ia in range(n):
                field[rows8(i * (n * 8) + ia * 8), :] = (float(w[ia]) * scale) * (fixed + float(k[ia, ia]) * c1)

        loop(2 * n, body, n < 8)

    quarter = in_a

    def pack_a(field, n, at):
        half = n // 2
        for m in range(half):
            rows = rows8(at + m * 8)
            to_up = to_down = None
            for k in range(4):
                g, iz = divmod(m + k * half, n)
                up = roll(field[block_at(n, g, iz, n - 1), :], 80 + 16 * k)
                down = roll(field[block_at(n, g, iz, 0), :], 16 * k)
                to_up = up if k == 0 else jnp.where(quarter == k, up, to_up)
                to_down = down if k == 0 else jnp.where(quarter == k, down, to_down)
            send[0, rows, :] = to_up
            send[1, rows, :] = to_down

    def pack_z(field, n, at):
        half = n // 2
        for m in range(half):
            rows = rows8(at + m * 8)
            hi = [field[block_at(n, 1, n - 1, ia), :] for ia in (m, m + half)]
            lo = [field[block_at(n, 0, 0, ia), :] for ia in (m, m + half)]
            send[2, rows, :] = jnp.where(low_half, roll(hi[0], 64), hi[1])
            send[3, rows, :] = jnp.where(low_half, lo[0], roll(lo[1], 64))

    def pack(field, n, at, at_diag):
        pack_a(field, n, at)
        pack_z(field, n, at)
        for d, (g, iz, ia) in enumerate(corners(n)):
            send_diag[d, rows8(at_diag), :] = field[block_at(n, g, iz, ia), :]

    def corners(n):
        return ((1, n - 1, n - 1), (1, n - 1, 0), (0, 0, n - 1), (0, 0, 0))

    def unpack(field, n, at, at_diag, fix=None):
        half = n // 2

        def add(place, keep, value):
            value = jnp.where(keep, value, 0.0)
            if fix is not None:
                fix(place, value)
            else:
                where = block_at(n, *place)
                field[where, :] = field[where, :] + value

        for m in range(half):
            rows = rows8(at + m * 8)
            got = [recv[d, rows, :] for d in range(4)]
            for k in range(4):
                g, iz = divmod(m + k * half, n)
                add((g, iz, 0), in_a == 0, roll(got[0], -16 * k))
                add((g, iz, n - 1), in_a == EA - 1, roll(got[1], 48 - 16 * k))
        for m in range(half):
            rows = rows8(at + m * 8)
            got = [recv[d, rows, :] for d in range(4)]
            for k in range(2):
                add((0, 0, m + k * half), low_half, roll(got[2], 64 * k))
                add((1, n - 1, m + k * half), jnp.logical_not(low_half), roll(got[3], 64 - 64 * k))
        rows = rows8(at_diag)
        add((0, 0, 0), lane < 16, roll(recv_diag[0, rows, :], 16))
        add((0, 0, n - 1), (lane >= 48) & (lane < 64), roll(recv_diag[1, rows, :], -16))
        add((1, n - 1, 0), (lane >= 64) & (lane < 80), roll(recv_diag[2, rows, :], 16))
        add((1, n - 1, n - 1), lane >= 112, roll(recv_diag[3, rows, :], -16))

    offsets, diag_offsets = [0], [0]
    for counts in ROUNDS:
        offsets.append(offsets[-1] + sum(counts) * 4)
        diag_offsets.append(diag_offsets[-1] + len(counts) * 8)
    state = {"next": 0}

    class Round:
        def __init__(self, *fields):
            self.turn = state["next"]
            state["next"] += 1
            self.counts = ROUNDS[self.turn]
            self.at, self.at_diag = offsets[self.turn], diag_offsets[self.turn]
            self.fields = fields
            self.copies = []

        def places(self):
            at, at_diag = self.at, self.at_diag
            for field, n in zip(self.fields, self.counts):
                yield field, n, at, at_diag
                at += n * 4
                at_diag += 8

        def pack(self):
            for place in self.places():
                pack(*place)

        def start(self, which):
            for d in which:
                dz, da = DIRS[d]
                if d < 4:
                    rows = pl.ds(self.at, sum(self.counts) * 4)
                    src, dst = send.at[d, rows], recv.at[d, rows]
                else:
                    rows = pl.ds(self.at_diag, len(self.counts) * 8)
                    src, dst = send_diag.at[d - 4, rows], recv_diag.at[d - 4, rows]
                copy = pltpu.make_async_remote_copy(
                    src_ref=src, dst_ref=dst, send_sem=send_sem.at[self.turn, d], recv_sem=recv_sem.at[self.turn, d],
                    device_id=at_device(dz, da), device_id_type=mesh_ids,
                )
                copy.start()
                self.copies.append(copy)

        def finish(self, fix=None):
            for copy in self.copies:
                copy.wait()
            for place in self.places():
                unpack(*place, fix)

        def finish_but_last(self):
            for copy in self.copies:
                copy.wait()
            *most, last = self.places()
            for place in most:
                unpack(*place)
            return lambda: unpack(*last)

    LATE_FIRST = (4, 5, 6, 7, 0, 1, 2, 3)

    def send_all(dirs, src, dst, sends, recvs):
        copies = []
        for d, (dz, da) in enumerate(dirs):
            copy = pltpu.make_async_remote_copy(
                src_ref=src, dst_ref=dst.at[d], send_sem=sends.at[d], recv_sem=recvs.at[d],
                device_id=at_device(dz, da), device_id_type=mesh_ids,
            )
            copy.start()
            copies.append(copy)
        return copies

    def wide(at):
        def block(dz, da):
            if (dz, da) == (0, 0):
                return send_block[rows8(at), :]
            return recv_block[DIRS.index((-dz, -da)), rows8(at), :]

        def left_part(dz):
            return jnp.where(low_half, block(dz, -1), roll(block(dz, 0), 64))

        def below(low, own):
            return jnp.where(sub < 4, low, pltpu.roll(own, 4, 0))

        top = jnp.concatenate([below(left_part(-1), left_part(0)), below(block(-1, 1), block(0, 1))], axis=1)
        bottom = jnp.concatenate([left_part(1), block(1, 1)], axis=1)
        return jnp.concatenate([top, bottom], axis=0)

    def assemble(field, n):
        turn = Round(field)
        for d, place in enumerate(corners(n)):
            send_diag[d, rows8(turn.at_diag), :] = with_r(field[block_at(n, *place), :], n)
        turn.start((4, 5, 6, 7))
        device_sum(field, n)
        pack_a(field, n, turn.at)
        turn.start((0, 1))
        pack_z(field, n, turn.at)
        turn.start((2, 3))
        turn.finish()

    def apply(field, image, n, during, fix):
        turn = Round(image)
        ends = (0, n - 1)
        for d, (g, iz) in enumerate(((1, n - 1), (0, 0))):
            along = {}
            for ia in ends:
                got = line(WK[n][1], [field[block_at(n, g, j, ia), :] for j in range(n)], (0,))
                along[ia] = coef[rows8(g * 24), :] * got[iz]
            (_, first), (_, last) = rest_values(field, image, n, g, iz, (0,), along)
            send_diag[2 * d, rows8(turn.at_diag), :] = with_r(last, n)
            send_diag[2 * d + 1, rows8(turn.at_diag), :] = with_r(first, n)
        turn.start((4, 5, 6, 7))
        for g in range(2):
            for ia in ends:
                along_z(field, image, n, g, ia)

        def outer(i):
            g, iz = split(i, n)
            for ia, value in rest_values(field, image, n, g, iz, (0,)):
                image[rows8(i * (n * 8) + ia * 8), :] = value

        loop(2 * n, outer, n < 8)
        for q in range(2 * n // 8):
            for ia in ends:
                add_r(image, n, q * (n * 64) + ia * 8, n * 8)
        for i in range(2 * n):
            add_a(image, n, i * n * 8)
        add_z(image, n, ends)
        pack_a(image, n, turn.at)
        turn.start((0, 1))

        def inner_z(i):
            g, ia = split(i, n - 2)
            along_z(field, image, n, g, ia + 1)

        loop(2 * (n - 2), inner_z, n < 8)

        def inner(q):
            for part in range(8 // n):
                i = q * (8 // n) + part
                g, iz = split(i, n)
                for ia, value in rest_values(field, image, n, g, iz, range(1, n // 2)):
                    image[rows8(i * (n * 8) + ia * 8), :] = value
            add_r(image, n, q * 64, 8, True)

        groups = 2 * n * n // 8
        inner(0)
        inner(groups - 1)
        pack_z(image, n, turn.at)
        turn.start((2, 3))
        loop(groups - 2, lambda q: inner(q + 1), n < 8)
        add_z(image, n, range(1, n - 1))
        during()
        turn.finish(fix)

    def blocks(n, body):
        def step(i):
            if isinstance(i, int):
                body(pl.ds(i * 64, 64))
            else:
                body(pl.ds(pl.multiple_of(i * 64, 64), 64))

        loop(2 * n * n // 8, step, n < 8)

    def masked(n, value):
        keep = jnp.concatenate([as_float(live(n))] * 8, axis=0)
        return keep * value

    for load in loads[1:]:
        load.wait()
    device_sum(r7, 8)
    diagonal(inv7, 8)
    device_sum(inv7, 8)
    diagonal(inv3, 4)
    device_sum(inv3, 4)
    for k in range(3):
        rows = jnp.where(sub < 2, coeff(0, k), coeff(1, k))
        send_block[rows8(k * 8), :] = jnp.where(sub % 2 == 0, rows, roll(rows, 64))
    first_round = Round(r7, inv7, inv3)
    first_round.pack()
    pl.semaphore_wait(barrier, len(DIRS))
    first_round.start(LATE_FIRST)
    stretch_copies = send_all(DIRS, send_block, recv_block, block_send, block_recv)
    unpack_inv3 = first_round.finish_but_last()
    greet(row_met.at[0], 0, 2)
    greet(gz_met.at[0], 2, 0)

    def invert(inv, n):
        keep = jnp.concatenate([live(n)] * 8, axis=0)

        def body(at):
            inv[at, :] = jnp.where(keep, 1.0 / jnp.where(keep, inv[at, :], 1.0), 0.0)

        blocks(n, body)

    def level_3_diagonal():
        unpack_inv3()
        invert(inv3, 4)

    def smooth_first(inv, r, d, n):
        def body(at):
            d[at, :] = (1.0 / THETA) * (inv[at, :] * r[at, :])

        blocks(n, body)

    def smooth_second(inv, r, d, x, image, n, result=None, beside=None):
        def body(at):
            step = d[at, :]
            left = r[at, :] - image[at, :]
            second = (RHO2 * RHO) * step + (2.0 * RHO2 / DELTA) * (inv[at, :] * left)
            if result is None:
                x[at, :] = step + second
                d[at, :] = second
                r[at, :] = left
            else:
                result(at, x[at, :] + (step + second))

        def fix(place, value):
            at = block_at(n, *place)
            change = (2.0 * RHO2 / DELTA) * (inv[at, :] * value)
            if result is None:
                r[at, :] = r[at, :] - value
                d[at, :] = d[at, :] - change
                x[at, :] = x[at, :] - change
            elif n == 8:
                g, iz, ia = place
                spot = rows8((iz * 8 + ia) * 8), pl.ds(g * LANES, LANES)
                out[spot] = out[spot] - change
            else:
                x[at, :] = x[at, :] - change

        def during():
            blocks(n, body)
            if beside is not None:
                beside()

        apply(d, image, n, during, fix)

    def r_line(name, field, at, count):
        part = None
        for j in range(count):
            term = const(name, j) * field[pl.ds(at + j, 1), :]
            part = term if part is None else part + term
        return part

    def restrict(fine, nf, nc, coarse, tz, ta):
        table = DOWN[nf, nc]

        def along_z(i):
            g, ia = split(i, nf)
            got = line(table, [fine[rows8((g * nf + iz) * (nf * 8) + ia * 8), :] for iz in range(nf)])
            for c in range(nc):
                tz[rows8((g * nc + c) * (nf * 8) + ia * 8), :] = got[c]

        def along_a(i):
            got = line(table, [tz[rows8(i * (nf * 8) + ia * 8), :] for ia in range(nf)])
            for c in range(nc):
                ta[rows8(i * (nc * 8) + c * 8), :] = got[c]
            for c in range(nc):
                at = i * (nc * 8) + c * 8
                coarse[rows8(at), :] = r_line(("j", nf, nc), ta, at, nf)

        loop(2 * nf, along_z, nf < 8)
        loop(2 * nc, along_a, nf < 8)

    def prolong(coarse, nc, nf, fields, tz, ta, add=True):
        table = UP[nc, nf]

        def along_a(i):
            for c in range(nc):
                at = i * (nc * 8) + c * 8
                ta[rows8(at), :] = r_line(("j", nc, nf), coarse, at, nc)
            got = line(table, [ta[rows8(i * (nc * 8) + c * 8), :] for c in range(nc)])
            for ia in range(nf):
                tz[rows8(i * (nf * 8) + ia * 8), :] = got[ia]

        def along_z(i):
            g, ia = split(i, nf)
            got = line(table, [tz[rows8((g * nc + c) * (nf * 8) + ia * 8), :] for c in range(nc)])
            for iz in range(nf):
                at = rows8((g * nf + iz) * (nf * 8) + ia * 8)
                for field in fields:
                    field[at, :] = field[at, :] + got[iz] if add else got[iz]

        loop(2 * nc, along_a, nf < 8)
        loop(2 * nf, along_z, nf < 8)

    keep_7 = jnp.concatenate([live(8)] * 8, axis=0)

    def invert_and_smooth(at):
        inverse = jnp.where(keep_7, 1.0 / jnp.where(keep_7, inv7[at, :], 1.0), 0.0)
        inv7[at, :] = inverse
        d7[at, :] = (1.0 / THETA) * (inverse * r7[at, :])

    blocks(8, invert_and_smooth)
    smooth_second(inv7, r7, d7, x7, o7, 8, beside=level_3_diagonal)
    pl.semaphore_wait(row_met.at[0], 2)
    pl.semaphore_wait(gz_met.at[0], 2)
    greet(row_met.at[1], 0, 4)
    greet(gz_met.at[1], 4, 0)
    element(d7, o7, 8, False, left=r7)

    restrict(o7, 8, 4, r3, t1, t2)
    assemble(r3, 4)
    pl.semaphore_wait(row_met.at[1], 2)
    pl.semaphore_wait(gz_met.at[1], 2)
    greet(row_met.at[2], 0, 8)
    smooth_first(inv3, r3, d3, 4)
    smooth_second(inv3, r3, d3, x3, o3, 4)
    pl.semaphore_wait(row_met.at[2], 2)
    element(d3, o3, 4, False, left=r3)

    restrict(o3, 4, 2, r1, t3, t2)
    per_z = []
    for iz in range(2):
        per_a = []
        for ia in range(2):
            at = [((g * 2 + iz) * 2 + ia) * 8 for g in range(2)]
            per_r = []
            for ir in range(2):
                rows = jnp.where(sub < 2, r1[pl.ds(at[0] + ir, 1), :], r1[pl.ds(at[1] + ir, 1), :])
                rows = jnp.where(sub % 2 == 0, rows, roll(rows, 64))
                per_r.append(jnp.where((sub < 4) & low_half, rows, 0.0))
            per_a.append(per_r[0] + roll(per_r[1], 1))
        per_z.append(per_a[0] + roll(per_a[1], ER))
    send_point[...] = per_z[0] + pltpu.roll(per_z[1], 1, 0)
    point_copies = send_all(FAR_DIRS, send_point, recv_point, point_send, point_recv)

    for copy in stretch_copies:
        copy.wait()
    lane_wide = lax.broadcasted_iota(jnp.int32, (16, 256), 1)
    inside = lane_wide % ER > 0

    def step(value, axis, amount):
        if axis == 0:
            return pltpu.roll(value, amount % 16, 0)
        return pltpu.roll(value, (amount * (ER if axis == 1 else 1)) % 256, 1)

    edges = []
    for axis in range(3):
        total = wide(axis * 8)
        for other in range(3):
            if other != axis:
                total = total + step(total, other, 1)
        edges.append(0.5 * total)

    def differences(value):
        return [value - step(value, axis, -1) for axis in range(3)]

    def vertex_image(slopes):
        total = None
        for axis in range(3):
            flux = edges[axis] * slopes[axis]
            flux = flux - step(flux, axis, 1)
            total = flux if total is None else total + flux
        return jnp.where(inside, (1.0 / SCALE) * total, 0.0)

    def summed_points():
        def from_device(dz, da):
            if (dz, da) == (0, 0):
                return send_point[...]
            return recv_point[FAR_DIRS.index((-dz, -da))]

        left, right = [], []
        for dz in (-2, -1, 0, 1, 2):
            far_left, near_left, mine, near_right, far_right = [from_device(dz, da) for da in (-2, -1, 0, 1, 2)]
            turned = roll(mine, 64)
            left.append(near_left + jnp.where(low_half, jnp.where(lane < ER, roll(far_left, 64), 0.0), turned))
            far_right = jnp.where((lane >= 64) & (lane < 64 + ER), roll(far_right, 64), 0.0)
            right.append(near_right + jnp.where(lane < ER, turned, far_right))
        halves_of = []
        for far_low, near_low, mine, near_high, far_high in (left, right):
            turned, far_low, far_high = [pltpu.roll(v, 4, 0) for v in (mine, far_low, far_high)]
            top = near_low + jnp.where(sub >= 4, turned, jnp.where(sub == 0, far_low, 0.0))
            bottom = near_high + jnp.where(sub == 0, turned, jnp.where(sub == 4, far_high, 0.0))
            halves_of.append(jnp.concatenate([top, bottom], axis=0))
        return jnp.where(inside, jnp.concatenate(halves_of, axis=1), 0.0)

    for copy in point_copies:
        copy.wait()
    basis = [summed_points()]
    slopes = [differences(basis[0])]
    for k in range(1, ITERS):
        basis.append(vertex_image(slopes[-1]))
        slopes.append(differences(basis[-1]))
    for k in range(ITERS):
        vertex[k] = basis[k]

    own = (sub >= 4) & jnp.logical_not(low_half)
    roots = [jnp.where(own, jnp.sqrt(edge[0:8, 0:LANES]), 0.0) for edge in edges]
    flows = [[halves(roots[axis] * slope[axis][0:8, 0:LANES]) for axis in range(3)] for slope in slopes]
    points = [halves(jnp.where(own, value[0:8, 0:LANES], 0.0)) for value in basis]

    tiles = [None] * 6
    for e, (i, j) in enumerate(PAIRS):
        if j < ITERS:
            total = two_prod(flows[i][0], flows[j][0])
            for axis in (1, 2):
                total = add2(total, two_prod(flows[i][axis], flows[j][axis]))
        else:
            total = two_prod(points[i], points[0])
        for amount in (2, 1):
            total = add2(total, tuple(pltpu.roll(part, amount, 0) for part in total))
        for half in range(2):
            row_of = jnp.broadcast_to(total[half][7:8, :], shape)
            slot = 2 * (e // 8) + half
            tiles[slot] = row_of if e % 8 == 0 else jnp.where(sub == e % 8, row_of, tiles[slot])
    sent = [0.0, 0.0]
    for t in range(3):
        total = (tiles[2 * t], tiles[2 * t + 1])
        for amount in (64, 32, 16, 8, 4, 2, 1):
            total = add2(total, tuple(roll(part, amount) for part in total))
        pick = sub < 0
        for e in range(8 * t, min(8 * t + 8, len(PAIRS))):
            i, j = PAIRS[e]
            spot = lane == 8 * i + j
            if j < ITERS:
                spot = spot | (lane == 8 * j + i)
            pick = pick | ((sub == e % 8) & spot)
        for half in range(2):
            sent[half] = sent[half] + jnp.sum(jnp.where(pick, total[half], 0.0), axis=0, keepdims=True)
    for half in range(2):
        row_box[0, pl.ds(half, 1), :] = sent[half]

    for o, target in row_targets():
        pltpu.make_async_remote_copy(
            src_ref=row_box.at[0], dst_ref=row_box.at[o], send_sem=row_send, recv_sem=row_recv,
            device_id=(gz, target), device_id_type=mesh_ids,
        ).start()

    def wait_for(box, count, sem):
        rest = box.at[pl.ds(1, count - 1)]
        pltpu.make_async_copy(rest, rest, sem).wait()

    def total_of(box, count):
        parts = [(box[o, pl.ds(0, 1), :], box[o, pl.ds(1, 1), :]) for o in range(count)]
        while len(parts) > 1:
            half = len(parts) // 2
            parts = [add2(parts[k], parts[k + half]) for k in range(half)] + parts[2 * half :]
        return parts[0]

    @pl.loop(0, ITERS)
    def _(k):
        value = vertex[k]
        for ia in range(2):
            at_node = []
            for ir in range(2):
                back = 64 + ER * ia + ir
                at_node.append([pltpu.roll(value, (shift - back) % 256, 1)[:, 0:LANES] for shift in (0, 64)])
            for g in range(2):
                for iz in range(2):
                    row_at = 4 + 2 * g + iz
                    pair = [
                        jnp.where(
                            low_half,
                            jnp.broadcast_to(v[0][row_at : row_at + 1], shape),
                            jnp.broadcast_to(v[1][row_at + 1 : row_at + 2], shape),
                        )
                        for v in at_node
                    ]
                    x1[block_at(2, g, iz, ia), :] = jnp.where(sub == 0, pair[0], jnp.where(sub == 1, pair[1], 0.0))
        prolong(x1, 2, 4, (lifted.at[k],), t3, t2, False)

    lifted[ITERS] = d3[...]

    @pl.loop(0, ITERS + 1)
    def _(k):
        element(lifted.at[k], images.at[k], 4, True)

    lifted_round = Round(*[images.at[k] for k in range(ITERS + 1)])
    lifted_round.pack()
    lifted_round.start(LATE_FIRST)

    wait_for(row_box, nr, row_recv)
    total = total_of(row_box, nr)
    for half in range(2):
        gz_box[0, pl.ds(half, 1), :] = total[half]

    for o in sorted(range(1, nz), key=lambda o: -min(o, nz - o)):
        pltpu.make_async_remote_copy(
            src_ref=gz_box.at[0], dst_ref=gz_box.at[o], send_sem=gz_send, recv_sem=gz_recv,
            device_id=(lax.rem(gz + o, nz), row), device_id_type=mesh_ids,
        ).start()

    lifted_round.finish()
    wait_for(gz_box, nz, gz_recv)
    total = total_of(gz_box, nz)

    system = []
    for half in range(2):
        wide_row = jnp.broadcast_to(total[half], shape)
        part = jnp.zeros(shape, jnp.float32)
        for i in range(ITERS):
            part = jnp.where(sub == i, roll(wide_row, -8 * i), part)
        system.append(jnp.where(lane <= ITERS, part, 0.0))
    start = system[0]
    for p in range(ITERS):
        column = [jnp.broadcast_to(part[:, p : p + 1], shape) for part in system]
        line_p = [jnp.broadcast_to(part[p : p + 1, :], shape) for part in system]
        pivot = [jnp.broadcast_to(part[p : p + 1, :], shape) for part in column]
        least = TINY * jnp.broadcast_to(jnp.broadcast_to(start[p : p + 1, :], shape)[:, p : p + 1], shape)
        usable = pivot[0] > least
        inverse = inverse2((jnp.where(usable, pivot[0], 1.0), jnp.where(usable, pivot[1], 0.0)))
        scaled = mul2(line_p, tuple(jnp.where(usable, part, 0.0) for part in inverse))
        taken = mul2(column, scaled)
        rest = add2(system, (-taken[0], -taken[1]))
        system = [jnp.where(sub == p, scaled[half], rest[half]) for half in range(2)]

    factors = []
    for k in range(ITERS):
        factor = jnp.broadcast_to(system[0][k : k + 1, :], shape)[:, ITERS : ITERS + 1]
        factors.append(jnp.concatenate([jnp.broadcast_to(factor, shape)] * 8, axis=0))

    def correct(at):
        gain, image = x3[at, :], images[ITERS, at, :]
        for k in range(ITERS):
            gain = gain + factors[k] * lifted[k, at, :]
            image = image + factors[k] * images[k, at, :]
        x3[at, :] = gain
        r3[at, :] = r3[at, :] - image

    blocks(4, correct)
    smooth_first(inv3, r3, d3, 4)

    def keep_x3(at, value):
        x3[at, :] = value

    smooth_second(inv3, r3, d3, x3, o3, 4, keep_x3)

    prolong(x3, 4, 8, (d7, x7), t1, t2)

    def before_last(at):
        left = r7[at, :] - o7[at, :]
        r7[at, :] = left
        d7[at, :] = (1.0 / THETA) * (inv7[at, :] * left)

    def fix_before_last(place, value):
        at = block_at(8, *place)
        r7[at, :] = r7[at, :] - value
        d7[at, :] = d7[at, :] - (1.0 / THETA) * (inv7[at, :] * value)

    apply(d7, o7, 8, lambda: blocks(8, before_last), fix_before_last)

    def write(at, value):
        i = lax.div(at.start, 64)
        rows = pl.ds(pl.multiple_of(lax.rem(i, 8) * 64, 64), 64)
        out[rows, pl.ds(pl.multiple_of(lax.div(i, 8) * LANES, LANES), LANES)] = value

    smooth_second(inv7, r7, d7, x7, o7, 8, write)
    wait_for(row_box, nr, row_send)
    wait_for(gz_box, nz, gz_send)


def per_device(rhs_local, stretch):
    nz = lax.axis_size("gz")
    nr = lax.axis_size("row")
    nodes = (ORDER + 1) ** 3
    elems = EZ * EA * ER
    face_rows = sum(sum(c) * 4 for c in ROUNDS)
    diag_rows = sum(len(c) * 8 for c in ROUNDS)

    def field(rows):
        return pltpu.VMEM((rows, LANES), jnp.float32)

    out = pl.pallas_call(
        functools.partial(kernel, nz, nr),
        out_shape=jax.ShapeDtypeStruct((nodes, elems), jnp.float32),
        in_specs=[pl.BlockSpec(memory_space=pltpu.HBM)] * 2,
        out_specs=pl.BlockSpec(memory_space=pltpu.VMEM),
        scratch_shapes=[pltpu.VMEM((3, elems), jnp.float32), field(CONST.shape[0] * 8)]
        + [field(1024)] * 5
        + [field(512), field(256)]
        + [field(256)] * 5
        + [field(128)]
        + [field(64)] * 2
        + [field(48)]
        + [
            pltpu.VMEM((ITERS, 16, 256), jnp.float32),
            pltpu.VMEM((ITERS + 1, 256, LANES), jnp.float32),
            pltpu.VMEM((ITERS + 1, 256, LANES), jnp.float32),
            pltpu.VMEM((4, face_rows, LANES), jnp.float32),
            pltpu.VMEM((4, face_rows, LANES), jnp.float32),
            pltpu.VMEM((4, diag_rows, LANES), jnp.float32),
            pltpu.VMEM((4, diag_rows, LANES), jnp.float32),
            pltpu.VMEM((24, LANES), jnp.float32),
            pltpu.VMEM((8, 24, LANES), jnp.float32),
            pltpu.VMEM((8, LANES), jnp.float32),
            pltpu.VMEM((len(FAR_DIRS), 8, LANES), jnp.float32),
            pltpu.VMEM((nr, 2, LANES), jnp.float32),
            pltpu.VMEM((nz, 2, LANES), jnp.float32),
            pltpu.SemaphoreType.DMA((3,)),
            pltpu.SemaphoreType.DMA((len(ROUNDS), 8)),
            pltpu.SemaphoreType.DMA((len(ROUNDS), 8)),
            pltpu.SemaphoreType.DMA((8,)),
            pltpu.SemaphoreType.DMA((8,)),
            pltpu.SemaphoreType.DMA((len(FAR_DIRS),)),
            pltpu.SemaphoreType.DMA((len(FAR_DIRS),)),
            pltpu.SemaphoreType.REGULAR((3,)),
            pltpu.SemaphoreType.REGULAR((2,)),
            pltpu.SemaphoreType.DMA,
            pltpu.SemaphoreType.DMA,
            pltpu.SemaphoreType.DMA,
            pltpu.SemaphoreType.DMA,
        ],
        compiler_params=pltpu.CompilerParams(
            collective_id=0, has_side_effects=True, vmem_limit_bytes=32 * 1024 * 1024
        ),
    )(pltpu.with_memory_space_constraint(rhs_local.reshape(nodes, elems), pltpu.HBM), pltpu.with_memory_space_constraint(stretch, pltpu.HBM))
    return out.reshape(rhs_local.shape)


def solution(mesh):
    placed = (P(None, None, None, ("gz", "row")), P(None, ("gz", "row")))
    return jax.shard_map(
        per_device,
        mesh=mesh,
        in_specs=placed,
        out_specs=P(None, None, None, ("gz", "row")),
        check_vma=False,
    )
```
